32 devices in a mesh: blk: 8 (over y, x, core), fsdp: 4 (over z).
Axes of the slice: x: 2, y: 2, z: 4, core: 2. Of those that a mesh axis runs over, the one named last changes fastest.
Arguments:
- tokens: bfloat16 [4096, 2048], P('blk'), may hold values from -6 to 6
- span_order: int32 [16], replicated, may hold values from 0 to 15, as said below
- input_gain: bfloat16 [2048], P('blk'), may hold values from 0.25 to 1.75
- query_weight: bfloat16 [2048, 2048], P('blk', 'fsdp'), may hold values from -0.125 to 0.125
- key_weight: bfloat16 [2048, 1024], P('blk', 'fsdp'), may hold values from -0.125 to 0.125
- value_weight: bfloat16 [2048, 1024], P('blk', 'fsdp'), may hold values from -0.125 to 0.125
- query_gain: bfloat16 [128], P('blk'), may hold values from 0.25 to 1.75
- key_gain: bfloat16 [128], P('blk'), may hold values from 0.25 to 1.75
- output_weight: bfloat16 [2048, 2048], P('fsdp', 'blk'), may hold values from -1 to 1
- post_gain: bfloat16 [2048], P('blk'), may hold values from 0.25 to 1.75
- gate_weight: bfloat16 [2048, 6144], P('blk', 'fsdp'), may hold values from -0.125 to 0.125
- up_weight: bfloat16 [2048, 6144], P('blk', 'fsdp'), may hold values from -0.125 to 0.125
- down_weight: bfloat16 [6144, 2048], P('fsdp', 'blk'), may hold values from -0.078125 to 0.078125
- cotangent: bfloat16 [4096, 2048], P('blk'), may hold values from -6 to 6
Outputs:
- layer_out: bfloat16 [4096, 2048], P('blk')
- tokens_gradient: float32 [4096, 2048], P('blk')
- input_gain_gradient: float32 [2048], P('blk')
- query_weight_gradient: float32 [2048, 2048], P('blk', 'fsdp')
- key_weight_gradient: float32 [2048, 1024], P('blk', 'fsdp')
- value_weight_gradient: float32 [2048, 1024], P('blk', 'fsdp')
- query_gain_gradient: float32 [128], P('blk')
- key_gain_gradient: float32 [128], P('blk')
- output_weight_gradient: float32 [2048, 2048], P('fsdp', 'blk')
- post_gain_gradient: float32 [2048], P('blk')
- gate_weight_gradient: float32 [2048, 6144], P('blk', 'fsdp')
- up_weight_gradient: float32 [2048, 6144], P('blk', 'fsdp')
- down_weight_gradient: float32 [6144, 2048], P('fsdp', 'blk')
The draws below stay inside these ranges and needn't reach their ends.
Inputs may be any that keep to these rules, and one draw needn't show every extreme that they name: Each span number appears once, and the two spans of one index d of blk, span_order[2 d] and span_order[2 d + 1], sum to 15, in either order.
All inputs are finite; a program needn't handle non-finite values.
Results may differ from the reference program's by a relative error of at most 0.025.
Values may be sent and summed in bfloat16 or wider, within the bound.
No kernel may reach another device: no remote copies, remote signals or barrier semaphores. Data moves between devices by JAX's collectives and lax.ppermute only.
A program may use at most 192 MiB of HBM per device.

```python
import math
import jax
import jax.numpy as jnp
from jax import lax

D = 2048
QH = 16
KH = 8
HD = 128
FF = 6144
SEQ = 4096
N_BLK = 8


def draw_span_order(key, part):
    key = jax.random.fold_in(key, 7)
    first_key, second_key = jax.random.split(key)
    ordering = jax.random.permutation(first_key, N_BLK).astype(jnp.int32)
    flipped = jax.random.randint(second_key, (N_BLK,), 0, 2).astype(jnp.int32)
    leading = jnp.where(flipped == 1, 2 * N_BLK - 1 - ordering, ordering).astype(jnp.int32)
    trailing = (2 * N_BLK - 1 - leading).astype(jnp.int32)
    return jnp.stack([leading, trailing], axis=1).reshape(-1).astype(jnp.int32)


def level_of(stream_key, shape, cuts, smallest, largest):
    factor_of = 1.0
    for position, blocks in cuts:
        draws = jax.random.uniform(jax.random.fold_in(jax.random.fold_in(stream_key, 6), position), (blocks,), jnp.float32, smallest / len(cuts), largest / len(cuts))
        factor_of = factor_of * jnp.repeat(jnp.exp(draws), shape[position] // blocks).reshape((-1,) + (1,) * (len(shape) - 1 - position))
    return factor_of


def gaussian(rng, extent, scale, reach, pieces=(), held_as=jnp.bfloat16):
    values = jax.random.normal(rng, extent, jnp.float32) * scale
    if len(pieces) > 0:
        values = level_of(rng, extent, pieces, -0.22, 0.18) * values
    return jnp.clip(values, min=-reach, max=reach).astype(held_as)


def setup_inputs(seed: int = 0) -> dict:
    key_of = jax.random.split(jax.random.key(seed), 15)
    return {
        "tokens": gaussian(key_of[0], (SEQ, D), 1.0, 6.0, ((0, 8),)),
        "span_order": draw_span_order(jax.random.fold_in(key_of[14], 71), 0),
        "input_gain": jnp.clip(1.0 + 0.15 * jax.random.normal(key_of[2], (D,), jnp.float32), 0.25, 1.75).astype(jnp.bfloat16),
        "query_weight": gaussian(key_of[3], (D, QH * HD), D ** -0.5, 0.125, ((0, 8), (1, 4))),
        "key_weight": gaussian(key_of[4], (D, KH * HD), D ** -0.5, 0.125, ((0, 8), (1, 4))),
        "value_weight": gaussian(key_of[5], (D, KH * HD), D ** -0.5, 0.125, ((0, 8), (1, 4))),
        "query_gain": jnp.clip(1.0 + 0.15 * jax.random.normal(key_of[6], (HD,), jnp.float32), 0.25, 1.75).astype(jnp.bfloat16),
        "key_gain": jnp.clip(1.0 + 0.15 * jax.random.normal(key_of[7], (HD,), jnp.float32), 0.25, 1.75).astype(jnp.bfloat16),
        "output_weight": gaussian(key_of[8], (QH * HD, D), (QH * HD // 64) ** -0.5, 1.0, ((0, 4), (1, 8))),
        "post_gain": jnp.clip(1.0 + 0.15 * jax.random.normal(key_of[9], (D,), jnp.float32), 0.25, 1.75).astype(jnp.bfloat16),
        "gate_weight": gaussian(key_of[10], (D, FF), D ** -0.5, 0.125, ((0, 8), (1, 4))),
        "up_weight": gaussian(key_of[11], (D, FF), D ** -0.5, 0.125, ((0, 8), (1, 4))),
        "down_weight": gaussian(key_of[12], (FF, D), FF ** -0.5, 0.078125, ((0, 4), (1, 8))),
        "cotangent": gaussian(key_of[13], (SEQ, D), 1.0, 6.0, ((0, 8),)),
    }


EPS = 1e-06
THETA = 1000000.0
NEG = -1e+30
HIGH = lax.Precision.HIGHEST

@jax.custom_vjp
def low(v):
    return lax.optimization_barrier(v.astype(jnp.bfloat16)).astype(jnp.float32)

@jax.custom_vjp
def low_back(v):
    return v

def low_keep(v):
    return (low(v), None)

def low_pass(kept, grad):
    return (grad,)

def back_keep(v):
    return (v, None)

def back_low(kept, grad):
    return (low(grad),)
low.defvjp(low_keep, low_pass)
low_back.defvjp(back_keep, back_low)

def row_norm(values, gain):
    return values * lax.rsqrt(lax.optimization_barrier(jnp.mean(values * values, axis=-1, keepdims=True)) + EPS) * gain

def rope_tables(places, width):
    half = width // 2
    freqs = THETA ** (-jnp.arange(half, dtype=jnp.float32) * 2.0 / width)
    angles = places.astype(jnp.float32)[:, None] * freqs[None, :]
    angles = jnp.concatenate([angles, angles], axis=1)
    return (jnp.cos(angles), jnp.sin(angles))

def rotate(values, cosine, sine):
    half = values.shape[-1] // 2
    turned = jnp.concatenate([-values[..., half:], values[..., :half]], axis=-1)
    return values * cosine[:, None, :] + turned * sine[:, None, :]

def mat(left, right):
    return jnp.dot(left, right, precision=HIGH)

def forward(inputs, input_gain, query_weight, key_weight, value_weight, query_gain, key_gain, output_weight, post_gain, gate_weight, up_weight, down_weight):
    length = inputs.shape[0]
    normed = low(row_norm(inputs, input_gain))
    q_proj = low_back(mat(normed, query_weight)).reshape(length, QH, HD)
    k_proj = low_back(mat(normed, key_weight)).reshape(length, KH, HD)
    values = low(low_back(mat(normed, value_weight))).reshape(length, KH, HD)
    cosine, sine = rope_tables(jnp.arange(length, dtype=jnp.int32), HD)
    queries = low(rotate(row_norm(q_proj, query_gain), cosine, sine)).reshape(length, KH, QH // KH, HD)
    keys = low(rotate(row_norm(k_proj, key_gain), cosine, sine))
    block = math.gcd(length, 512)
    starts = jnp.arange(length // block, dtype=jnp.int32) * block

    def attend(start):
        query_block = lax.dynamic_slice_in_dim(queries, start, block, 0)
        scores = low_back(jnp.einsum('qhgd,khd->hgqk', query_block, keys, precision=HIGH) * HD ** (-0.5))
        allowed = (start + jnp.arange(block, dtype=jnp.int32))[:, None] >= jnp.arange(length, dtype=jnp.int32)[None, :]
        scores = jnp.where(allowed, scores, NEG)
        probs = low(jax.nn.softmax(scores, axis=-1))
        return jnp.einsum('hgqk,khd->qhgd', probs, values, precision=HIGH)
    context = lax.map(jax.checkpoint(attend), starts)
    context = low(low_back(context.reshape(length, QH * HD)))
    hidden = inputs + low_back(mat(context, output_weight))
    post = low(row_norm(hidden, post_gain))
    gate = low_back(mat(post, gate_weight))
    up = low_back(mat(post, up_weight))
    act = low(jax.nn.silu(gate) * up)
    return hidden + low_back(mat(act, down_weight))

def reference(tokens, span_order, input_gain, query_weight, key_weight, value_weight, query_gain, key_gain, output_weight, post_gain, gate_weight, up_weight, down_weight, cotangent):
    span_rows = tokens.shape[0] // span_order.shape[0]
    places = (span_order[:, None] * span_rows + jnp.arange(span_rows, dtype=jnp.int32)[None, :]).reshape(-1).astype(jnp.int32)
    inverse = jnp.argsort(places).astype(jnp.int32)
    inputs = tokens.astype(jnp.float32)[inverse]
    upstream = cotangent.astype(jnp.float32)[inverse]
    result, pull = jax.vjp(forward, inputs, input_gain.astype(jnp.float32), query_weight.astype(jnp.float32), key_weight.astype(jnp.float32), value_weight.astype(jnp.float32), query_gain.astype(jnp.float32), key_gain.astype(jnp.float32), output_weight.astype(jnp.float32), post_gain.astype(jnp.float32), gate_weight.astype(jnp.float32), up_weight.astype(jnp.float32), down_weight.astype(jnp.float32))
    grads = pull(upstream)
    return (result[places].astype(jnp.bfloat16), grads[0][places], grads[1], grads[2], grads[3], grads[4], grads[5], grads[6], grads[7], grads[8], grads[9], grads[10], grads[11])
```

```python
import functools
import math

import jax
import jax.numpy as jnp
from jax import lax
from jax.experimental import pallas as pl
from jax.experimental.pallas import tpu as pltpu
from jax.sharding import PartitionSpec as P

HD = 128
EPS = 1e-06
THETA = 1000000.0
LOG2E = math.log2(math.e)
LN2 = math.log(2.0)
MIB = 1024 * 1024

F32 = jnp.float32
BF16 = jnp.bfloat16


def dims(lhs, rhs, left, right):
    return lax.dot_general(lhs, rhs, (((left,), (right,)), ((), ())), preferred_element_type=F32)


def mask_order(n):
    return [2 * i for i in range(n // 2)] + [2 * i + 1 for i in range(n // 2)]


def high_bits(n):
    return [1 << i for i in range(1, n.bit_length() - 1)]


def exchange(block, bit):
    n = lax.axis_size("blk")
    return lax.ppermute(block, "blk", [(i, i ^ bit) for i in range(n)])


def gather_rows(piece, bits):
    rows = piece.shape[0]
    held = {0: piece}
    for bit in bits:
        masks = sorted(held)
        sent = [held[m] for m in masks]
        got = exchange(sent[0] if len(sent) == 1 else jnp.concatenate(sent, axis=0), bit)
        for i, m in enumerate(masks):
            held[m | bit] = got[i * rows : (i + 1) * rows]
    own = jnp.concatenate([held[m] for m in sorted(held)], axis=0)
    return own, exchange(own, 1)


def add_low(a, b):
    return (a.astype(F32) + b.astype(F32)).astype(BF16)


def scatter_sum(own, got, bits):
    count = 2 ** len(bits)
    rows = own.shape[0] // count
    held = {}
    for i in range(count):
        part = slice(i * rows, (i + 1) * rows)
        held[2 * i] = (own[part], got[part])
    for bit in bits:
        leave = [m for m in sorted(held) if m & bit]
        stay = [m for m in sorted(held) if not m & bit]
        sent = [add_low(*held[m]) for m in leave]
        back = exchange(sent[0] if len(sent) == 1 else jnp.concatenate(sent, axis=0), bit)
        held = {
            m: (add_low(*held[m]), back[i * rows : (i + 1) * rows]) for i, m in enumerate(stay)
        }
    return held[0][0].astype(F32) + held[0][1].astype(F32)


def row_norm(values, gain):
    scale = lax.rsqrt(jnp.mean(values * values, axis=-1, keepdims=True) + EPS)
    return (values * scale * gain, scale)


def norm_back(values, scale, weighted):
    inner = jnp.mean(weighted * values, axis=-1, keepdims=True)
    return scale * (weighted - values * scale * scale * inner)


def rope_tables(places, width):
    half = width // 2
    freqs = THETA ** (-jnp.arange(half, dtype=F32) * 2.0 / width)
    angles = places.astype(F32)[:, None] * freqs[None, :]
    sine = jnp.sin(angles)
    cosine = jnp.cos(angles)
    return (jnp.concatenate([cosine, cosine], axis=1), jnp.concatenate([-sine, sine], axis=1))


def turned(values):
    half = values.shape[-1] // 2
    return jnp.concatenate([values[..., half:], values[..., :half]], axis=-1)


def attend_kernel(span, sc, q_ref, k0, k1, v0, v1, ctx_ref, lse_ref, k_s, v_s, acc_s, sum_s):
    half = k0.shape[0]
    k_s[:half] = k0[...]
    k_s[half:] = k1[...]
    v_s[:half] = v0[...]
    v_s[half:] = v1[...]
    group = q_ref.shape[1] // HD
    rows = span * group
    for s in range(2):
        top = slice(s * span, (s + 1) * span)
        q = jnp.concatenate([q_ref[top, g * HD : (g + 1) * HD] for g in range(group)], axis=0)
        acc_s[...] = jnp.zeros_like(acc_s)
        sum_s[...] = jnp.zeros_like(sum_s)

        def step(p, masked):
            at = pl.ds(pl.multiple_of(sc[2 + p] * span, span), span)
            e = jnp.exp2(dims(q, k_s[at, :], 1, 1))
            if masked:
                row = lax.broadcasted_iota(jnp.int32, (rows, span), 0) % span
                col = lax.broadcasted_iota(jnp.int32, (rows, span), 1)
                e = jnp.where(row >= col, e, 0.0)
            part = e[:, :HD]
            for c in range(HD, span, HD):
                part = part + e[:, c : c + HD]
            sum_s[...] += part
            acc_s[...] += dims(e.astype(BF16), v_s[at, :], 1, 0)

        pl.loop(0, sc[s])(lambda p: step(p, False))
        step(sc[s], True)
        total = jnp.sum(sum_s[...], axis=1, keepdims=True)
        ctx = (acc_s[...] / total).astype(BF16)
        for g in range(group):
            ctx_ref[top, g * HD : (g + 1) * HD] = ctx[g * span : (g + 1) * span]
        wide = jnp.broadcast_to(jnp.log2(total), (rows, HD))
        lse_ref[0, s : s + 1, :] = wide.T[0:1]


def attend_back_kernel(
    span, sc, q_ref, do_ref, ctx_ref, lse_ref, k0, k1, v0, v1, dq_ref, dk0, dk1, dv0, dv1, k_s, v_s, dk_s, dv_s, dq_s
):
    half = k0.shape[0]
    k_s[:half] = k0[...]
    k_s[half:] = k1[...]
    v_s[:half] = v0[...]
    v_s[half:] = v1[...]
    dk_s[...] = jnp.zeros_like(dk_s)
    dv_s[...] = jnp.zeros_like(dv_s)
    group = q_ref.shape[1] // HD
    rows = span * group
    for s in range(2):
        top = slice(s * span, (s + 1) * span)

        def stacked(ref):
            return jnp.concatenate([ref[top, g * HD : (g + 1) * HD] for g in range(group)], axis=0)

        q = stacked(q_ref)
        do = stacked(do_ref)
        q_t = q.T
        do_t = do.T
        product = do.astype(F32) * stacked(ctx_ref).astype(F32)
        delta = jnp.sum(product.T, axis=0, keepdims=True)
        lse = lse_ref[0, s : s + 1, :]
        dq_s[...] = jnp.zeros_like(dq_s)

        def step(p, masked):
            at = pl.ds(pl.multiple_of(sc[2 + p] * span, span), span)
            k = k_s[at, :]
            probs = jnp.exp2(dims(k, q_t, 1, 0) - lse)
            if masked:
                key = lax.broadcasted_iota(jnp.int32, (span, rows), 0)
                query = lax.broadcasted_iota(jnp.int32, (span, rows), 1) % span
                probs = jnp.where(query >= key, probs, 0.0)
            dv_s[at, :] += dims(probs.astype(BF16), do, 1, 0)
            grad = (probs * (dims(v_s[at, :], do_t, 1, 0) - delta)).astype(BF16)
            dk_s[at, :] += dims(grad, q, 1, 0)
            dq_s[...] += dims(grad, k, 0, 0)

        pl.loop(0, sc[s])(lambda p: step(p, False))
        step(sc[s], True)
        dq = dq_s[...] * (HD**-0.5)
        for g in range(group):
            dq_ref[top, g * HD : (g + 1) * HD] = dq[g * span : (g + 1) * span]
    dk0[...] = (dk_s[:half] * LN2).astype(BF16)
    dk1[...] = (dk_s[half:] * LN2).astype(BF16)
    dv0[...] = dv_s[:half].astype(BF16)
    dv1[...] = dv_s[half:].astype(BF16)


def attend(scalars, queries, keys, values, span):
    rows, width = queries.shape
    kv_local = keys[0].shape[1] // HD
    across = width // kv_local
    half = keys[0].shape[0]
    wide = pl.BlockSpec((rows, across), lambda h, sc: (0, h))
    slots = pl.Buffered(2 if half <= 4096 else 1)
    tall = pl.BlockSpec((half, HD), lambda h, sc: (0, h))
    read = pl.BlockSpec((half, HD), lambda h, sc: (0, h), pipeline_mode=slots)
    stacked = across // HD * span
    flops = 4 * rows * half * width
    return pl.pallas_call(
        functools.partial(attend_kernel, span),
        grid_spec=pltpu.PrefetchScalarGridSpec(
            num_scalar_prefetch=1,
            grid=(kv_local,),
            in_specs=[wide, read, read, read, read],
            out_specs=[wide, pl.BlockSpec((1, 2, stacked), lambda h, sc: (h, 0, 0))],
            scratch_shapes=[
                pltpu.VMEM((2 * half, HD), BF16),
                pltpu.VMEM((2 * half, HD), BF16),
                pltpu.VMEM((stacked, HD), F32),
                pltpu.VMEM((stacked, HD), F32),
            ],
        ),
        out_shape=[
            jax.ShapeDtypeStruct((rows, width), BF16),
            jax.ShapeDtypeStruct((kv_local, 2, stacked), F32),
        ],
        compiler_params=pltpu.CompilerParams(vmem_limit_bytes=min(60 * MIB, 16 * MIB + 44 * HD * half)),
        cost_estimate=pl.CostEstimate(
            flops=4 * flops, bytes_accessed=16 * half * HD, transcendentals=rows * half
        ),
        name="attend",
    )(scalars, queries, *keys, *values)


def attend_back(scalars, queries, grad_context, context, lse, keys, values, span):
    rows, width = queries.shape
    kv_local = keys[0].shape[1] // HD
    across = width // kv_local
    half = keys[0].shape[0]
    wide = pl.BlockSpec((rows, across), lambda h, sc: (0, h))
    slots = pl.Buffered(2 if half <= 4096 else 1)
    tall = pl.BlockSpec((half, HD), lambda h, sc: (0, h))
    read = pl.BlockSpec((half, HD), lambda h, sc: (0, h), pipeline_mode=slots)
    stacked = across // HD * span
    flops = 10 * rows * half * width
    grads = jax.ShapeDtypeStruct(keys[0].shape, BF16)
    return pl.pallas_call(
        functools.partial(attend_back_kernel, span),
        grid_spec=pltpu.PrefetchScalarGridSpec(
            num_scalar_prefetch=1,
            grid=(kv_local,),
            in_specs=[wide, wide, wide, pl.BlockSpec((1, 2, stacked), lambda h, sc: (h, 0, 0))]
            + [read] * 4,
            out_specs=[wide] + [tall] * 4,
            scratch_shapes=[
                pltpu.VMEM((2 * half, HD), BF16),
                pltpu.VMEM((2 * half, HD), BF16),
                pltpu.VMEM((2 * half, HD), F32),
                pltpu.VMEM((2 * half, HD), F32),
                pltpu.VMEM((stacked, HD), F32),
            ],
        ),
        out_shape=[jax.ShapeDtypeStruct((rows, width), F32)] + [grads] * 4,
        compiler_params=pltpu.CompilerParams(vmem_limit_bytes=min(60 * MIB, 16 * MIB + 44 * HD * half)),
        cost_estimate=pl.CostEstimate(
            flops=4 * flops, bytes_accessed=32 * half * HD, transcendentals=rows * half
        ),
        name="attend_back",
    )(scalars, queries, grad_context, context, lse, *keys, *values)


def shards(
    tokens,
    span_order,
    input_gain,
    query_weight,
    key_weight,
    value_weight,
    query_gain,
    key_gain,
    output_weight,
    post_gain,
    gate_weight,
    up_weight,
    down_weight,
    cotangent,
):
    n = lax.axis_size("blk")
    me = lax.axis_index("blk")
    bits = high_bits(n)
    flipped = bits[::-1]
    masks = mask_order(n)
    rows, width = tokens.shape
    block = width // n
    split = width // 2
    span = rows // 2
    q_cols = query_weight.shape[1]
    kv_cols = key_weight.shape[1]
    heads = q_cols // HD
    kv_heads = kv_cols // HD
    units = gate_weight.shape[1]
    o_cols = output_weight.shape[0]

    def in_masks(array):
        return jnp.concatenate(
            [lax.dynamic_slice_in_dim(array, (me ^ m) * block, block, 1) for m in masks], axis=1
        )

    def in_blocks(array):
        places = [((me ^ j) >> 1) + ((me ^ j) & 1) * (n // 2) for j in range(n)]
        return jnp.concatenate(
            [lax.dynamic_slice_in_dim(array, p * block, block, 1) for p in places], axis=1
        )

    gains = jnp.concatenate([input_gain, post_gain, query_gain, key_gain]).reshape(1, -1)
    gains = jnp.concatenate(gather_rows(gains, bits), axis=0).astype(F32)
    wq = gather_rows(query_weight, bits)
    wkv = gather_rows(jnp.concatenate([key_weight, value_weight], axis=1), flipped)
    gain_input = gains[:, :block].reshape(1, width)
    gain_post = gains[:, block : 2 * block].reshape(1, width)
    chosen = (me ^ jnp.arange(n))[:, None] == jnp.array(masks)[None, :]
    head_gains = jnp.sum(jnp.where(chosen[:, :, None], gains[None, :, 2 * block :], 0.0), axis=1)
    part = head_gains.shape[1] // 2
    gain_query = head_gains[:, :part].reshape(HD)
    gain_key = head_gains[:, part:].reshape(HD)

    tokens = in_masks(tokens)
    cotangent = in_masks(cotangent)
    inputs = tokens.astype(F32)
    normed, scale_in = row_norm(inputs, gain_input)
    normed_low = normed.astype(BF16)

    def project(left, pair):
        return dims(left[:, :split], pair[0], 1, 0) + dims(left[:, split:], pair[1], 1, 0)

    q_proj = project(normed_low, wq).reshape(rows, heads, HD)
    kv_proj = project(normed_low, wkv)
    k_proj = kv_proj[:, :kv_cols].reshape(rows, kv_heads, HD)

    spans = span_order.reshape(n, 2)
    chunk_ids = jnp.sum(
        jnp.where(
            (me ^ jnp.array(masks))[:, None, None] == jnp.arange(n)[None, :, None], spans[None], 0
        ),
        axis=1,
    ).reshape(-1)
    count = 2 * n
    positions = jnp.sum(
        jnp.where(
            chunk_ids[None, :] == jnp.arange(count)[:, None], jnp.arange(count)[None, :], 0
        ),
        axis=1,
    )
    scalars = jnp.concatenate([chunk_ids[:2], positions]).astype(jnp.int32)
    places = (chunk_ids[:2, None] * span + jnp.arange(span)[None, :]).reshape(-1)
    cosine, sine = rope_tables(places, HD)
    cosine, sine = cosine[:, None, :], sine[:, None, :]

    def rotate(values):
        return values * cosine + turned(values) * sine

    def rotate_back(grads):
        return grads * cosine + turned(grads * sine)

    q_normed, q_scale = row_norm(q_proj, gain_query)
    queries = (rotate(q_normed) * (HD**-0.5 * LOG2E)).astype(BF16).reshape(rows, q_cols)
    k_normed, k_scale = row_norm(k_proj, gain_key)
    keys = rotate(k_normed).astype(BF16).reshape(rows, kv_cols)
    values = kv_proj[:, kv_cols:].astype(BF16)
    all_keys = gather_rows(keys, bits)
    all_values = gather_rows(values, flipped)

    down_t = down_weight.T
    cut = (units - o_cols) // 2
    side_a = jnp.concatenate([output_weight.T, down_t[:, :cut]], axis=1)
    side_b = down_t[:, cut:]
    side_a, side_b, _ = lax.optimization_barrier((side_a, side_b, wkv[1]))
    side_a = gather_rows(side_a, bits)
    side_b = gather_rows(side_b, flipped)
    wo = [w[:, :o_cols] for w in side_a]
    wd_a = [w[:, o_cols:] for w in side_a]
    wd_b = side_b
    wg = gather_rows(gate_weight, bits)
    wu = gather_rows(up_weight, flipped)

    context, lse = attend(scalars, queries, all_keys, all_values, span)

    attn_part = jnp.concatenate([dims(context, w, 1, 1) for w in wo], axis=1).astype(BF16)
    attn = lax.psum(attn_part, "fsdp").astype(F32)
    hidden = inputs + attn
    post, scale_post = row_norm(hidden, gain_post)
    post_low = post.astype(BF16)
    grad_act = jnp.concatenate([project(cotangent, wd_a), project(cotangent, wd_b)], axis=1)
    gate = project(post_low, wg)
    up = project(post_low, wu)
    sigma = jax.nn.sigmoid(gate)
    silu = gate * sigma
    act = (silu * up).astype(BF16)
    grad_up = (grad_act * silu).astype(BF16)
    grad_gate = (grad_act * up * sigma * (1.0 + gate * (1.0 - sigma))).astype(BF16)
    post_part = jnp.concatenate(
        [dims(grad_gate, g, 1, 1) + dims(grad_up, u, 1, 1) for g, u in zip(wg, wu)], axis=1
    ).astype(BF16)
    grad_post = lax.psum(post_part, "fsdp").astype(F32)
    mlp_part = jnp.concatenate(
        [dims(act[:, :cut], a, 1, 1) + dims(act[:, cut:], b, 1, 1) for a, b in zip(wd_a, wd_b)],
        axis=1,
    ).astype(BF16)
    mlp_part, grad_post = lax.optimization_barrier((mlp_part, grad_post))
    mlp = lax.psum(mlp_part, "fsdp").astype(F32)
    layer_out = in_blocks((hidden + mlp).astype(BF16))

    def weight_grad(left, right, order):
        away = dims(left[:, split:], right, 0, 0).astype(BF16)
        home = dims(left[:, :split], right, 0, 0).astype(BF16)
        return scatter_sum(home, exchange(away, 1), order)

    middle = units // 2
    down_a = weight_grad(cotangent, act[:, :middle], bits)
    down_b = weight_grad(cotangent, act[:, middle:], flipped)
    gate_sum = weight_grad(post_low, grad_gate, bits)
    up_sum = weight_grad(post_low, grad_up, flipped)
    down_sum = jnp.concatenate([down_a, down_b], axis=1).T

    grad_hidden = cotangent.astype(F32) + norm_back(hidden, scale_post, grad_post * gain_post)
    hidden_low = grad_hidden.astype(BF16)
    grad_context = (
        dims(hidden_low[:, :split], wo[0], 1, 0) + dims(hidden_low[:, split:], wo[1], 1, 0)
    ).astype(BF16)
    dq, dk_own, dk_other, dv_own, dv_other = attend_back(
        scalars, queries, grad_context, context, lse, all_keys, all_values, span
    )
    grad_k = scatter_sum(dk_own, exchange(dk_other, 1), bits).reshape(rows, kv_heads, HD)
    grad_v = scatter_sum(dv_own, exchange(dv_other, 1), flipped)

    rotated_q = rotate_back(dq.reshape(rows, heads, HD))
    q_gain_part = jnp.sum(rotated_q * q_proj * q_scale, axis=(0, 1))
    grad_q_low = norm_back(q_proj, q_scale, rotated_q * gain_query)
    grad_q_low = grad_q_low.astype(BF16).reshape(rows, q_cols)
    rotated_k = rotate_back(grad_k)
    k_gain_part = jnp.sum(rotated_k * k_proj * k_scale, axis=(0, 1))
    grad_k_low = norm_back(k_proj, k_scale, rotated_k * gain_key).astype(BF16)
    grad_kv_low = jnp.concatenate(
        [grad_k_low.reshape(rows, kv_cols), grad_v.astype(BF16)], axis=1
    )
    normed_part = jnp.concatenate(
        [dims(grad_q_low, q, 1, 1) + dims(grad_kv_low, kv, 1, 1) for q, kv in zip(wq, wkv)],
        axis=1,
    ).astype(BF16)
    grad_normed = lax.psum(normed_part, "fsdp").astype(F32)

    o_half = o_cols // 2
    qo = weight_grad_two(
        (normed_low, grad_q_low), (hidden_low, context[:, :o_half]), split, bits
    )
    kvo = weight_grad_two(
        (normed_low, grad_kv_low), (hidden_low, context[:, o_half:]), split, flipped
    )
    query_sum = qo[:, :q_cols]
    key_sum = kvo[:, :kv_cols]
    value_sum = kvo[:, kv_cols : 2 * kv_cols]
    out_sum = jnp.concatenate([qo[:, q_cols:], kvo[:, 2 * kv_cols :]], axis=1).T

    def along_rows(weight, grad):
        return jnp.sum(weight.astype(F32) * grad, axis=1)

    input_gain_part = (
        along_rows(query_weight, query_sum)
        + along_rows(key_weight, key_sum)
        + along_rows(value_weight, value_sum)
    ) / input_gain.astype(F32)
    post_gain_part = (
        along_rows(gate_weight, gate_sum) + along_rows(up_weight, up_sum)
    ) / post_gain.astype(F32)
    mine = (jnp.arange(n) == me)[:, None]
    widths = jnp.concatenate([input_gain_part, post_gain_part])[None, :]
    small = jnp.concatenate(
        [
            jnp.where(mine, widths, 0.0),
            jnp.concatenate([q_gain_part.reshape(n, -1), k_gain_part.reshape(n, -1)], axis=1),
        ],
        axis=1,
    )
    small = lax.dynamic_slice_in_dim(lax.psum(small, ("blk", "fsdp")), me, 1, 0)[0]
    head = HD // n

    tokens_grad = in_blocks(grad_hidden + norm_back(inputs, scale_in, grad_normed * gain_input))
    return (
        layer_out,
        tokens_grad,
        small[:block],
        query_sum,
        key_sum,
        value_sum,
        small[2 * block : 2 * block + head],
        small[2 * block + head :],
        out_sum,
        small[block : 2 * block],
        gate_sum,
        up_sum,
        down_sum,
    )


def weight_grad_two(first, second, split, order):
    def side(columns):
        return jnp.concatenate(
            [dims(left[:, columns], right, 0, 0) for left, right in (first, second)], axis=1
        ).astype(BF16)

    away = side(slice(split, None))
    home = side(slice(0, split))
    return scatter_sum(home, exchange(away, 1), order)


def solution(mesh):
    placed = (
        P("blk", None),
        P(),
        P("blk"),
        P("blk", "fsdp"),
        P("blk", "fsdp"),
        P("blk", "fsdp"),
        P("blk"),
        P("blk"),
        P("fsdp", "blk"),
        P("blk"),
        P("blk", "fsdp"),
        P("blk", "fsdp"),
        P("fsdp", "blk"),
        P("blk", None),
    )
    return jax.shard_map(
        shards,
        mesh=mesh,
        in_specs=placed,
        out_specs=(
            P("blk", None),
            P("blk", None),
            P("blk"),
            P("blk", "fsdp"),
            P("blk", "fsdp"),
            P("blk", "fsdp"),
            P("blk"),
            P("blk"),
            P("fsdp", "blk"),
            P("blk"),
            P("blk", "fsdp"),
            P("blk", "fsdp"),
            P("fsdp", "blk"),
        ),
        check_vma=False,
    )
```

```python
import functools
import math

import jax
import jax.numpy as jnp
from jax import lax
from jax.experimental import pallas as pl
from jax.experimental.pallas import tpu as pltpu
from jax.sharding import PartitionSpec as P

HD = 128
EPS = 1e-06
THETA = 1000000.0
LOG2E = math.log2(math.e)
LN2 = math.log(2.0)
MIB = 1024 * 1024

F32 = jnp.float32
BF16 = jnp.bfloat16


def dims(lhs, rhs, left, right):
    return lax.dot_general(lhs, rhs, (((left,), (right,)), ((), ())), preferred_element_type=F32)


def mask_order(n):
    return [2 * i for i in range(n // 2)] + [2 * i + 1 for i in range(n // 2)]


def high_bits(n):
    return [1 << i for i in range(1, n.bit_length() - 1)]


def exchange(block, bit):
    n = lax.axis_size("blk")
    return lax.ppermute(block, "blk", [(i, i ^ bit) for i in range(n)])


def together(values, others=()):
    return lax.optimization_barrier((*values, *others))[: len(values)]


def after(value, *others):
    return lax.optimization_barrier((value,) + others)[0]


def gather_rows(pieces, orders, before=(), beside=(), closing=()):
    count = len(pieces)
    held = [{0: piece} for piece in pieces]
    gots = []
    for step in range(len(orders[0])):
        sent = []
        for have in held:
            one = [have[m] for m in sorted(have)]
            sent.append(one[0] if len(one) == 1 else jnp.concatenate(one, axis=0))
        sent = together(sent, before[step] if step < len(before) else ())
        got = [exchange(x, order[step]) for x, order in zip(sent, orders)]
        gots.append(got)
        last = step == len(orders[0]) - 1
        got = together(got, (beside[step] if step < len(beside) else ()) + (tuple(closing) if last else ()))
        for have, brought, order in zip(held, got, orders):
            rows = have[0].shape[0]
            for i, m in enumerate(sorted(have)):
                have[m | order[step]] = brought[i * rows : (i + 1) * rows]
    own = [jnp.concatenate([have[m] for m in sorted(have)], axis=0) for have in held]
    return [(x, exchange(x, 1)) for x in own], gots


def add_low(a, b):
    return (a.astype(F32) + b.astype(F32)).astype(BF16)


def scatter_terms(parts, orders):
    held = []
    sent = [part[0] for part in parts]
    for (leave, stay), order in zip(parts, orders):
        masks = [m for m in range(0, 4 * stay.shape[0], 2) if not m & order[0]][: 2 ** (len(order) - 1)]
        rows = stay.shape[0] // len(masks)
        held.append({m: stay[i * rows : (i + 1) * rows] for i, m in enumerate(masks)})
    sends, gots = [], []
    for step in range(len(orders[0])):
        if step:
            sent = []
            for have, order in zip(held, orders):
                leave = [add_low(*have.pop(m)) for m in sorted(have) if m & order[step]]
                sent.append(leave[0] if len(leave) == 1 else jnp.concatenate(leave, axis=0))
                for m in have:
                    have[m] = add_low(*have[m])
        sent = together(sent)
        sends.append(sent)
        got = together([exchange(x, order[step]) for x, order in zip(sent, orders)])
        gots.append(got)
        for have, back in zip(held, got):
            rows = back.shape[0] // len(have)
            for i, m in enumerate(sorted(have)):
                have[m] = (have[m], back[i * rows : (i + 1) * rows])
    return [have[0] for have in held], sends, gots


def scatter_sums(parts, orders):
    terms, sends, gots = scatter_terms(parts, orders)
    return [a.astype(F32) + b.astype(F32) for a, b in terms], sends, gots


def leaving_first(n, bit):
    masks = [2 * i for i in range(n // 2)]
    return [i for i, m in enumerate(masks) if m & bit] + [i for i, m in enumerate(masks) if not m & bit]


def split_sum(own, got, n, bit):
    rows = own.shape[0] // (n // 2)
    at = leaving_first(n, bit)

    def part(array, which):
        return jnp.concatenate([array[i * rows : (i + 1) * rows] for i in which], axis=0)

    half = len(at) // 2
    return tuple(add_low(part(own, w), part(got, w)) for w in (at[:half], at[half:]))


def norm_scale(values):
    return lax.rsqrt(jnp.mean(values * values, axis=-1, keepdims=True) + EPS)


def norm_back(values, scale, weighted):
    inner = jnp.mean(weighted * values, axis=-1, keepdims=True)
    return scale * (weighted - values * scale * scale * inner)


def rope_tables(places, width):
    half = width // 2
    freqs = THETA ** (-jnp.arange(half, dtype=F32) * 2.0 / width)
    angles = places.astype(F32)[:, None] * freqs[None, :]
    sine = jnp.sin(angles)
    cosine = jnp.cos(angles)
    return (jnp.concatenate([cosine, cosine], axis=1), jnp.concatenate([-sine, sine], axis=1))


def turned(values):
    return pltpu.roll(values, HD // 2, 1)


def call(kernel, name, grid, in_specs, out_specs, out_shape, args, flops, scratch=(), scalars=None):
    if scalars is None:
        spec = {"grid": grid, "in_specs": in_specs, "out_specs": out_specs, "scratch_shapes": scratch}
    else:
        spec = {
            "grid_spec": pltpu.PrefetchScalarGridSpec(
                num_scalar_prefetch=1,
                grid=grid,
                in_specs=in_specs,
                out_specs=out_specs,
                scratch_shapes=scratch,
            )
        }
        args = (scalars,) + tuple(args)
    return pl.pallas_call(
        kernel,
        out_shape=out_shape,
        compiler_params=pltpu.CompilerParams(vmem_limit_bytes=28 * MIB),
        cost_estimate=pl.CostEstimate(flops=0, bytes_accessed=0, transcendentals=0),
        name=name,
        **spec,
    )(*args)


def shape(dims_, dtype):
    return jax.ShapeDtypeStruct(dims_, dtype)


def picked(array, order):
    n = order.shape[0]
    block = array.shape[1] // n
    return jnp.concatenate(
        [lax.dynamic_slice_in_dim(array, order[i] * block, block, 1) for i in range(n)], axis=1
    )


def enter_kernel(sc, a_ref, b_ref, a_out, b_out):
    a_out[...] = a_ref[...]
    b_out[...] = b_ref[...]


def enter(order, first, second):
    rows, width = first.shape
    n = order.shape[0]
    block = width // n
    if block % 128:
        return picked(first, order), picked(second, order)
    source = pl.BlockSpec((rows, block), lambda p, sc: (0, sc[p]))
    target = pl.BlockSpec((rows, block), lambda p, sc: (0, p))
    return call(
        enter_kernel,
        "enter",
        (n,),
        [source, source],
        [target, target],
        [shape(first.shape, first.dtype), shape(second.shape, second.dtype)],
        (first, second),
        0,
        scalars=order,
    )


def leave_blocks(sc, out_ref, result):
    width = result.shape[1]
    n = sc.shape[0]
    block = width // n
    if block % 128:
        out_ref[...] = result.astype(out_ref.dtype)
        return
    for p in range(n):
        at = pl.ds(pl.multiple_of(sc[p] * block, 128), block)
        out_ref[:, at] = result[:, p * block : (p + 1) * block].astype(out_ref.dtype)


def leave_kernel(sc, *refs):
    count = len(refs) // 2
    for value_ref, out_ref in zip(refs[:count], refs[count:]):
        leave_blocks(sc, out_ref, value_ref[...])


def leave(name, order, value, dtype):
    rows, width = value.shape
    n = order.shape[0]
    height = rows // 4
    spec = pl.BlockSpec((height, width), lambda i, sc: (i, 0))
    result = call(
        leave_kernel, name, (4,), [spec], [spec], [shape((rows, width), dtype)], (value,), 0, scalars=order
    )[0]
    if width // n % 128:
        index = jnp.arange(n)
        back = jnp.sum(jnp.where(order[None, :] == index[:, None], index[None, :], 0), axis=1)
        return picked(result, back)
    return result


def post_kernel(tokens_ref, attn_ref, gain_ref, out_ref):
    hidden = tokens_ref[...].astype(F32) + attn_ref[...].astype(F32)
    out_ref[...] = (hidden * norm_scale(hidden) * gain_ref[...]).astype(BF16)


def layer_out_kernel(tokens_ref, attn_ref, mlp_ref, out_ref):
    hidden = tokens_ref[...].astype(F32) + attn_ref[...].astype(F32)
    out_ref[...] = (hidden + mlp_ref[...].astype(F32)).astype(BF16)


def grad_hidden_kernel(tokens_ref, attn_ref, cotangent_ref, grad_ref, gain_ref, out_ref, low_ref):
    hidden = tokens_ref[...].astype(F32) + attn_ref[...].astype(F32)
    weighted = grad_ref[...].astype(F32) * gain_ref[...]
    grad = cotangent_ref[...].astype(F32) + norm_back(hidden, norm_scale(hidden), weighted)
    out_ref[...] = grad
    low_ref[...] = grad.astype(BF16)


def tokens_grad_kernel(tokens_ref, hidden_ref, grad_ref, gain_ref, out_ref):
    inputs = tokens_ref[...].astype(F32)
    weighted = grad_ref[...].astype(F32) * gain_ref[...]
    back = norm_back(inputs, norm_scale(inputs), weighted)
    out_ref[...] = (hidden_ref[...] + back).astype(BF16)


def on_quarter(kernel, name, arrays, gains, dtypes):
    rows, width = arrays[0].shape
    spec = pl.BlockSpec((rows, width), lambda i: (0, 0))
    full = [pl.BlockSpec(g.shape, lambda i: (0, 0)) for g in gains]
    return call(
        kernel,
        name,
        (1,),
        [spec] * len(arrays) + full,
        [spec] * len(dtypes),
        [shape((rows, width), dtype) for dtype in dtypes],
        tuple(arrays) + tuple(gains),
        0,
    )


def project_kernel(
    q_steps, split, tokens_ref, gain_ref, wq0, wq1, wkv0, wkv1, cos_ref, sin_ref, gq_ref, gk_ref,
    normed_ref, q_proj, k_proj, queries, keys, values,
):
    j = pl.program_id(0)

    @pl.when(j == 0)
    def _():
        inputs = tokens_ref[...].astype(F32)
        normed_ref[...] = (inputs * norm_scale(inputs) * gain_ref[...]).astype(BF16)

    def product(w0, w1):
        return dims(normed_ref[:, :split], w0[...], 1, 0) + dims(normed_ref[:, split:], w1[...], 1, 0)

    def heads(proj, proj_ref, out_ref, gain, factor):
        proj_ref[...] = proj
        for h in range(proj.shape[1] // HD):
            one = slice(h * HD, (h + 1) * HD)
            u = proj[:, one]
            u = u * norm_scale(u) * gain
            u = u * cos_ref[...] + turned(u) * sin_ref[...]
            out_ref[:, one] = (u * factor if factor else u).astype(BF16)

    @pl.when(j < q_steps)
    def _():
        heads(product(wq0, wq1), q_proj, queries, gq_ref[...], HD**-0.5 * LOG2E)

    @pl.when(j == q_steps)
    def _():
        heads(product(wkv0, wkv1), k_proj, keys, gk_ref[...], None)

    @pl.when(j == q_steps + 1)
    def _():
        values[...] = product(wkv0, wkv1).astype(BF16)


def projections(tokens, gain, wq, wkv, cosine, sine, gain_query, gain_key):
    rows, width = tokens.shape
    q_cols = wq[0].shape[1]
    kv_cols = wkv[0].shape[1] // 2
    steps = q_cols // kv_cols
    split = width // 2

    def whole(array):
        return pl.BlockSpec(array.shape, lambda j: (0, 0))

    q_tile = pl.BlockSpec((split, kv_cols), lambda j: (0, jnp.minimum(j, steps - 1)))
    kv_tile = pl.BlockSpec((split, kv_cols), lambda j: (0, jnp.maximum(j - steps, 0)))
    q_out = pl.BlockSpec((rows, kv_cols), lambda j: (0, jnp.minimum(j, steps - 1)))
    kv_out = pl.BlockSpec((rows, kv_cols), lambda j: (0, 0))
    small = [cosine, sine, gain_query, gain_key]
    return call(
        functools.partial(project_kernel, steps, split),
        "projections",
        (steps + 2,),
        [whole(tokens), whole(gain), q_tile, q_tile, kv_tile, kv_tile] + [whole(a) for a in small],
        [whole(tokens), q_out, kv_out, q_out, kv_out, kv_out],
        [
            shape((rows, width), BF16),
            shape((rows, q_cols), F32),
            shape((rows, kv_cols), F32),
            shape((rows, q_cols), BF16),
            shape((rows, kv_cols), BF16),
            shape((rows, kv_cols), BF16),
        ],
        (tokens, gain, *wq, *wkv, *small),
        2 * rows * width * (q_cols + 2 * kv_cols),
    )


def to_width_kernel(count, half, *refs):
    i = pl.program_id(0)
    lefts = refs[:count]
    rights = refs[count : 3 * count]
    out_ref = refs[-1]
    for parity, here in ((0, i < half), (1, i >= half)):

        @pl.when(here)
        def _(parity=parity):
            total = None
            for left, pair in zip(lefts, zip(rights[::2], rights[1::2])):
                term = dims(left[...], pair[parity][...], 1, 1)
                total = term if total is None else total + term
            out_ref[...] = total.astype(out_ref.dtype)


def to_width(name, *terms, tile=256):
    rows = terms[0][0].shape[0]
    split = terms[0][2][0].shape[0]
    half = split // tile
    in_specs = []
    for left, at, pair, where, columns in terms:
        in_specs.append(pl.BlockSpec((rows, columns), lambda i, at=at: (0, at)))
    args = [t[0] for t in terms]
    flops = 0
    for left, at, pair, where, columns in terms:
        in_specs.append(
            pl.BlockSpec((tile, columns), lambda i, w=where: (jnp.minimum(i, half - 1), w))
        )
        in_specs.append(
            pl.BlockSpec((tile, columns), lambda i, w=where: (jnp.maximum(i - half, 0), w))
        )
        args += list(pair)
        flops += 4 * rows * split * columns
    return call(
        functools.partial(to_width_kernel, len(terms), half),
        name,
        (2 * half,),
        in_specs,
        [pl.BlockSpec((rows, tile), lambda i: (0, i))],
        [shape((rows, 2 * split), BF16)],
        tuple(args),
        flops,
    )[0]


def from_width_kernel(split, bounds, left_ref, *refs):
    out_ref = refs[-1]
    j = pl.program_id(0)
    for k in range(len(bounds) - 1):

        @pl.when((j >= bounds[k]) & (j < bounds[k + 1]))
        def _(w0=refs[2 * k], w1=refs[2 * k + 1]):
            product = dims(left_ref[:, :split], w0[...], 1, 0) + dims(left_ref[:, split:], w1[...], 1, 0)
            out_ref[...] = product.astype(out_ref.dtype)


def from_width(name, left, *sides, tile=256):
    rows, width = left.shape
    split = width // 2
    bounds = [0]
    specs, args = [], [left]
    for pair, start, columns in sides:
        low, high = bounds[-1], bounds[-1] + columns // tile
        bounds.append(high)
        specs += [
            pl.BlockSpec(
                (split, tile),
                lambda j, low=low, high=high, first=start // tile: (0, first + jnp.clip(j, low, high - 1) - low),
            )
        ] * 2
        args += list(pair)
    return call(
        functools.partial(from_width_kernel, split, tuple(bounds)),
        name,
        (bounds[-1],),
        [pl.BlockSpec((rows, width), lambda j: (0, 0))] + specs,
        [pl.BlockSpec((rows, tile), lambda j: (0, j))],
        [shape((rows, bounds[-1] * tile), BF16)],
        tuple(args),
        2 * rows * width * bounds[-1] * tile,
    )[0]


def units_kernel(split, post_ref, wg0, wg1, wu0, wu1, grad_ref, act_ref, gate_out, up_out):
    def product(w0, w1):
        return dims(post_ref[:, :split], w0[...], 1, 0) + dims(post_ref[:, split:], w1[...], 1, 0)

    gate = product(wg0, wg1)
    up = product(wu0, wu1)
    grad_act = grad_ref[...].astype(F32)
    sigma = jax.nn.sigmoid(gate)
    silu = gate * sigma
    act_ref[...] = (silu * up).astype(BF16)
    up_out[...] = (grad_act * silu).astype(BF16)
    gate_out[...] = (grad_act * up * sigma * (1.0 + gate * (1.0 - sigma))).astype(BF16)


def hidden_units(post, wg, wu, grad_act, tile=256):
    rows, width = post.shape
    units = grad_act.shape[1]
    split = width // 2
    side = pl.BlockSpec((split, tile), lambda j: (0, j))
    part = pl.BlockSpec((rows, tile), lambda j: (0, j))
    unit = shape((rows, units), BF16)
    return call(
        functools.partial(units_kernel, split),
        "hidden_units",
        (units // tile,),
        [pl.BlockSpec(post.shape, lambda j: (0, 0)), side, side, side, side, part],
        [part, part, part],
        [unit, unit, unit],
        (post, *wg, *wu, grad_act),
        4 * rows * width * units,
    )


def away_kernel(count, *refs):
    out_ref = refs[-1]
    start = 0
    for left, right in zip(refs[:count], refs[count : 2 * count]):
        columns = right.shape[1]
        out_ref[:, start : start + columns] = dims(left[...].T, right[...], 1, 0).astype(BF16)
        start += columns


def home_kernel(count, leaving, sc, *refs):
    got_ref, leave_ref, stay_ref = refs[2 * count :]
    step = pl.program_id(0)
    for out_ref, here in ((leave_ref, step < leaving), (stay_ref, step >= leaving)):

        @pl.when(here)
        def _(out_ref=out_ref):
            start = 0
            for left, right in zip(refs[:count], refs[count : 2 * count]):
                columns = right.shape[1]
                at = slice(start, start + columns)
                term = dims(left[...].T, right[...], 1, 0) + got_ref[:, at].astype(F32)
                out_ref[:, at] = term.astype(BF16)
                start += columns


def weight_grad(name, n, bit, *pairs):
    rows, width = pairs[0][0].shape
    split = width // 2
    total = sum(p[3] for p in pairs)
    flops = rows * width * total
    right_specs = [(p[2], p[3]) for p in pairs]
    lefts = [p[0] for p in pairs]
    rights = [p[1] for p in pairs]
    tile = 256
    tiles = split // tile
    away = call(
        functools.partial(away_kernel, len(pairs)),
        name + "_away",
        (tiles,),
        [pl.BlockSpec((rows, tile), lambda i: (0, tiles + i))] * len(pairs)
        + [pl.BlockSpec((rows, c), lambda i, w=w: (0, w)) for w, c in right_specs],
        [pl.BlockSpec((tile, total), lambda i: (i, 0))],
        [shape((split, total), BF16)],
        (*lefts, *rights),
        flops,
    )[0]
    got = exchange(away, 1)
    block = width // n
    order = leaving_first(n, bit)
    leaving = len(order) // 2
    if block % 128:
        home = call(
            functools.partial(away_kernel, len(pairs)),
            name,
            (tiles,),
            [pl.BlockSpec((rows, tile), lambda i: (0, i))] * len(pairs)
            + [pl.BlockSpec((rows, c), lambda i, w=w: (0, w)) for w, c in right_specs],
            [pl.BlockSpec((tile, total), lambda i: (i, 0))],
            [shape((split, total), BF16)],
            (*lefts, *rights),
            flops,
        )[0]
        return split_sum(home, got, n, bit)
    return call(
        functools.partial(home_kernel, len(pairs), leaving),
        name,
        (len(order),),
        [pl.BlockSpec((rows, block), lambda i, sc: (0, sc[i]))] * len(pairs)
        + [pl.BlockSpec((rows, c), lambda i, sc, w=w: (0, w)) for w, c in right_specs]
        + [pl.BlockSpec((block, total), lambda i, sc: (sc[i], 0))],
        [
            pl.BlockSpec((block, total), lambda i, sc: (jnp.minimum(i, leaving - 1), 0)),
            pl.BlockSpec((block, total), lambda i, sc: (jnp.maximum(i - leaving, 0), 0)),
        ],
        [shape((split // 2, total), BF16)] * 2,
        (*lefts, *rights, got),
        flops,
        scalars=jnp.array(order, jnp.int32),
    )


def heads_back_kernel(terms, passed, *refs):
    grads, refs = refs[:terms], refs[terms:]
    others, refs = refs[:passed], refs[passed:]
    proj_ref, cos_ref, sin_ref, gain_ref, out_ref, sum_ref = refs
    columns = proj_ref.shape[1]
    total = None
    for h in range(columns // HD):
        one = slice(h * HD, (h + 1) * HD)
        grad = grads[0][:, one].astype(F32)
        for more in grads[1:]:
            grad = grad + more[:, one].astype(F32)
        grad = grad * cos_ref[...] + turned(grad * sin_ref[...])
        u = proj_ref[:, one]
        scale = norm_scale(u)
        term = jnp.sum((grad * u * scale).reshape(-1, 8, HD), axis=0)
        total = term if total is None else total + term
        out_ref[:, one] = norm_back(u, scale, grad * gain_ref[...]).astype(BF16)
    sum_ref[...] = total
    if passed:
        other = others[0][...].astype(F32)
        for more in others[1:]:
            other = other + more[...].astype(F32)
        out_ref[:, columns:] = other.astype(BF16)


def heads_back(name, grads, others, proj, cosine, sine, gain):
    rows, columns = proj.shape
    args = (*grads, *others, proj, cosine, sine, gain)
    total = columns + (others[0].shape[1] if others else 0)
    return call(
        functools.partial(heads_back_kernel, len(grads), len(others)),
        name,
        (1,),
        [pl.BlockSpec(a.shape, lambda i: (0, 0)) for a in args],
        [pl.BlockSpec((rows, total), lambda i: (0, 0)), pl.BlockSpec((8, HD), lambda i: (0, 0))],
        [shape((rows, total), BF16), shape((8, HD), F32)],
        args,
        20 * rows * columns,
    )


def attend_kernel(span, sc, q_ref, k0, k1, v0, v1, ctx_ref, lse_ref, k_s, v_s, acc_s, sum_s):
    half = k0.shape[0]
    k_s[:half] = k0[...]
    k_s[half:] = k1[...]
    v_s[:half] = v0[...]
    v_s[half:] = v1[...]
    group = q_ref.shape[1] // HD
    rows = span * group
    for s in range(2):
        top = slice(s * span, (s + 1) * span)
        q = jnp.concatenate([q_ref[top, g * HD : (g + 1) * HD] for g in range(group)], axis=0)
        acc_s[...] = jnp.zeros_like(acc_s)
        sum_s[...] = jnp.zeros_like(sum_s)

        def step(p, masked):
            at = pl.ds(pl.multiple_of(sc[2 + p] * span, span), span)
            e = jnp.exp2(dims(q, k_s[at, :], 1, 1))
            if masked:
                row = lax.broadcasted_iota(jnp.int32, (rows, span), 0) % span
                col = lax.broadcasted_iota(jnp.int32, (rows, span), 1)
                e = jnp.where(row >= col, e, 0.0)
            part = e[:, :HD]
            for c in range(HD, span, HD):
                part = part + e[:, c : c + HD]
            sum_s[...] += part
            acc_s[...] += dims(e.astype(BF16), v_s[at, :], 1, 0)

        pl.loop(0, sc[s])(lambda p: step(p, False))
        step(sc[s], True)
        total = jnp.sum(sum_s[...], axis=1, keepdims=True)
        ctx = (acc_s[...] / total).astype(BF16)
        for g in range(group):
            ctx_ref[top, g * HD : (g + 1) * HD] = ctx[g * span : (g + 1) * span]
        wide = jnp.broadcast_to(jnp.log2(total), (rows, HD))
        lse_ref[0, s : s + 1, :] = wide.T[0:1]


def attend_back_kernel(
    span, sc, q_ref, do_ref, ctx_ref, lse_ref, k0, k1, v0, v1, dq_ref, dk0, dk1, dv0, dv1, k_s, v_s, dk_s, dv_s, dq_s
):
    half = k0.shape[0]
    k_s[:half] = k0[...]
    k_s[half:] = k1[...]
    v_s[:half] = v0[...]
    v_s[half:] = v1[...]
    dk_s[...] = jnp.zeros_like(dk_s)
    dv_s[...] = jnp.zeros_like(dv_s)
    group = q_ref.shape[1] // HD
    rows = span * group
    for s in range(2):
        top = slice(s * span, (s + 1) * span)

        def stacked(ref):
            return jnp.concatenate([ref[top, g * HD : (g + 1) * HD] for g in range(group)], axis=0)

        q = stacked(q_ref)
        do = stacked(do_ref)
        q_t = q.T
        do_t = do.T
        product = do.astype(F32) * stacked(ctx_ref).astype(F32)
        delta = jnp.sum(product.T, axis=0, keepdims=True)
        lse = lse_ref[0, s : s + 1, :]
        dq_s[...] = jnp.zeros_like(dq_s)

        def step(p, masked):
            at = pl.ds(pl.multiple_of(sc[2 + p] * span, span), span)
            k = k_s[at, :]
            probs = jnp.exp2(dims(k, q_t, 1, 0) - lse)
            if masked:
                key = lax.broadcasted_iota(jnp.int32, (span, rows), 0)
                query = lax.broadcasted_iota(jnp.int32, (span, rows), 1) % span
                probs = jnp.where(query >= key, probs, 0.0)
            dv_s[at, :] += dims(probs.astype(BF16), do, 1, 0)
            grad = (probs * (dims(v_s[at, :], do_t, 1, 0) - delta)).astype(BF16)
            dk_s[at, :] += dims(grad, q, 1, 0)
            dq_s[...] += dims(grad, k, 0, 0)

        pl.loop(0, sc[s])(lambda p: step(p, False))
        step(sc[s], True)
        dq = dq_s[...] * (HD**-0.5)
        for g in range(group):
            dq_ref[top, g * HD : (g + 1) * HD] = dq[g * span : (g + 1) * span]
    dk0[...] = (dk_s[:half] * LN2).astype(BF16)
    dk1[...] = (dk_s[half:] * LN2).astype(BF16)
    dv0[...] = dv_s[:half].astype(BF16)
    dv1[...] = dv_s[half:].astype(BF16)


def attend(scalars, queries, keys, values, span):
    rows, width = queries.shape
    kv_local = keys[0].shape[1] // HD
    across = width // kv_local
    half = keys[0].shape[0]
    wide = pl.BlockSpec((rows, across), lambda h, sc: (0, h))
    slots = pl.Buffered(2 if half <= 4096 else 1)
    tall = pl.BlockSpec((half, HD), lambda h, sc: (0, h))
    read = pl.BlockSpec((half, HD), lambda h, sc: (0, h), pipeline_mode=slots)
    stacked = across // HD * span
    flops = 4 * rows * half * width
    return pl.pallas_call(
        functools.partial(attend_kernel, span),
        grid_spec=pltpu.PrefetchScalarGridSpec(
            num_scalar_prefetch=1,
            grid=(kv_local,),
            in_specs=[wide, read, read, read, read],
            out_specs=[wide, pl.BlockSpec((1, 2, stacked), lambda h, sc: (h, 0, 0))],
            scratch_shapes=[
                pltpu.VMEM((2 * half, HD), BF16),
                pltpu.VMEM((2 * half, HD), BF16),
                pltpu.VMEM((stacked, HD), F32),
                pltpu.VMEM((stacked, HD), F32),
            ],
        ),
        out_shape=[
            jax.ShapeDtypeStruct((rows, width), BF16),
            jax.ShapeDtypeStruct((kv_local, 2, stacked), F32),
        ],
        compiler_params=pltpu.CompilerParams(vmem_limit_bytes=min(60 * MIB, 16 * MIB + 44 * HD * half)),
        cost_estimate=pl.CostEstimate(
            flops=4 * flops, bytes_accessed=16 * half * HD, transcendentals=rows * half
        ),
        name="attend",
    )(scalars, queries, *keys, *values)


def attend_back(scalars, queries, grad_context, context, lse, keys, values, span):
    rows, width = queries.shape
    kv_local = keys[0].shape[1] // HD
    across = width // kv_local
    half = keys[0].shape[0]
    wide = pl.BlockSpec((rows, across), lambda h, sc: (0, h))
    slots = pl.Buffered(2 if half <= 4096 else 1)
    tall = pl.BlockSpec((half, HD), lambda h, sc: (0, h))
    read = pl.BlockSpec((half, HD), lambda h, sc: (0, h), pipeline_mode=slots)
    stacked = across // HD * span
    flops = 10 * rows * half * width
    grads = jax.ShapeDtypeStruct(keys[0].shape, BF16)
    return pl.pallas_call(
        functools.partial(attend_back_kernel, span),
        grid_spec=pltpu.PrefetchScalarGridSpec(
            num_scalar_prefetch=1,
            grid=(kv_local,),
            in_specs=[wide, wide, wide, pl.BlockSpec((1, 2, stacked), lambda h, sc: (h, 0, 0))]
            + [read] * 4,
            out_specs=[wide] + [tall] * 4,
            scratch_shapes=[
                pltpu.VMEM((2 * half, HD), BF16),
                pltpu.VMEM((2 * half, HD), BF16),
                pltpu.VMEM((2 * half, HD), F32),
                pltpu.VMEM((2 * half, HD), F32),
                pltpu.VMEM((stacked, HD), F32),
            ],
        ),
        out_shape=[jax.ShapeDtypeStruct((rows, width), F32)] + [grads] * 4,
        compiler_params=pltpu.CompilerParams(vmem_limit_bytes=min(60 * MIB, 16 * MIB + 44 * HD * half)),
        cost_estimate=pl.CostEstimate(
            flops=4 * flops, bytes_accessed=32 * half * HD, transcendentals=rows * half
        ),
        name="attend_back",
    )(scalars, queries, grad_context, context, lse, *keys, *values)


def sum_of_parts(part):
    return lax.psum_scatter(part, "fsdp", scatter_dimension=0, tiled=True)


def all_parts(mine):
    return lax.all_gather(mine, "fsdp", axis=0, tiled=True)


def shards(
    tokens,
    span_order,
    input_gain,
    query_weight,
    key_weight,
    value_weight,
    query_gain,
    key_gain,
    output_weight,
    post_gain,
    gate_weight,
    up_weight,
    down_weight,
    cotangent,
):
    n = lax.axis_size("blk")
    me = lax.axis_index("blk")
    bits = high_bits(n)
    flipped = bits[::-1]
    masks = mask_order(n)
    rows, width = tokens.shape
    block = width // n
    split = width // 2
    span = rows // 2
    q_cols = query_weight.shape[1]
    kv_cols = key_weight.shape[1]
    heads = q_cols // HD
    kv_heads = kv_cols // HD
    units = gate_weight.shape[1]
    o_cols = output_weight.shape[0]

    mask_list = jnp.array(masks, jnp.int32)
    order = me ^ mask_list
    pair = [bits, flipped]

    spans = span_order.reshape(n, 2)
    chunk_ids = jnp.sum(
        jnp.where(order[:, None, None] == jnp.arange(n)[None, :, None], spans[None], 0),
        axis=1,
    ).reshape(-1)
    count = 2 * n
    positions = jnp.sum(
        jnp.where(
            chunk_ids[None, :] == jnp.arange(count)[:, None], jnp.arange(count)[None, :], 0
        ),
        axis=1,
    )
    scalars = jnp.concatenate([chunk_ids[:2], positions]).astype(jnp.int32)
    places = (chunk_ids[:2, None] * span + jnp.arange(span)[None, :]).reshape(-1)
    cosine, sine = rope_tables(places, HD)

    parts = lax.axis_size("fsdp")
    quarter = rows // parts
    my_part = lax.axis_index("fsdp") * quarter

    def mine(array):
        return lax.dynamic_slice_in_dim(array, my_part, quarter, 0)

    tokens, cotangent = enter(order, tokens, cotangent)
    my_tokens = mine(tokens)
    my_cotangent = mine(cotangent)
    down_t = down_weight.T
    cut = (units - o_cols) // 2
    side_a = jnp.concatenate([output_weight.T, down_t[:, :cut]], axis=1)
    side_b = down_t[:, cut:]
    gains = jnp.concatenate([input_gain, post_gain, query_gain, key_gain]).reshape(1, -1)
    (wq, wkv, gains), _ = gather_rows(
        [query_weight, jnp.concatenate([key_weight, value_weight], axis=1), gains],
        [bits, flipped, bits],
        beside=((tokens, cotangent), (side_a, side_b, cosine, sine, scalars)),
    )
    gains = jnp.concatenate(gains, axis=0).astype(F32)
    gain_input = gains[:, :block].reshape(1, width)
    gain_post = gains[:, block : 2 * block].reshape(1, width)
    chosen = (me ^ jnp.arange(n))[:, None] == mask_list[None, :]
    head_gains = jnp.sum(jnp.where(chosen[:, :, None], gains[None, :, 2 * block :], 0.0), axis=1)
    part = head_gains.shape[1] // 2
    gain_query = head_gains[:, :part].reshape(1, HD)
    gain_key = head_gains[:, part:].reshape(1, HD)

    normed_low, q_proj, k_proj, queries, keys, values = projections(
        tokens, gain_input, wq, wkv, cosine, sine, gain_query, gain_key
    )
    (all_keys, all_values), key_gots = gather_rows([keys, values], pair)
    context, lse = attend(scalars, queries, all_keys, all_values, span)

    (side_a, side_b), _ = gather_rows(
        [side_a, side_b], pair, before=(tuple(wq[:1]), tuple(key_gots[-1])), closing=[context]
    )
    (wg, wu), _ = gather_rows([gate_weight, up_weight], pair, before=((context,),))

    attn_part = to_width("attention_out", (context, 0, side_a, 0, o_cols))
    my_attn = sum_of_parts(attn_part)
    my_post = on_quarter(post_kernel, "post", (my_tokens, my_attn), (gain_post,), (BF16,))[0]
    post_low = all_parts(my_post)
    grad_act = from_width("grad_act", cotangent, (side_a, o_cols, cut), (side_b, 0, units - cut))
    act, grad_gate, grad_up = hidden_units(post_low, wg, wu, grad_act)
    post_part = to_width("grad_post", (grad_gate, 0, wg, 0, units), (grad_up, 0, wu, 0, units))
    my_grad_post = sum_of_parts(post_part)

    act_later = after(act, post_part)
    gate_later = after(grad_gate, post_part)
    up_later = after(grad_up, post_part)
    middle = units // 2
    down_a = weight_grad("down_a", n, bits[0], (cotangent, act_later, 0, middle))
    down_b = weight_grad("down_b", n, flipped[0], (cotangent, act_later, 1, middle))
    gate_terms = weight_grad("gate_grad", n, bits[0], (post_low, gate_later, 0, units))
    up_terms = weight_grad("up_grad", n, flipped[0], (post_low, up_later, 0, units))
    (gate_sum, up_sum), sends, gots = scatter_sums([gate_terms, up_terms], pair)
    (down_a, down_b), _, _ = scatter_sums([down_a, down_b], pair)
    down_sum = jnp.concatenate([down_a, down_b], axis=1).T

    mlp_part = to_width(
        "units_out",
        (act_later, 0, side_a, 1, cut),
        (act_later, 1, side_b, 0, cut),
        (act_later, 2, side_b, 1, cut),
    )
    my_grad_hidden, my_hidden_low = on_quarter(
        grad_hidden_kernel,
        "grad_hidden",
        (my_tokens, my_attn, my_cotangent, my_grad_post),
        (gain_post,),
        (F32, BF16),
    )
    hidden_low = all_parts(my_hidden_low)
    mlp_part, hidden_low = together((mlp_part, hidden_low), tuple(gots[0]))
    my_mlp = sum_of_parts(mlp_part)
    my_layer_out = on_quarter(
        layer_out_kernel, "layer_out_rows", (my_tokens, my_attn, my_mlp), (), (BF16,)
    )[0]

    grad_context = from_width("grad_context", hidden_low, (side_a, 0, o_cols))
    grad_context = after(grad_context, *gots[-1])
    dq, dk_own, dk_other, dv_own, dv_other = attend_back(
        scalars, queries, grad_context, context, lse, all_keys, all_values, span
    )
    dk_got, dv_got = together((exchange(dk_other, 1), exchange(dv_other, 1)))
    key_sums = split_sum(dk_own, dk_got, n, bits[0])
    value_sums = split_sum(dv_own, dv_got, n, flipped[0])
    (key_terms, value_terms), sends, _ = scatter_terms([key_sums, value_sums], pair)
    dq, hidden_later = together((dq, hidden_low), tuple(sends[0]))
    grad_q_low, q_gain_part = heads_back("queries_back", [dq], [], q_proj, cosine, sine, gain_query)
    grad_kv_low, k_gain_part = heads_back(
        "keys_back", key_terms, value_terms, k_proj, cosine, sine, gain_key
    )
    normed_part = to_width(
        "grad_normed", (grad_q_low, 0, wq, 0, q_cols), (grad_kv_low, 0, wkv, 0, 2 * kv_cols)
    )
    my_grad_normed = sum_of_parts(after(normed_part, my_mlp))
    my_tokens_grad = on_quarter(
        tokens_grad_kernel,
        "tokens_grad_rows",
        (my_tokens, my_grad_hidden, my_grad_normed),
        (gain_input,),
        (BF16,),
    )[0]

    o_half = o_cols // 2
    qo = weight_grad(
        "query_grad", n, bits[0], (normed_low, grad_q_low, 0, q_cols), (hidden_later, context, 0, o_half)
    )
    kvo = weight_grad(
        "key_value_grad",
        n,
        flipped[0],
        (normed_low, grad_kv_low, 0, 2 * kv_cols),
        (hidden_later, context, 1, o_half),
    )
    (qo, kvo), _, _ = scatter_sums([qo, kvo], pair)
    query_sum = qo[:, :q_cols]
    key_sum = kvo[:, :kv_cols]
    value_sum = kvo[:, kv_cols : 2 * kv_cols]
    out_sum = jnp.concatenate([qo[:, q_cols:], kvo[:, 2 * kv_cols :]], axis=1).T

    heads_sum = jnp.concatenate([jnp.sum(q_gain_part, axis=0), jnp.sum(k_gain_part, axis=0)])[None, :]
    for bit in [1] + bits:
        heads_sum = heads_sum + exchange(heads_sum, bit)
    head = HD // n
    heads_sum = lax.dynamic_slice_in_dim(heads_sum.reshape(2, n, head), me, 1, 1).reshape(-1)

    def along_rows(weight, grad):
        return jnp.sum(weight.astype(F32) * grad, axis=1)

    input_gain_part = (
        along_rows(query_weight, query_sum)
        + along_rows(key_weight, key_sum)
        + along_rows(value_weight, value_sum)
    ) / input_gain.astype(F32)
    post_gain_part = (
        along_rows(gate_weight, gate_sum) + along_rows(up_weight, up_sum)
    ) / post_gain.astype(F32)
    small = jnp.concatenate([input_gain_part, post_gain_part, heads_sum])[None, :]
    step = 1
    while step < parts:
        small = small + lax.ppermute(small, "fsdp", [(i, i ^ step) for i in range(parts)])
        step *= 2
    small = small[0]

    tokens_grad = leave("tokens_grad", order, all_parts(my_tokens_grad), F32)
    layer_out = leave("layer_out", order, all_parts(my_layer_out), BF16)
    return (
        layer_out,
        tokens_grad,
        small[:block],
        query_sum,
        key_sum,
        value_sum,
        small[2 * block : 2 * block + head],
        small[2 * block + head :],
        out_sum,
        small[block : 2 * block],
        gate_sum,
        up_sum,
        down_sum,
    )


def solution(mesh):
    placed = (
        P("blk", None),
        P(),
        P("blk"),
        P("blk", "fsdp"),
        P("blk", "fsdp"),
        P("blk", "fsdp"),
        P("blk"),
        P("blk"),
        P("fsdp", "blk"),
        P("blk"),
        P("blk", "fsdp"),
        P("blk", "fsdp"),
        P("fsdp", "blk"),
        P("blk", None),
    )
    return jax.shard_map(
        shards,
        mesh=mesh,
        in_specs=placed,
        out_specs=(
            P("blk", None),
            P("blk", None),
            P("blk"),
            P("blk", "fsdp"),
            P("blk", "fsdp"),
            P("blk", "fsdp"),
            P("blk"),
            P("blk"),
            P("fsdp", "blk"),
            P("blk"),
            P("blk", "fsdp"),
            P("blk", "fsdp"),
            P("fsdp", "blk"),
        ),
        check_vma=False,
    )
```

```python
import functools
import math

import jax
import jax.numpy as jnp
from jax import lax
from jax.experimental import pallas as pl
from jax.experimental.pallas import tpu as pltpu
from jax.sharding import PartitionSpec as P

HD = 128
EPS = 1e-06
THETA = 1000000.0
LOG2E = math.log2(math.e)
LN2 = math.log(2.0)
MIB = 1024 * 1024

F32 = jnp.float32
BF16 = jnp.bfloat16


def dims(lhs, rhs, left, right):
    return lax.dot_general(lhs, rhs, (((left,), (right,)), ((), ())), preferred_element_type=F32)


def mask_order(n):
    return [2 * i for i in range(n // 2)] + [2 * i + 1 for i in range(n // 2)]


def high_bits(n):
    return [1 << i for i in range(1, n.bit_length() - 1)]


def exchange(block, bit):
    n = lax.axis_size("blk")
    return lax.ppermute(block, "blk", [(i, i ^ bit) for i in range(n)])


def together(values, others=()):
    return lax.optimization_barrier((*values, *others))[: len(values)]


def after(value, *others):
    return lax.optimization_barrier((value,) + others)[0]


def gather_step(held, orders, step, before=(), beside=()):
    sent = []
    for have in held:
        one = [have[m] for m in sorted(have)]
        sent.append(one[0] if len(one) == 1 else jnp.concatenate(one, axis=0))
    sent = together(sent, before)
    raw = [exchange(x, order[step]) for x, order in zip(sent, orders)]
    got = together(raw, beside)
    for have, brought, order in zip(held, got, orders):
        rows = have[0].shape[0]
        for i, m in enumerate(sorted(have)):
            have[m | order[step]] = brought[i * rows : (i + 1) * rows]
    return tuple(raw)


def gather_end(held):
    own = [jnp.concatenate([have[m] for m in sorted(have)], axis=0) for have in held]
    return [(x, exchange(x, 1)) for x in own]


def gather_rest(held, orders, start, before=(), beside=()):
    raw = ()
    for step in range(start, len(orders[0])):
        raw = gather_step(
            held,
            orders,
            step,
            before if step == start else (),
            beside if step == len(orders[0]) - 1 else (),
        )
    return raw


def add_low(a, b):
    return (a.astype(F32) + b.astype(F32)).astype(BF16)


def scatter_terms(parts, orders, beside=()):
    held = []
    sent = [part[0] for part in parts]
    for (leave, stay), order in zip(parts, orders):
        masks = [m for m in range(0, 4 * stay.shape[0], 2) if not m & order[0]][: 2 ** (len(order) - 1)]
        rows = stay.shape[0] // len(masks)
        held.append({m: stay[i * rows : (i + 1) * rows] for i, m in enumerate(masks)})
    sends, gots = [], []
    for step in range(len(orders[0])):
        if step:
            sent = []
            for have, order in zip(held, orders):
                leave = [add_low(*have.pop(m)) for m in sorted(have) if m & order[step]]
                sent.append(leave[0] if len(leave) == 1 else jnp.concatenate(leave, axis=0))
                for m in have:
                    have[m] = add_low(*have[m])
        sent = together(sent)
        sends.append(sent)
        raw = [exchange(x, order[step]) for x, order in zip(sent, orders)]
        gots.append(tuple(raw))
        got = together(raw, beside[step] if step < len(beside) else ())
        for have, back in zip(held, got):
            rows = back.shape[0] // len(have)
            for i, m in enumerate(sorted(have)):
                have[m] = (have[m], back[i * rows : (i + 1) * rows])
    return [have[0] for have in held], sends, gots


def scatter_sums(parts, orders, beside=()):
    terms, sends, gots = scatter_terms(parts, orders, beside)
    return [a.astype(F32) + b.astype(F32) for a, b in terms], sends, gots


def leaving_first(n, bit):
    masks = [2 * i for i in range(n // 2)]
    return [i for i, m in enumerate(masks) if m & bit] + [i for i, m in enumerate(masks) if not m & bit]


def split_sum(own, got, n, bit):
    rows = own.shape[0] // (n // 2)
    at = leaving_first(n, bit)

    def part(array, which):
        return jnp.concatenate([array[i * rows : (i + 1) * rows] for i in which], axis=0)

    half = len(at) // 2
    return tuple(add_low(part(own, w), part(got, w)) for w in (at[:half], at[half:]))


def norm_scale(values):
    return lax.rsqrt(jnp.mean(values * values, axis=-1, keepdims=True) + EPS)


def norm_back(values, scale, weighted):
    inner = jnp.mean(weighted * values, axis=-1, keepdims=True)
    return scale * (weighted - values * scale * scale * inner)


def rope_tables(places, width):
    half = width // 2
    freqs = THETA ** (-jnp.arange(half, dtype=F32) * 2.0 / width)
    angles = places.astype(F32)[:, None] * freqs[None, :]
    sine = jnp.sin(angles)
    cosine = jnp.cos(angles)
    return (jnp.concatenate([cosine, cosine], axis=1), jnp.concatenate([-sine, sine], axis=1))


def turned(values):
    return pltpu.roll(values, HD // 2, 1)


def call(kernel, name, grid, in_specs, out_specs, out_shape, args, flops, scratch=(), scalars=None, near=False):
    if scalars is None:
        spec = {"grid": grid, "in_specs": in_specs, "out_specs": out_specs, "scratch_shapes": scratch}
    else:
        spec = {
            "grid_spec": pltpu.PrefetchScalarGridSpec(
                num_scalar_prefetch=1,
                grid=grid,
                in_specs=in_specs,
                out_specs=out_specs,
                scratch_shapes=scratch,
            )
        }
    if not near:
        args = in_far(*args)
        out_shape = [pltpu.HBM(o.shape, o.dtype) for o in out_shape]
    if scalars is not None:
        args = (scalars, *args)
    return pl.pallas_call(
        kernel,
        out_shape=out_shape,
        compiler_params=pltpu.CompilerParams(vmem_limit_bytes=28 * MIB),
        cost_estimate=pl.CostEstimate(flops=0, bytes_accessed=0, transcendentals=0),
        name=name,
        **spec,
    )(*args)


def in_far(*arrays):
    big = 1 << 17
    return [
        pltpu.with_memory_space_constraint(a, pltpu.HBM) if a.size * a.dtype.itemsize >= big else a
        for a in arrays
    ]


def shape(dims_, dtype):
    return jax.ShapeDtypeStruct(dims_, dtype)


def picked(array, order):
    n = order.shape[0]
    block = array.shape[1] // n
    return jnp.concatenate(
        [lax.dynamic_slice_in_dim(array, order[i] * block, block, 1) for i in range(n)], axis=1
    )


def enter_kernel(sc, a_ref, b_ref, a_out, b_out):
    a_out[...] = a_ref[...]
    b_out[...] = b_ref[...]


def enter(order, first, second):
    rows, width = first.shape
    n = order.shape[0]
    block = width // n
    if block % 128:
        return picked(first, order), picked(second, order)
    source = pl.BlockSpec((rows, block), lambda p, sc: (0, sc[p]))
    target = pl.BlockSpec((rows, block), lambda p, sc: (0, p))
    return call(
        enter_kernel,
        "enter",
        (n,),
        [source, source],
        [target, target],
        [shape(first.shape, first.dtype), shape(second.shape, second.dtype)],
        (first, second),
        0,
        scalars=order,
        near=True,
    )


def leave_blocks(sc, out_ref, result):
    width = result.shape[1]
    n = len(sc)
    block = width // n
    if block % 128:
        out_ref[...] = result.astype(out_ref.dtype)
        return
    for p in range(n):
        at = pl.ds(pl.multiple_of(sc[p] * block, 128), block)
        out_ref[:, at] = result[:, p * block : (p + 1) * block].astype(out_ref.dtype)


def leave_kernel(n, sc, value_ref, out_ref):
    leave_blocks([sc[p] for p in range(n)], out_ref, value_ref[...])


def leave(name, order, value, places, dtype):
    rows, width = value.shape
    n = order.shape[0]
    parts = places.shape[0]
    height = rows // parts
    result = call(
        functools.partial(leave_kernel, n),
        name,
        (parts,),
        [pl.BlockSpec((height, width), lambda i, sc: (sc[n + i], 0))],
        [pl.BlockSpec((height, width), lambda i, sc: (i, 0))],
        [shape((rows, width), dtype)],
        (value,),
        0,
        scalars=jnp.concatenate([order, places.astype(jnp.int32)]),
    )[0]
    if width // n % 128:
        index = jnp.arange(n)
        back = jnp.sum(jnp.where(order[None, :] == index[:, None], index[None, :], 0), axis=1)
        return picked(result, back)
    return result


def post_kernel(tokens_ref, attn_ref, gain_ref, out_ref):
    hidden = tokens_ref[...].astype(F32) + attn_ref[...].astype(F32)
    out_ref[...] = (hidden * norm_scale(hidden) * gain_ref[...]).astype(BF16)


def layer_out_kernel(tokens_ref, attn_ref, mlp_ref, out_ref):
    hidden = tokens_ref[...].astype(F32) + attn_ref[...].astype(F32)
    out_ref[...] = (hidden + mlp_ref[...].astype(F32)).astype(BF16)


def grad_hidden_kernel(tokens_ref, attn_ref, cotangent_ref, grad_ref, gain_ref, out_ref, low_ref):
    hidden = tokens_ref[...].astype(F32) + attn_ref[...].astype(F32)
    weighted = grad_ref[...].astype(F32) * gain_ref[...]
    grad = cotangent_ref[...].astype(F32) + norm_back(hidden, norm_scale(hidden), weighted)
    out_ref[...] = grad
    low_ref[...] = grad.astype(BF16)


def tokens_grad_kernel(tokens_ref, hidden_ref, grad_ref, gain_ref, out_ref):
    inputs = tokens_ref[...].astype(F32)
    weighted = grad_ref[...].astype(F32) * gain_ref[...]
    back = norm_back(inputs, norm_scale(inputs), weighted)
    out_ref[...] = (hidden_ref[...] + back).astype(BF16)


def on_quarter(kernel, name, arrays, gains, dtypes):
    rows, width = arrays[0].shape
    spec = pl.BlockSpec((rows, width), lambda i: (0, 0))
    full = [pl.BlockSpec(g.shape, lambda i: (0, 0)) for g in gains]
    return call(
        kernel,
        name,
        (1,),
        [spec] * len(arrays) + full,
        [spec] * len(dtypes),
        [shape((rows, width), dtype) for dtype in dtypes],
        tuple(arrays) + tuple(gains),
        0,
    )


def project_kernel(
    q_steps, split, tokens_ref, gain_ref, wq0, wq1, wkv0, wkv1, cos_ref, sin_ref, gq_ref, gk_ref,
    normed_ref, q_proj, k_proj, queries, keys, values,
):
    j = pl.program_id(0)

    @pl.when(j == 0)
    def _():
        inputs = tokens_ref[...].astype(F32)
        normed_ref[...] = (inputs * norm_scale(inputs) * gain_ref[...]).astype(BF16)

    def product(w0, w1):
        return dims(normed_ref[:, :split], w0[...], 1, 0) + dims(normed_ref[:, split:], w1[...], 1, 0)

    def heads(proj, proj_ref, out_ref, gain, factor):
        proj_ref[...] = proj
        for h in range(proj.shape[1] // HD):
            one = slice(h * HD, (h + 1) * HD)
            u = proj[:, one]
            u = u * norm_scale(u) * gain
            u = u * cos_ref[...] + turned(u) * sin_ref[...]
            out_ref[:, one] = (u * factor if factor else u).astype(BF16)

    @pl.when(j < q_steps)
    def _():
        heads(product(wq0, wq1), q_proj, queries, gq_ref[...], HD**-0.5 * LOG2E)

    @pl.when(j == q_steps)
    def _():
        heads(product(wkv0, wkv1), k_proj, keys, gk_ref[...], None)

    @pl.when(j == q_steps + 1)
    def _():
        values[...] = product(wkv0, wkv1).astype(BF16)


def projections(tokens, gain, wq, wkv, cosine, sine, gain_query, gain_key):
    rows, width = tokens.shape
    q_cols = wq[0].shape[1]
    kv_cols = wkv[0].shape[1] // 2
    steps = q_cols // kv_cols
    split = width // 2

    def whole(array):
        return pl.BlockSpec(array.shape, lambda j: (0, 0))

    q_tile = pl.BlockSpec((split, kv_cols), lambda j: (0, jnp.minimum(j, steps - 1)))
    kv_tile = pl.BlockSpec((split, kv_cols), lambda j: (0, jnp.maximum(j - steps, 0)))
    q_out = pl.BlockSpec((rows, kv_cols), lambda j: (0, jnp.minimum(j, steps - 1)))
    kv_out = pl.BlockSpec((rows, kv_cols), lambda j: (0, 0))
    small = [cosine, sine, gain_query, gain_key]
    return call(
        functools.partial(project_kernel, steps, split),
        "projections",
        (steps + 2,),
        [whole(tokens), whole(gain), q_tile, q_tile, kv_tile, kv_tile] + [whole(a) for a in small],
        [whole(tokens), q_out, kv_out, q_out, kv_out, kv_out],
        [
            shape((rows, width), BF16),
            shape((rows, q_cols), F32),
            shape((rows, kv_cols), F32),
            shape((rows, q_cols), BF16),
            shape((rows, kv_cols), BF16),
            shape((rows, kv_cols), BF16),
        ],
        (tokens, gain, *wq, *wkv, *small),
        2 * rows * width * (q_cols + 2 * kv_cols),
    )


def to_width_kernel(count, half, *refs):
    i = pl.program_id(0)
    lefts = refs[:count]
    rights = refs[count : 3 * count]
    out_ref = refs[-1]
    for parity, here in ((0, i < half), (1, i >= half)):

        @pl.when(here)
        def _(parity=parity):
            total = None
            for left, pair in zip(lefts, zip(rights[::2], rights[1::2])):
                term = dims(left[...], pair[parity][...], 1, 1)
                total = term if total is None else total + term
            out_ref[...] = total.astype(out_ref.dtype)


def to_width(name, *terms, tile=256):
    rows = terms[0][0].shape[0]
    split = terms[0][2][0].shape[0]
    half = split // tile
    in_specs = []
    for left, at, pair, where, columns in terms:
        in_specs.append(pl.BlockSpec((rows, columns), lambda i, at=at: (0, at)))
    args = [t[0] for t in terms]
    flops = 0
    for left, at, pair, where, columns in terms:
        in_specs.append(
            pl.BlockSpec((tile, columns), lambda i, w=where: (jnp.minimum(i, half - 1), w))
        )
        in_specs.append(
            pl.BlockSpec((tile, columns), lambda i, w=where: (jnp.maximum(i - half, 0), w))
        )
        args += list(pair)
        flops += 4 * rows * split * columns
    return call(
        functools.partial(to_width_kernel, len(terms), half),
        name,
        (2 * half,),
        in_specs,
        [pl.BlockSpec((rows, tile), lambda i: (0, i))],
        [shape((rows, 2 * split), BF16)],
        tuple(args),
        flops,
    )[0]


def from_width_kernel(split, bounds, left_ref, *refs):
    out_ref = refs[-1]
    j = pl.program_id(0)
    for k in range(len(bounds) - 1):

        @pl.when((j >= bounds[k]) & (j < bounds[k + 1]))
        def _(w0=refs[2 * k], w1=refs[2 * k + 1]):
            product = dims(left_ref[:, :split], w0[...], 1, 0) + dims(left_ref[:, split:], w1[...], 1, 0)
            out_ref[...] = product.astype(out_ref.dtype)


def from_width(name, left, *sides, tile=256):
    rows, width = left.shape
    split = width // 2
    bounds = [0]
    specs, args = [], [left]
    for pair, start, columns in sides:
        low, high = bounds[-1], bounds[-1] + columns // tile
        bounds.append(high)
        specs += [
            pl.BlockSpec(
                (split, tile),
                lambda j, low=low, high=high, first=start // tile: (0, first + jnp.clip(j, low, high - 1) - low),
            )
        ] * 2
        args += list(pair)
    return call(
        functools.partial(from_width_kernel, split, tuple(bounds)),
        name,
        (bounds[-1],),
        [pl.BlockSpec((rows, width), lambda j: (0, 0))] + specs,
        [pl.BlockSpec((rows, tile), lambda j: (0, j))],
        [shape((rows, bounds[-1] * tile), BF16)],
        tuple(args),
        2 * rows * width * bounds[-1] * tile,
    )[0]


def units_kernel(split, post_ref, wg0, wg1, wu0, wu1, grad_ref, act_ref, gate_out, up_out):
    def product(w0, w1):
        return dims(post_ref[:, :split], w0[...], 1, 0) + dims(post_ref[:, split:], w1[...], 1, 0)

    gate = product(wg0, wg1)
    up = product(wu0, wu1)
    grad_act = grad_ref[...].astype(F32)
    sigma = jax.nn.sigmoid(gate)
    silu = gate * sigma
    act_ref[...] = (silu * up).astype(BF16)
    up_out[...] = (grad_act * silu).astype(BF16)
    gate_out[...] = (grad_act * up * sigma * (1.0 + gate * (1.0 - sigma))).astype(BF16)


def hidden_units(post, wg, wu, grad_act, tile=256):
    rows, width = post.shape
    units = grad_act.shape[1]
    split = width // 2
    side = pl.BlockSpec((split, tile), lambda j: (0, j))
    part = pl.BlockSpec((rows, tile), lambda j: (0, j))
    unit = shape((rows, units), BF16)
    return call(
        functools.partial(units_kernel, split),
        "hidden_units",
        (units // tile,),
        [pl.BlockSpec(post.shape, lambda j: (0, 0)), side, side, side, side, part],
        [part, part, part],
        [unit, unit, unit],
        (post, *wg, *wu, grad_act),
        4 * rows * width * units,
    )


def away_kernel(count, *refs):
    out_ref = refs[-1]
    start = 0
    for left, right in zip(refs[:count], refs[count : 2 * count]):
        columns = right.shape[1]
        out_ref[:, start : start + columns] = dims(left[...].T, right[...], 1, 0).astype(BF16)
        start += columns


def home_kernel(count, leaving, sc, *refs):
    got_ref, leave_ref, stay_ref = refs[2 * count :]
    step = pl.program_id(0)
    for out_ref, here in ((leave_ref, step < leaving), (stay_ref, step >= leaving)):

        @pl.when(here)
        def _(out_ref=out_ref):
            start = 0
            for left, right in zip(refs[:count], refs[count : 2 * count]):
                columns = right.shape[1]
                at = slice(start, start + columns)
                term = dims(left[...].T, right[...], 1, 0) + got_ref[:, at].astype(F32)
                out_ref[:, at] = term.astype(BF16)
                start += columns


def weight_grad(name, n, bit, *pairs):
    rows, width = pairs[0][0].shape
    split = width // 2
    total = sum(p[3] for p in pairs)
    flops = rows * width * total
    right_specs = [(p[2], p[3]) for p in pairs]
    lefts = [p[0] for p in pairs]
    rights = [p[1] for p in pairs]
    tile = 256
    tiles = split // tile
    away = call(
        functools.partial(away_kernel, len(pairs)),
        name + "_away",
        (tiles,),
        [pl.BlockSpec((rows, tile), lambda i: (0, tiles + i))] * len(pairs)
        + [pl.BlockSpec((rows, c), lambda i, w=w: (0, w)) for w, c in right_specs],
        [pl.BlockSpec((tile, total), lambda i: (i, 0))],
        [shape((split, total), BF16)],
        (*lefts, *rights),
        flops,
    )[0]
    got = exchange(away, 1)
    block = width // n
    order = leaving_first(n, bit)
    leaving = len(order) // 2
    if block % 128:
        home = call(
            functools.partial(away_kernel, len(pairs)),
            name,
            (tiles,),
            [pl.BlockSpec((rows, tile), lambda i: (0, i))] * len(pairs)
            + [pl.BlockSpec((rows, c), lambda i, w=w: (0, w)) for w, c in right_specs],
            [pl.BlockSpec((tile, total), lambda i: (i, 0))],
            [shape((split, total), BF16)],
            (*lefts, *rights),
            flops,
        )[0]
        return split_sum(home, got, n, bit)
    return call(
        functools.partial(home_kernel, len(pairs), leaving),
        name,
        (len(order),),
        [pl.BlockSpec((rows, block), lambda i, sc: (0, sc[i]))] * len(pairs)
        + [pl.BlockSpec((rows, c), lambda i, sc, w=w: (0, w)) for w, c in right_specs]
        + [pl.BlockSpec((block, total), lambda i, sc: (sc[i], 0))],
        [
            pl.BlockSpec((block, total), lambda i, sc: (jnp.minimum(i, leaving - 1), 0)),
            pl.BlockSpec((block, total), lambda i, sc: (jnp.maximum(i - leaving, 0), 0)),
        ],
        [shape((split // 2, total), BF16)] * 2,
        (*lefts, *rights, got),
        flops,
        scalars=jnp.array(order, jnp.int32),
    )


def heads_back_kernel(terms, passed, *refs):
    grads, refs = refs[:terms], refs[terms:]
    others, refs = refs[:passed], refs[passed:]
    proj_ref, cos_ref, sin_ref, gain_ref, out_ref, sum_ref = refs
    columns = proj_ref.shape[1]
    total = None
    for h in range(columns // HD):
        one = slice(h * HD, (h + 1) * HD)
        grad = grads[0][:, one].astype(F32)
        for more in grads[1:]:
            grad = grad + more[:, one].astype(F32)
        grad = grad * cos_ref[...] + turned(grad * sin_ref[...])
        u = proj_ref[:, one]
        scale = norm_scale(u)
        term = jnp.sum((grad * u * scale).reshape(-1, 8, HD), axis=0)
        total = term if total is None else total + term
        out_ref[:, one] = norm_back(u, scale, grad * gain_ref[...]).astype(BF16)
    sum_ref[...] = total
    if passed:
        other = others[0][...].astype(F32)
        for more in others[1:]:
            other = other + more[...].astype(F32)
        out_ref[:, columns:] = other.astype(BF16)


def heads_back(name, grads, others, proj, cosine, sine, gain):
    rows, columns = proj.shape
    args = (*grads, *others, proj, cosine, sine, gain)
    total = columns + (others[0].shape[1] if others else 0)
    return call(
        functools.partial(heads_back_kernel, len(grads), len(others)),
        name,
        (1,),
        [pl.BlockSpec(a.shape, lambda i: (0, 0)) for a in args],
        [pl.BlockSpec((rows, total), lambda i: (0, 0)), pl.BlockSpec((8, HD), lambda i: (0, 0))],
        [shape((rows, total), BF16), shape((8, HD), F32)],
        args,
        20 * rows * columns,
    )


def attend_kernel(span, sc, q_ref, k0, k1, v0, v1, ctx_ref, lse_ref, k_s, v_s, acc_s, sum_s):
    half = k0.shape[0]
    k_s[:half] = k0[...]
    k_s[half:] = k1[...]
    v_s[:half] = v0[...]
    v_s[half:] = v1[...]
    group = q_ref.shape[1] // HD
    rows = span * group
    for s in range(2):
        top = slice(s * span, (s + 1) * span)
        q = jnp.concatenate([q_ref[top, g * HD : (g + 1) * HD] for g in range(group)], axis=0)
        acc_s[...] = jnp.zeros_like(acc_s)
        sum_s[...] = jnp.zeros_like(sum_s)

        def step(p, masked):
            at = pl.ds(pl.multiple_of(sc[2 + p] * span, span), span)
            e = jnp.exp2(dims(q, k_s[at, :], 1, 1))
            if masked:
                row = lax.broadcasted_iota(jnp.int32, (rows, span), 0) % span
                col = lax.broadcasted_iota(jnp.int32, (rows, span), 1)
                e = jnp.where(row >= col, e, 0.0)
            part = e[:, :HD]
            for c in range(HD, span, HD):
                part = part + e[:, c : c + HD]
            sum_s[...] += part
            acc_s[...] += dims(e.astype(BF16), v_s[at, :], 1, 0)

        pl.loop(0, sc[s])(lambda p: step(p, False))
        step(sc[s], True)
        total = jnp.sum(sum_s[...], axis=1, keepdims=True)
        ctx = (acc_s[...] / total).astype(BF16)
        for g in range(group):
            ctx_ref[top, g * HD : (g + 1) * HD] = ctx[g * span : (g + 1) * span]
        wide = jnp.broadcast_to(jnp.log2(total), (rows, HD))
        lse_ref[0, s : s + 1, :] = wide.T[0:1]


def attend_back_kernel(
    span, sc, q_ref, do_ref, ctx_ref, lse_ref, k0, k1, v0, v1, dq_ref, dk0, dk1, dv0, dv1, k_s, v_s, dk_s, dv_s, dq_s
):
    half = k0.shape[0]
    k_s[:half] = k0[...]
    k_s[half:] = k1[...]
    v_s[:half] = v0[...]
    v_s[half:] = v1[...]
    dk_s[...] = jnp.zeros_like(dk_s)
    dv_s[...] = jnp.zeros_like(dv_s)
    group = q_ref.shape[1] // HD
    rows = span * group
    for s in range(2):
        top = slice(s * span, (s + 1) * span)

        def stacked(ref):
            return jnp.concatenate([ref[top, g * HD : (g + 1) * HD] for g in range(group)], axis=0)

        q = stacked(q_ref)
        do = stacked(do_ref)
        q_t = q.T
        do_t = do.T
        product = do.astype(F32) * stacked(ctx_ref).astype(F32)
        delta = jnp.sum(product.T, axis=0, keepdims=True)
        lse = lse_ref[0, s : s + 1, :]
        dq_s[...] = jnp.zeros_like(dq_s)

        def step(p, masked):
            at = pl.ds(pl.multiple_of(sc[2 + p] * span, span), span)
            k = k_s[at, :]
            probs = jnp.exp2(dims(k, q_t, 1, 0) - lse)
            if masked:
                key = lax.broadcasted_iota(jnp.int32, (span, rows), 0)
                query = lax.broadcasted_iota(jnp.int32, (span, rows), 1) % span
                probs = jnp.where(query >= key, probs, 0.0)
            dv_s[at, :] += dims(probs.astype(BF16), do, 1, 0)
            grad = (probs * (dims(v_s[at, :], do_t, 1, 0) - delta)).astype(BF16)
            dk_s[at, :] += dims(grad, q, 1, 0)
            dq_s[...] += dims(grad, k, 0, 0)

        pl.loop(0, sc[s])(lambda p: step(p, False))
        step(sc[s], True)
        dq = dq_s[...] * (HD**-0.5)
        for g in range(group):
            dq_ref[top, g * HD : (g + 1) * HD] = dq[g * span : (g + 1) * span]
    dk0[...] = (dk_s[:half] * LN2).astype(BF16)
    dk1[...] = (dk_s[half:] * LN2).astype(BF16)
    dv0[...] = dv_s[:half].astype(BF16)
    dv1[...] = dv_s[half:].astype(BF16)


def attend(scalars, queries, keys, values, span):
    rows, width = queries.shape
    kv_local = keys[0].shape[1] // HD
    across = width // kv_local
    half = keys[0].shape[0]
    wide = pl.BlockSpec((rows, across), lambda h, sc: (0, h))
    slots = pl.Buffered(2 if half <= 4096 else 1)
    tall = pl.BlockSpec((half, HD), lambda h, sc: (0, h))
    read = pl.BlockSpec((half, HD), lambda h, sc: (0, h), pipeline_mode=slots)
    stacked = across // HD * span
    flops = 4 * rows * half * width
    return pl.pallas_call(
        functools.partial(attend_kernel, span),
        grid_spec=pltpu.PrefetchScalarGridSpec(
            num_scalar_prefetch=1,
            grid=(kv_local,),
            in_specs=[wide, read, read, read, read],
            out_specs=[wide, pl.BlockSpec((1, 2, stacked), lambda h, sc: (h, 0, 0))],
            scratch_shapes=[
                pltpu.VMEM((2 * half, HD), BF16),
                pltpu.VMEM((2 * half, HD), BF16),
                pltpu.VMEM((stacked, HD), F32),
                pltpu.VMEM((stacked, HD), F32),
            ],
        ),
        out_shape=[
            jax.ShapeDtypeStruct((rows, width), BF16),
            jax.ShapeDtypeStruct((kv_local, 2, stacked), F32),
        ],
        compiler_params=pltpu.CompilerParams(vmem_limit_bytes=min(60 * MIB, 16 * MIB + 44 * HD * half)),
        cost_estimate=pl.CostEstimate(
            flops=4 * flops, bytes_accessed=16 * half * HD, transcendentals=rows * half
        ),
        name="attend",
    )(scalars, queries, *in_far(*keys, *values))


def attend_back(scalars, queries, grad_context, context, lse, keys, values, span):
    rows, width = queries.shape
    kv_local = keys[0].shape[1] // HD
    across = width // kv_local
    half = keys[0].shape[0]
    wide = pl.BlockSpec((rows, across), lambda h, sc: (0, h))
    slots = pl.Buffered(2 if half <= 4096 else 1)
    tall = pl.BlockSpec((half, HD), lambda h, sc: (0, h))
    read = pl.BlockSpec((half, HD), lambda h, sc: (0, h), pipeline_mode=slots)
    stacked = across // HD * span
    flops = 10 * rows * half * width
    grads = pltpu.HBM(keys[0].shape, BF16)
    return pl.pallas_call(
        functools.partial(attend_back_kernel, span),
        grid_spec=pltpu.PrefetchScalarGridSpec(
            num_scalar_prefetch=1,
            grid=(kv_local,),
            in_specs=[wide, wide, wide, pl.BlockSpec((1, 2, stacked), lambda h, sc: (h, 0, 0))]
            + [read] * 4,
            out_specs=[wide] + [tall] * 4,
            scratch_shapes=[
                pltpu.VMEM((2 * half, HD), BF16),
                pltpu.VMEM((2 * half, HD), BF16),
                pltpu.VMEM((2 * half, HD), F32),
                pltpu.VMEM((2 * half, HD), F32),
                pltpu.VMEM((stacked, HD), F32),
            ],
        ),
        out_shape=[pltpu.HBM((rows, width), F32)] + [grads] * 4,
        compiler_params=pltpu.CompilerParams(vmem_limit_bytes=min(60 * MIB, 16 * MIB + 44 * HD * half)),
        cost_estimate=pl.CostEstimate(
            flops=4 * flops, bytes_accessed=32 * half * HD, transcendentals=rows * half
        ),
        name="attend_back",
    )(scalars, *in_far(queries, grad_context, context, lse, *keys, *values))


def sum_of_parts(part):
    return lax.psum_scatter(part, "fsdp", scatter_dimension=0, tiled=True)


def all_parts(mine):
    return lax.all_gather(mine, "fsdp", axis=0, tiled=True)


def shards(
    tokens,
    span_order,
    input_gain,
    query_weight,
    key_weight,
    value_weight,
    query_gain,
    key_gain,
    output_weight,
    post_gain,
    gate_weight,
    up_weight,
    down_weight,
    cotangent,
):
    n = lax.axis_size("blk")
    me = lax.axis_index("blk")
    bits = high_bits(n)
    flipped = bits[::-1]
    masks = mask_order(n)
    rows, width = tokens.shape
    block = width // n
    split = width // 2
    span = rows // 2
    q_cols = query_weight.shape[1]
    kv_cols = key_weight.shape[1]
    heads = q_cols // HD
    kv_heads = kv_cols // HD
    units = gate_weight.shape[1]
    o_cols = output_weight.shape[0]

    mask_list = jnp.array(masks, jnp.int32)
    order = me ^ mask_list
    pair = [bits, flipped]

    spans = span_order.reshape(n, 2)
    chunk_ids = jnp.sum(
        jnp.where(order[:, None, None] == jnp.arange(n)[None, :, None], spans[None], 0),
        axis=1,
    ).reshape(-1)
    count = 2 * n
    positions = jnp.sum(
        jnp.where(
            chunk_ids[None, :] == jnp.arange(count)[:, None], jnp.arange(count)[None, :], 0
        ),
        axis=1,
    )
    scalars = jnp.concatenate([chunk_ids[:2], positions]).astype(jnp.int32)
    places = (chunk_ids[:2, None] * span + jnp.arange(span)[None, :]).reshape(-1)
    cosine, sine = rope_tables(places, HD)

    parts = lax.axis_size("fsdp")
    quarter = rows // parts
    my_part = lax.axis_index("fsdp") * quarter

    def mine(array):
        return lax.dynamic_slice_in_dim(array, my_part, quarter, 0)

    gains = jnp.concatenate([input_gain, post_gain, query_gain, key_gain]).reshape(1, -1)
    first = [{0: query_weight}, {0: jnp.concatenate([key_weight, value_weight], axis=1)}, {0: gains}]
    triple = [bits, flipped, bits]
    out_t = output_weight.T
    o_half = o_cols // 2
    gather_step(first, triple, 0, beside=(out_t,))
    tokens, cotangent = enter(order, tokens, cotangent)
    my_tokens = mine(tokens)
    my_cotangent = mine(cotangent)
    late = gather_rest(first, triple, 1, beside=(tokens, cotangent, cosine, sine, scalars))
    wq, wkv, gains = gather_end(first)
    gains = jnp.concatenate(gains, axis=0).astype(F32)
    gain_input = gains[:, :block].reshape(1, width)
    gain_post = gains[:, block : 2 * block].reshape(1, width)
    chosen = (me ^ jnp.arange(n))[:, None] == mask_list[None, :]
    head_gains = jnp.sum(jnp.where(chosen[:, :, None], gains[None, :, 2 * block :], 0.0), axis=1)
    part = head_gains.shape[1] // 2
    gain_query = head_gains[:, :part].reshape(1, HD)
    gain_key = head_gains[:, part:].reshape(1, HD)

    normed_low, q_proj, k_proj, queries, keys, values = projections(
        tokens, gain_input, wq, wkv, cosine, sine, gain_query, gain_key
    )
    outs = [{0: out_t[:, :o_half]}, {0: out_t[:, o_half:]}]
    out_got = gather_step(outs, pair, 0, before=late)
    rows_held = [{0: keys}, {0: values}]
    gather_step(rows_held, pair, 0, before=out_got)
    gather_rest(outs, pair, 1)
    key_got = gather_rest(rows_held, pair, 1)
    all_keys, all_values = gather_end(rows_held)
    wo_a, wo_b = gather_end(outs)
    wide = [{0: gate_weight}, {0: up_weight}]
    context, lse = attend(scalars, queries, all_keys, all_values, span)
    wide_got = gather_step(wide, pair, 0, before=key_got, beside=(context,))
    down_t = down_weight.T
    middle = units // 2
    downs = [{0: down_t[:, :middle]}, {0: down_t[:, middle:]}]
    attn_part = to_width(
        "attention_out",
        (after(context, *wide_got), 0, wo_a, 0, o_half),
        (after(context, *wide_got), 1, wo_b, 0, o_half),
        tile=512,
    )
    my_attn = sum_of_parts(attn_part)
    my_post = on_quarter(post_kernel, "post", (my_tokens, my_attn), (gain_post,), (BF16,))[0]
    post_low = all_parts(my_post)
    wide_got = gather_rest(wide, pair, 1)
    wg, wu = gather_end(wide)
    gather_step(downs, pair, 0, before=(my_post, *wide_got))
    gather_rest(downs, pair, 1)
    side_a, side_b = gather_end(downs)
    grad_act = from_width(
        "grad_act", cotangent, (side_a, 0, middle), (side_b, 0, middle)
    )
    act, grad_gate, grad_up = hidden_units(post_low, wg, wu, grad_act)
    post_part = to_width("grad_post", (grad_gate, 0, wg, 0, units), (grad_up, 0, wu, 0, units))
    my_grad_post = sum_of_parts(post_part)

    gate_later = after(grad_gate, post_part)
    up_later = after(grad_up, post_part)
    gate_terms = weight_grad("gate_grad", n, bits[0], (post_low, gate_later, 0, units))
    up_terms = weight_grad("up_grad", n, flipped[0], (post_low, up_later, 0, units))
    act_later = after(act, post_part)
    down_terms = [
        weight_grad("down_a", n, bits[0], (cotangent, act_later, 0, middle)),
        weight_grad("down_b", n, flipped[0], (cotangent, act_later, 1, middle)),
    ]
    mlp_part = to_width(
        "units_out",
        (act_later, 0, side_a, 0, middle),
        (act_later, 1, side_b, 0, middle),
    )
    my_grad_post = after(my_grad_post, gate_terms[0], up_terms[0])
    my_grad_hidden, my_hidden_low = on_quarter(
        grad_hidden_kernel,
        "grad_hidden",
        (my_tokens, my_attn, my_cotangent, my_grad_post),
        (gain_post,),
        (F32, BF16),
    )
    hidden_low = all_parts(my_hidden_low)
    mlp_part, hidden_low = together((mlp_part, hidden_low), (down_terms[0][0], down_terms[1][0]))
    my_mlp = sum_of_parts(mlp_part)

    grad_context = from_width("grad_context", hidden_low, (wo_a, 0, o_half), (wo_b, 0, o_half))
    dq, dk_own, dk_other, dv_own, dv_other = attend_back(
        scalars, queries, grad_context, context, lse, all_keys, all_values, span
    )
    (gate_sum, up_sum), _, unit_gots = scatter_sums(
        [gate_terms, up_terms], pair, beside=((), (dk_own,))
    )
    (down_a, down_b), _, down_gots = scatter_sums(down_terms, pair, beside=((dk_own,),))
    down_sum = jnp.concatenate([down_a, down_b], axis=1).T
    my_layer_out = on_quarter(
        layer_out_kernel, "layer_out_rows", (my_tokens, my_attn, after(my_mlp, dk_own, *down_gots[0], *unit_gots[-1])), (), (BF16,)
    )[0]
    all_layer_out = all_parts(my_layer_out)
    dk_got, dv_got = together((exchange(dk_other, 1), exchange(dv_other, 1)))
    key_sums = split_sum(dk_own, dk_got, n, bits[0])
    value_sums = split_sum(dv_own, dv_got, n, flipped[0])
    (key_terms, value_terms), sends, _ = scatter_terms([key_sums, value_sums], pair)
    dq, hidden_later = together((dq, hidden_low), tuple(sends[0]))
    grad_q_low, q_gain_part = heads_back("queries_back", [dq], [], q_proj, cosine, sine, gain_query)
    grad_kv_low, k_gain_part = heads_back(
        "keys_back", key_terms, value_terms, k_proj, cosine, sine, gain_key
    )
    normed_part = to_width(
        "grad_normed", (grad_q_low, 0, wq, 0, q_cols), (grad_kv_low, 0, wkv, 0, 2 * kv_cols), tile=512
    )
    my_grad_normed = sum_of_parts(after(normed_part, all_layer_out))
    query_terms = [
        weight_grad(
            "query_grad", n, bits[0], (normed_low, grad_q_low, 0, q_cols), (hidden_later, context, 0, o_half)
        ),
        weight_grad(
            "key_value_grad",
            n,
            flipped[0],
            (normed_low, after(grad_kv_low, normed_part), 0, 2 * kv_cols),
            (hidden_later, context, 1, o_half),
        ),
    ]
    my_grad_normed = after(my_grad_normed, *down_gots[-1], query_terms[0][0], query_terms[1][0])
    my_tokens_grad = on_quarter(
        tokens_grad_kernel,
        "tokens_grad_rows",
        (my_tokens, my_grad_hidden, my_grad_normed),
        (gain_input,),
        (BF16,),
    )[0]

    (qo, kvo), _, _ = scatter_sums(query_terms, pair, beside=((my_tokens_grad,),))
    query_sum = qo[:, :q_cols]
    key_sum = kvo[:, :kv_cols]
    value_sum = kvo[:, kv_cols : 2 * kv_cols]
    out_sum = jnp.concatenate([qo[:, q_cols:], kvo[:, 2 * kv_cols :]], axis=1).T

    heads_sum = jnp.concatenate([jnp.sum(q_gain_part, axis=0), jnp.sum(k_gain_part, axis=0)])[None, :]
    for bit in [1] + bits:
        heads_sum = heads_sum + exchange(heads_sum, bit)
    head = HD // n
    heads_sum = lax.dynamic_slice_in_dim(heads_sum.reshape(2, n, head), me, 1, 1).reshape(-1)

    def along_rows(weight, grad):
        return jnp.sum(weight.astype(F32) * grad, axis=1)

    input_gain_part = (
        along_rows(query_weight, query_sum)
        + along_rows(key_weight, key_sum)
        + along_rows(value_weight, value_sum)
    ) / input_gain.astype(F32)
    post_gain_part = (
        along_rows(gate_weight, gate_sum) + along_rows(up_weight, up_sum)
    ) / post_gain.astype(F32)
    small = jnp.concatenate([input_gain_part, post_gain_part, heads_sum])[None, :]
    step = 1
    while step < parts:
        small = small + lax.ppermute(small, "fsdp", [(i, i ^ step) for i in range(parts)])
        step *= 2
    small = small[0]

    tokens_grad = leave("tokens_grad", order, all_parts(my_tokens_grad), jnp.arange(parts), F32)
    layer_out = leave("layer_out", order, all_layer_out, jnp.arange(parts), BF16)
    return (
        layer_out,
        tokens_grad,
        small[:block],
        query_sum,
        key_sum,
        value_sum,
        small[2 * block : 2 * block + head],
        small[2 * block + head :],
        out_sum,
        small[block : 2 * block],
        gate_sum,
        up_sum,
        down_sum,
    )


def solution(mesh):
    placed = (
        P("blk", None),
        P(),
        P("blk"),
        P("blk", "fsdp"),
        P("blk", "fsdp"),
        P("blk", "fsdp"),
        P("blk"),
        P("blk"),
        P("fsdp", "blk"),
        P("blk"),
        P("blk", "fsdp"),
        P("blk", "fsdp"),
        P("fsdp", "blk"),
        P("blk", None),
    )
    return jax.shard_map(
        shards,
        mesh=mesh,
        in_specs=placed,
        out_specs=(
            P("blk", None),
            P("blk", None),
            P("blk"),
            P("blk", "fsdp"),
            P("blk", "fsdp"),
            P("blk", "fsdp"),
            P("blk"),
            P("blk"),
            P("fsdp", "blk"),
            P("blk"),
            P("blk", "fsdp"),
            P("blk", "fsdp"),
            P("fsdp", "blk"),
        ),
        check_vma=False,
    )
```

```python
import functools
import math

import jax
import jax.numpy as jnp
from jax import lax
from jax.experimental import pallas as pl
from jax.experimental.pallas import tpu as pltpu
from jax.sharding import PartitionSpec as P

HD = 128
EPS = 1e-06
THETA = 1000000.0
LOG2E = math.log2(math.e)
LN2 = math.log(2.0)
MIB = 1024 * 1024

F32 = jnp.float32
BF16 = jnp.bfloat16


def dims(lhs, rhs, left, right):
    return lax.dot_general(lhs, rhs, (((left,), (right,)), ((), ())), preferred_element_type=F32)


def mask_order(n):
    return [2 * i for i in range(n // 2)] + [2 * i + 1 for i in range(n // 2)]


def high_bits(n):
    return [1 << i for i in range(1, n.bit_length() - 1)]


def exchange(block, bit):
    n = lax.axis_size("blk")
    return lax.ppermute(block, "blk", [(i, i ^ bit) for i in range(n)])


def together(values, others=()):
    return lax.optimization_barrier((*values, *others))[: len(values)]


def after(value, *others):
    return lax.optimization_barrier((value,) + others)[0]


def gather_step(held, orders, step, before=(), beside=()):
    sent = []
    for have in held:
        one = [have[m] for m in sorted(have)]
        sent.append(one[0] if len(one) == 1 else jnp.concatenate(one, axis=0))
    sent = together(sent, before)
    raw = [exchange(x, order[step]) for x, order in zip(sent, orders)]
    got = together(raw, beside)
    for have, brought, order in zip(held, got, orders):
        rows = have[0].shape[0]
        for i, m in enumerate(sorted(have)):
            have[m | order[step]] = brought[i * rows : (i + 1) * rows]
    return tuple(raw)


def gather_end(held):
    own = [jnp.concatenate([have[m] for m in sorted(have)], axis=0) for have in held]
    return [(x, exchange(x, 1)) for x in own]


def gather_rest(held, orders, start, before=(), beside=()):
    raw = ()
    for step in range(start, len(orders[0])):
        raw = gather_step(
            held,
            orders,
            step,
            before if step == start else (),
            beside if step == len(orders[0]) - 1 else (),
        )
    return raw


def add_low(a, b):
    return (a.astype(F32) + b.astype(F32)).astype(BF16)


def scatter_terms(parts, orders, beside=()):
    held = []
    sent = [part[0] for part in parts]
    for (leave, stay), order in zip(parts, orders):
        masks = [m for m in range(0, 4 * stay.shape[0], 2) if not m & order[0]][: 2 ** (len(order) - 1)]
        rows = stay.shape[0] // len(masks)
        held.append({m: stay[i * rows : (i + 1) * rows] for i, m in enumerate(masks)})
    sends, gots = [], []
    for step in range(len(orders[0])):
        if step:
            sent = []
            for have, order in zip(held, orders):
                leave = [add_low(*have.pop(m)) for m in sorted(have) if m & order[step]]
                sent.append(leave[0] if len(leave) == 1 else jnp.concatenate(leave, axis=0))
                for m in have:
                    have[m] = add_low(*have[m])
        sent = together(sent)
        sends.append(sent)
        raw = [exchange(x, order[step]) for x, order in zip(sent, orders)]
        gots.append(tuple(raw))
        got = together(raw, beside[step] if step < len(beside) else ())
        for have, back in zip(held, got):
            rows = back.shape[0] // len(have)
            for i, m in enumerate(sorted(have)):
                have[m] = (have[m], back[i * rows : (i + 1) * rows])
    return [have[0] for have in held], sends, gots


def scatter_sums(parts, orders, beside=()):
    terms, sends, gots = scatter_terms(parts, orders, beside)
    return [a.astype(F32) + b.astype(F32) for a, b in terms], sends, gots


def leaving_first(n, bit):
    masks = [2 * i for i in range(n // 2)]
    return [i for i, m in enumerate(masks) if m & bit] + [i for i, m in enumerate(masks) if not m & bit]


def split_sum(own, got, n, bit):
    rows = own.shape[0] // (n // 2)
    at = leaving_first(n, bit)

    def part(array, which):
        return jnp.concatenate([array[i * rows : (i + 1) * rows] for i in which], axis=0)

    half = len(at) // 2
    return tuple(add_low(part(own, w), part(got, w)) for w in (at[:half], at[half:]))


def norm_scale(values):
    return lax.rsqrt(jnp.mean(values * values, axis=-1, keepdims=True) + EPS)


def norm_back(values, scale, weighted):
    inner = jnp.mean(weighted * values, axis=-1, keepdims=True)
    return scale * (weighted - values * scale * scale * inner)


def rope_tables(places, width):
    half = width // 2
    freqs = THETA ** (-jnp.arange(half, dtype=F32) * 2.0 / width)
    angles = places.astype(F32)[:, None] * freqs[None, :]
    sine = jnp.sin(angles)
    cosine = jnp.cos(angles)
    return (jnp.concatenate([cosine, cosine], axis=1), jnp.concatenate([-sine, sine], axis=1))


def turned(values):
    return pltpu.roll(values, HD // 2, 1)


def call(kernel, name, grid, in_specs, out_specs, out_shape, args, flops, scratch=(), scalars=None, near=(), near_out=False):
    if scalars is None:
        spec = {"grid": grid, "in_specs": in_specs, "out_specs": out_specs, "scratch_shapes": scratch}
    else:
        spec = {
            "grid_spec": pltpu.PrefetchScalarGridSpec(
                num_scalar_prefetch=1,
                grid=grid,
                in_specs=in_specs,
                out_specs=out_specs,
                scratch_shapes=scratch,
            )
        }
    args = [a if i in near else in_far(a)[0] for i, a in enumerate(args)]
    if not near_out:
        out_shape = [pltpu.HBM(o.shape, o.dtype) for o in out_shape]
    if scalars is not None:
        args = (scalars, *args)
    return pl.pallas_call(
        kernel,
        out_shape=out_shape,
        compiler_params=pltpu.CompilerParams(vmem_limit_bytes=28 * MIB),
        cost_estimate=pl.CostEstimate(flops=0, bytes_accessed=0, transcendentals=0),
        name=name,
        **spec,
    )(*args)


def in_far(*arrays):
    big = 1 << 17
    return [
        pltpu.with_memory_space_constraint(a, pltpu.HBM) if a.size * a.dtype.itemsize >= big else a
        for a in arrays
    ]


def shape(dims_, dtype):
    return jax.ShapeDtypeStruct(dims_, dtype)


def picked(array, order):
    n = order.shape[0]
    block = array.shape[1] // n
    return jnp.concatenate(
        [lax.dynamic_slice_in_dim(array, order[i] * block, block, 1) for i in range(n)], axis=1
    )


def enter_kernel(sc, a_ref, b_ref, a_out, b_out):
    a_out[...] = a_ref[...]
    b_out[...] = b_ref[...]


def enter(order, first, second):
    rows, width = first.shape
    n = order.shape[0]
    block = width // n
    if block % 128:
        return picked(first, order), picked(second, order)
    source = pl.BlockSpec((rows, block), lambda p, sc: (0, sc[p]))
    target = pl.BlockSpec((rows, block), lambda p, sc: (0, p))
    return call(
        enter_kernel,
        "enter",
        (n,),
        [source, source],
        [target, target],
        [shape(first.shape, first.dtype), shape(second.shape, second.dtype)],
        (first, second),
        0,
        scalars=order,
        near=(0, 1),
        near_out=True,
    )


def leave_blocks(sc, out_ref, result):
    width = result.shape[1]
    n = len(sc)
    block = width // n
    if block % 128:
        out_ref[...] = result.astype(out_ref.dtype)
        return
    for p in range(n):
        at = pl.ds(pl.multiple_of(sc[p] * block, 128), block)
        out_ref[:, at] = result[:, p * block : (p + 1) * block].astype(out_ref.dtype)


def leave_kernel(n, sc, value_ref, out_ref):
    leave_blocks([sc[p] for p in range(n)], out_ref, value_ref[...])


def leave(name, order, value, places, dtype):
    rows, width = value.shape
    n = order.shape[0]
    parts = places.shape[0]
    height = rows // parts
    result = call(
        functools.partial(leave_kernel, n),
        name,
        (parts,),
        [pl.BlockSpec((height, width), lambda i, sc: (sc[n + i], 0))],
        [pl.BlockSpec((height, width), lambda i, sc: (i, 0))],
        [shape((rows, width), dtype)],
        (value,),
        0,
        scalars=jnp.concatenate([order, places.astype(jnp.int32)]),
    )[0]
    if width // n % 128:
        index = jnp.arange(n)
        back = jnp.sum(jnp.where(order[None, :] == index[:, None], index[None, :], 0), axis=1)
        return picked(result, back)
    return result


def post_kernel(tokens_ref, attn_ref, gain_ref, out_ref):
    hidden = tokens_ref[...].astype(F32) + attn_ref[...].astype(F32)
    out_ref[...] = (hidden * norm_scale(hidden) * gain_ref[...]).astype(BF16)


def layer_out_kernel(tokens_ref, attn_ref, mlp_ref, out_ref):
    hidden = tokens_ref[...].astype(F32) + attn_ref[...].astype(F32)
    out_ref[...] = (hidden + mlp_ref[...].astype(F32)).astype(BF16)


def grad_hidden_kernel(tokens_ref, attn_ref, cotangent_ref, grad_ref, gain_ref, out_ref, low_ref):
    hidden = tokens_ref[...].astype(F32) + attn_ref[...].astype(F32)
    weighted = grad_ref[...].astype(F32) * gain_ref[...]
    grad = cotangent_ref[...].astype(F32) + norm_back(hidden, norm_scale(hidden), weighted)
    out_ref[...] = grad
    low_ref[...] = grad.astype(BF16)


def tokens_grad_kernel(tokens_ref, hidden_ref, grad_ref, gain_ref, out_ref):
    inputs = tokens_ref[...].astype(F32)
    weighted = grad_ref[...].astype(F32) * gain_ref[...]
    back = norm_back(inputs, norm_scale(inputs), weighted)
    out_ref[...] = (hidden_ref[...] + back).astype(BF16)


def on_quarter(kernel, name, arrays, gains, dtypes):
    rows, width = arrays[0].shape
    spec = pl.BlockSpec((rows, width), lambda i: (0, 0))
    full = [pl.BlockSpec(g.shape, lambda i: (0, 0)) for g in gains]
    return call(
        kernel,
        name,
        (1,),
        [spec] * len(arrays) + full,
        [spec] * len(dtypes),
        [shape((rows, width), dtype) for dtype in dtypes],
        tuple(arrays) + tuple(gains),
        0,
    )


def head_outputs(product, proj_ref, out_ref, cos_ref, sin_ref, gain_ref, factor):
    proj_ref[...] = product
    for h in range(product.shape[1] // HD):
        one = slice(h * HD, (h + 1) * HD)
        u = product[:, one]
        u = u * norm_scale(u) * gain_ref[...]
        u = u * cos_ref[...] + turned(u) * sin_ref[...]
        out_ref[:, one] = (u * factor if factor else u).astype(BF16)


def halves_product(left_ref, split, w0, w1):
    return dims(left_ref[:, :split], w0[...], 1, 0) + dims(left_ref[:, split:], w1[...], 1, 0)


def keys_kernel(
    split, tokens_ref, gain_ref, w0, w1, cos_ref, sin_ref, head_gain, normed_ref, proj_ref, keys, values
):
    @pl.when(pl.program_id(0) == 0)
    def _():
        inputs = tokens_ref[...].astype(F32)
        normed_ref[...] = (inputs * norm_scale(inputs) * gain_ref[...]).astype(BF16)
        product = halves_product(normed_ref, split, w0, w1)
        head_outputs(product, proj_ref, keys, cos_ref, sin_ref, head_gain, None)

    @pl.when(pl.program_id(0) == 1)
    def _():
        values[...] = halves_product(normed_ref, split, w0, w1).astype(BF16)


def queries_kernel(split, normed_ref, w0, w1, cos_ref, sin_ref, head_gain, proj_ref, queries):
    product = halves_product(normed_ref, split, w0, w1)
    head_outputs(product, proj_ref, queries, cos_ref, sin_ref, head_gain, HD**-0.5 * LOG2E)


def whole_block(array):
    return pl.BlockSpec(array.shape, lambda *i: (0, 0))


def project_keys(tokens, gain, pair, cosine, sine, head_gain):
    rows, width = tokens.shape
    columns = pair[0].shape[1] // 2
    split = width // 2
    side = pl.BlockSpec((split, columns), lambda j: (0, j))
    out = pl.BlockSpec((rows, columns), lambda j: (0, 0))
    small = [cosine, sine, head_gain]
    return call(
        functools.partial(keys_kernel, split),
        "project_keys",
        (2,),
        [whole_block(tokens), whole_block(gain), side, side] + [whole_block(a) for a in small],
        [whole_block(tokens), out, out, out],
        [
            shape((rows, width), BF16),
            shape((rows, columns), F32),
            shape((rows, columns), BF16),
            shape((rows, columns), BF16),
        ],
        (tokens, gain, *pair, *small),
        4 * rows * width * columns,
        near=range(7),
    )


def project_queries(normed, pair, cosine, sine, head_gain, tile=256):
    rows, width = normed.shape
    columns = pair[0].shape[1]
    split = width // 2
    side = pl.BlockSpec((split, tile), lambda j: (0, j))
    out = pl.BlockSpec((rows, tile), lambda j: (0, j))
    small = [cosine, sine, head_gain]
    return call(
        functools.partial(queries_kernel, split),
        "project_queries",
        (columns // tile,),
        [whole_block(normed), side, side] + [whole_block(a) for a in small],
        [out, out],
        [shape((rows, columns), F32), shape((rows, columns), BF16)],
        (normed, *pair, *small),
        2 * rows * width * columns,
    )


def to_width_kernel(count, half, *refs):
    i = pl.program_id(0)
    lefts = refs[:count]
    rights = refs[count : 3 * count]
    out_ref = refs[-1]
    for parity, here in ((0, i < half), (1, i >= half)):

        @pl.when(here)
        def _(parity=parity):
            total = None
            for left, pair in zip(lefts, zip(rights[::2], rights[1::2])):
                term = dims(left[...], pair[parity][...], 1, 1)
                total = term if total is None else total + term
            out_ref[...] = total.astype(out_ref.dtype)


def to_width(name, *terms, tile=256, near=()):
    rows = terms[0][0].shape[0]
    split = terms[0][2][0].shape[0]
    half = split // tile
    in_specs = []
    for left, at, pair, where, columns in terms:
        in_specs.append(pl.BlockSpec((rows, columns), lambda i, at=at: (0, at)))
    args = [t[0] for t in terms]
    flops = 0
    for left, at, pair, where, columns in terms:
        in_specs.append(
            pl.BlockSpec((tile, columns), lambda i, w=where: (jnp.minimum(i, half - 1), w))
        )
        in_specs.append(
            pl.BlockSpec((tile, columns), lambda i, w=where: (jnp.maximum(i - half, 0), w))
        )
        args += list(pair)
        flops += 4 * rows * split * columns
    return call(
        functools.partial(to_width_kernel, len(terms), half),
        name,
        (2 * half,),
        in_specs,
        [pl.BlockSpec((rows, tile), lambda i: (0, i))],
        [shape((rows, 2 * split), BF16)],
        tuple(args),
        flops,
        near=near,
    )[0]


def from_width_kernel(split, bounds, left_ref, *refs):
    out_ref = refs[-1]
    j = pl.program_id(0)
    for k in range(len(bounds) - 1):

        @pl.when((j >= bounds[k]) & (j < bounds[k + 1]))
        def _(w0=refs[2 * k], w1=refs[2 * k + 1]):
            product = dims(left_ref[:, :split], w0[...], 1, 0) + dims(left_ref[:, split:], w1[...], 1, 0)
            out_ref[...] = product.astype(out_ref.dtype)


def from_width(name, left, *sides, tile=256):
    rows, width = left.shape
    split = width // 2
    bounds = [0]
    specs, args = [], [left]
    for pair, start, columns in sides:
        low, high = bounds[-1], bounds[-1] + columns // tile
        bounds.append(high)
        specs += [
            pl.BlockSpec(
                (split, tile),
                lambda j, low=low, high=high, first=start // tile: (0, first + jnp.clip(j, low, high - 1) - low),
            )
        ] * 2
        args += list(pair)
    return call(
        functools.partial(from_width_kernel, split, tuple(bounds)),
        name,
        (bounds[-1],),
        [pl.BlockSpec((rows, width), lambda j: (0, 0))] + specs,
        [pl.BlockSpec((rows, tile), lambda j: (0, j))],
        [shape((rows, bounds[-1] * tile), BF16)],
        tuple(args),
        2 * rows * width * bounds[-1] * tile,
    )[0]


def units_kernel(split, post_ref, wg0, wg1, wu0, wu1, grad_ref, act_ref, gate_out, up_out):
    def product(w0, w1):
        return dims(post_ref[:, :split], w0[...], 1, 0) + dims(post_ref[:, split:], w1[...], 1, 0)

    gate = product(wg0, wg1)
    up = product(wu0, wu1)
    grad_act = grad_ref[...].astype(F32)
    sigma = jax.nn.sigmoid(gate)
    silu = gate * sigma
    act_ref[...] = (silu * up).astype(BF16)
    up_out[...] = (grad_act * silu).astype(BF16)
    gate_out[...] = (grad_act * up * sigma * (1.0 + gate * (1.0 - sigma))).astype(BF16)


def hidden_units(post, wg, wu, grad_act, tile=256):
    rows, width = post.shape
    units = grad_act.shape[1]
    split = width // 2
    side = pl.BlockSpec((split, tile), lambda j: (0, j))
    part = pl.BlockSpec((rows, tile), lambda j: (0, j))
    unit = shape((rows, units), BF16)
    return call(
        functools.partial(units_kernel, split),
        "hidden_units",
        (units // tile,),
        [pl.BlockSpec(post.shape, lambda j: (0, 0)), side, side, side, side, part],
        [part, part, part],
        [unit, unit, unit],
        (post, *wg, *wu, grad_act),
        4 * rows * width * units,
        near=(1, 2, 3, 4),
    )


def side_products(count, sides, refs):
    turned_lefts = [left[...].T for left in refs[:count]]
    at = count
    for side in sides:
        start = 0
        terms = []
        for which in side:
            right = refs[at]
            at += 1
            columns = slice(start, start + right.shape[1])
            terms.append((columns, dims(turned_lefts[which], right[...], 1, 0)))
            start = columns.stop
        yield terms


def away_kernel(count, sides, *refs):
    outs = refs[-len(sides) :]
    for out_ref, terms in zip(outs, side_products(count, sides, refs)):
        for columns, term in terms:
            out_ref[:, columns] = term.astype(BF16)


def home_kernel(count, sides, steps, sc, *refs):
    inputs = count + sum(len(side) for side in sides)
    gots = refs[inputs : inputs + len(sides)]
    outs = refs[inputs + len(sides) :]
    step = pl.program_id(0)
    for i, terms in enumerate(side_products(count, sides, refs)):
        leaves = sc[(5 * i + 1) * steps + step] == 1
        for columns, term in terms:
            total = (term + gots[i][:, columns].astype(F32)).astype(BF16)

            @pl.when(leaves)
            def _(i=i, columns=columns, total=total):
                outs[2 * i][:, columns] = total

            @pl.when(jnp.logical_not(leaves))
            def _(i=i, columns=columns, total=total):
                outs[2 * i + 1][:, columns] = total


def visits(places, wanted):
    held = []
    for step, (place, own) in enumerate(zip(places, wanted)):
        if own:
            held.append(place)
        elif any(wanted[:step]):
            held.append(held[-1])
        else:
            held.append(next(p for p, o in zip(places[step:], wanted[step:]) if o))
    return held


def weight_grads(name, n, bits_of, lefts, *sides, tile=512):
    rows, width = lefts[0].shape
    split = width // 2
    count = len(lefts)
    kinds = [[term[0] for term in side] for side in sides]
    rights = [(term[1], term[2], term[3]) for side in sides for term in side]
    totals = [sum(term[3] for term in side) for side in sides]
    args = (*lefts, *[r[0] for r in rights])

    def products(first):
        tiles = split // tile
        return call(
            functools.partial(away_kernel, count, kinds),
            name + "_away" if first else name,
            (tiles,),
            [pl.BlockSpec((rows, tile), lambda i, f=first: (0, f + i))] * count
            + [pl.BlockSpec((rows, c), lambda i, w=w: (0, w)) for _, w, c in rights],
            [pl.BlockSpec((tile, total), lambda i: (i, 0)) for total in totals],
            [shape((split, total), BF16) for total in totals],
            args,
            0,
        )

    gots = together([exchange(away, 1) for away in products(split // tile)])
    block = width // n
    if block % 128:
        return [split_sum(home, got, n, bit) for home, got, bit in zip(products(0), gots, bits_of)]
    steps = n // 2
    order = leaving_first(n, bits_of[0])
    table = []
    for bit in bits_of:
        masks = [2 * i for i in range(steps)]
        gone = [i for i, m in enumerate(masks) if m & bit]
        kept = [i for i, m in enumerate(masks) if not m & bit]
        leaves = [i in gone for i in order]
        places = [(gone if i in gone else kept).index(i) for i in order]
        table += order + [int(x) for x in leaves]
        table += visits(places, leaves) + visits(places, [not x for x in leaves]) + [0] * steps
    outs = call(
        functools.partial(home_kernel, count, kinds, steps),
        name,
        (steps,),
        [pl.BlockSpec((rows, block), lambda i, sc: (0, sc[i]))] * count
        + [pl.BlockSpec((rows, c), lambda i, sc, w=w: (0, w)) for _, w, c in rights]
        + [pl.BlockSpec((block, total), lambda i, sc: (sc[i], 0)) for total in totals],
        [
            pl.BlockSpec((block, total), lambda i, sc, at=(5 * k + 2 + part) * steps: (sc[at + i], 0))
            for k, total in enumerate(totals)
            for part in range(2)
        ],
        [shape((split // 2, total), BF16) for total in totals for part in range(2)],
        (*args, *gots),
        0,
        scalars=jnp.array(table, jnp.int32),
    )
    return list(zip(outs[::2], outs[1::2]))


def heads_back_kernel(terms, passed, *refs):
    grads, refs = refs[:terms], refs[terms:]
    others, refs = refs[:passed], refs[passed:]
    proj_ref, cos_ref, sin_ref, gain_ref, out_ref, sum_ref = refs
    columns = proj_ref.shape[1]
    total = None
    for h in range(columns // HD):
        one = slice(h * HD, (h + 1) * HD)
        grad = grads[0][:, one].astype(F32)
        for more in grads[1:]:
            grad = grad + more[:, one].astype(F32)
        grad = grad * cos_ref[...] + turned(grad * sin_ref[...])
        u = proj_ref[:, one]
        scale = norm_scale(u)
        term = jnp.sum((grad * u * scale).reshape(-1, 8, HD), axis=0)
        total = term if total is None else total + term
        out_ref[:, one] = norm_back(u, scale, grad * gain_ref[...]).astype(BF16)
    sum_ref[...] = total
    if passed:
        other = others[0][...].astype(F32)
        for more in others[1:]:
            other = other + more[...].astype(F32)
        out_ref[:, columns:] = other.astype(BF16)


def heads_back(name, grads, others, proj, cosine, sine, gain):
    rows, columns = proj.shape
    args = (*grads, *others, proj, cosine, sine, gain)
    total = columns + (others[0].shape[1] if others else 0)
    return call(
        functools.partial(heads_back_kernel, len(grads), len(others)),
        name,
        (1,),
        [pl.BlockSpec(a.shape, lambda i: (0, 0)) for a in args],
        [pl.BlockSpec((rows, total), lambda i: (0, 0)), pl.BlockSpec((8, HD), lambda i: (0, 0))],
        [shape((rows, total), BF16), shape((8, HD), F32)],
        args,
        20 * rows * columns,
    )


def fetch(halves, columns, scratch, sems):
    copies = []
    for i, half in enumerate(halves):
        rows = half.shape[0]
        at = pl.ds((i % 2) * rows, rows)
        copy = pltpu.make_async_copy(half.at[:, columns], scratch[i // 2].at[at], sems.at[i])
        copy.start()
        copies.append(copy)
    return copies


def attend_kernel(
    span, head, heads, sc, q_ref, k0, k1, v0, v1, ctx_ref, lse_ref, k_s, v_s, acc_s, sum_s, sems
):
    columns = slice(head * HD, (head + heads) * HD)
    copies = fetch((k0, k1, v0, v1), columns, (k_s, v_s), sems)
    group = q_ref.shape[1] // HD // heads
    rows = span * group
    for copy in copies:
        copy.wait()
    for s in range(2):
        top = slice(s * span, (s + 1) * span)

        def stacked(h):
            parts = range(h * group, (h + 1) * group)
            return jnp.concatenate([q_ref[top, g * HD : (g + 1) * HD] for g in parts], axis=0)

        qs = [stacked(h) for h in range(heads)]
        acc_s[...] = jnp.zeros_like(acc_s)
        sum_s[...] = jnp.zeros_like(sum_s)

        def step(p, masked):
            at = pl.ds(pl.multiple_of(sc[2 + p] * span, span), span)
            es = [jnp.exp2(dims(qs[h], k_s[at, h * HD : (h + 1) * HD], 1, 1)) for h in range(heads)]
            if masked:
                row = lax.broadcasted_iota(jnp.int32, (rows, span), 0) % span
                col = lax.broadcasted_iota(jnp.int32, (rows, span), 1)
                es = [jnp.where(row >= col, e, 0.0) for e in es]
            for h, e in enumerate(es):
                part = e[:, :HD]
                for c in range(HD, span, HD):
                    part = part + e[:, c : c + HD]
                sum_s[h] += part
                acc_s[h] += dims(e.astype(BF16), v_s[at, h * HD : (h + 1) * HD], 1, 0)

        pl.loop(0, sc[s])(lambda p: step(p, False))
        step(sc[s], True)
        for h in range(heads):
            total = jnp.sum(sum_s[h], axis=1, keepdims=True)
            ctx = (acc_s[h] / total).astype(BF16)
            for g in range(group):
                at = slice((h * group + g) * HD, (h * group + g + 1) * HD)
                ctx_ref[top, at] = ctx[g * span : (g + 1) * span]
            wide = jnp.broadcast_to(jnp.log2(total), (rows, HD))
            lse_ref[h, s : s + 1, :] = wide.T[0:1]


def attend_back_kernel(
    span, head, heads, sc, q_ref, do_ref, ctx_ref, lse_ref, k0, k1, v0, v1,
    dq_ref, dk0, dk1, dv0, dv1, k_s, v_s, dk_s, dv_s, dq_s, sems,
):
    half = k0.shape[0]
    columns = slice(head * HD, (head + heads) * HD)
    copies = fetch((k0, k1, v0, v1), columns, (k_s, v_s), sems)
    group = q_ref.shape[1] // HD // heads
    rows = span * group
    chunks = 2 * half // span
    cols = [slice(h * HD, (h + 1) * HD) for h in range(heads)]
    later = (sc[1] > sc[0]).astype(jnp.int32)

    def clear(p):
        at = pl.ds(pl.multiple_of(sc[2 + p] * span, span), span)
        dk_s[at] = jnp.zeros((span, heads * HD), F32)
        dv_s[at] = jnp.zeros((span, heads * HD), F32)

    pl.loop(jnp.maximum(sc[0], sc[1]) + 1, chunks)(clear)
    for first in (True, False):
        which = later if first else 1 - later
        top = pl.ds(pl.multiple_of(which * span, span), span)

        def stacked(ref, h):
            parts = range(h * group, (h + 1) * group)
            return jnp.concatenate([ref[top, g * HD : (g + 1) * HD] for g in parts], axis=0)

        qs = [stacked(q_ref, h) for h in range(heads)]
        dos = [stacked(do_ref, h) for h in range(heads)]
        q_ts = [q.T for q in qs]
        do_ts = [do.T for do in dos]
        products = [dos[h].astype(F32) * stacked(ctx_ref, h).astype(F32) for h in range(heads)]
        deltas = [jnp.sum(product.T, axis=0, keepdims=True) for product in products]
        lses = [lse_ref[h, pl.ds(which, 1), :] for h in range(heads)]
        dq_s[...] = jnp.zeros_like(dq_s)
        if first:
            for copy in copies:
                copy.wait()

        def step(p, masked):
            at = pl.ds(pl.multiple_of(sc[2 + p] * span, span), span)
            ks = [k_s[at, c] for c in cols]
            scores = [dims(ks[h], q_ts[h], 1, 0) for h in range(heads)]
            grad_probs = [dims(v_s[at, cols[h]], do_ts[h], 1, 0) for h in range(heads)]
            probs = [jnp.exp2(scores[h] - lses[h]) for h in range(heads)]
            if masked:
                key = lax.broadcasted_iota(jnp.int32, (span, rows), 0)
                query = lax.broadcasted_iota(jnp.int32, (span, rows), 1) % span
                probs = [jnp.where(query >= key, p, 0.0) for p in probs]
            grads = [(probs[h] * (grad_probs[h] - deltas[h])).astype(BF16) for h in range(heads)]
            for h in range(heads):
                dv = dims(probs[h].astype(BF16), dos[h], 1, 0)
                dk = dims(grads[h], qs[h], 1, 0)
                if first:
                    dv_s[at, cols[h]] = dv
                    dk_s[at, cols[h]] = dk
                else:
                    dv_s[at, cols[h]] += dv
                    dk_s[at, cols[h]] += dk
                dq_s[h] += dims(ks[h], grads[h], 0, 0)

        pl.loop(0, sc[which])(lambda p: step(p, False))
        step(sc[which], True)
        for h in range(heads):
            dq = dq_s[h].T * (HD**-0.5)
            for g in range(group):
                at = slice((h * group + g) * HD, (h * group + g + 1) * HD)
                dq_ref[top, at] = dq[g * span : (g + 1) * span]
    dk0[...] = (dk_s[:half] * LN2).astype(BF16)
    dk1[...] = (dk_s[half:] * LN2).astype(BF16)
    dv0[...] = dv_s[:half].astype(BF16)
    dv1[...] = dv_s[half:].astype(BF16)


def head_groups(kv_local, half):
    heads = kv_local if half <= 4096 else 1
    return heads, range(0, kv_local, heads)


def attend(scalars, queries, keys, values, span):
    rows, width = queries.shape
    half = keys[0].shape[0]
    kv_local = keys[0].shape[1] // HD
    heads, firsts = head_groups(kv_local, half)
    across = width // kv_local * heads
    stacked = width // kv_local // HD * span
    far = pl.BlockSpec(memory_space=pl.ANY)
    results = []
    for head in firsts:
        results.append(
            pl.pallas_call(
                functools.partial(attend_kernel, span, head, heads),
                grid_spec=pltpu.PrefetchScalarGridSpec(
                    num_scalar_prefetch=1,
                    grid=(1,),
                    in_specs=[pl.BlockSpec((rows, across), lambda i, sc, at=head // heads: (0, at))]
                    + [far] * 4,
                    out_specs=[
                        pl.BlockSpec((rows, across), lambda i, sc: (0, 0)),
                        pl.BlockSpec((heads, 2, stacked), lambda i, sc: (0, 0, 0)),
                    ],
                    scratch_shapes=[pltpu.VMEM((2 * half, heads * HD), BF16)] * 2
                    + [pltpu.VMEM((heads, stacked, HD), F32)] * 2
                    + [pltpu.SemaphoreType.DMA((4,))],
                ),
                out_shape=[shape((rows, across), BF16), shape((heads, 2, stacked), F32)],
                compiler_params=pltpu.CompilerParams(
                    vmem_limit_bytes=min(60 * MIB, 16 * MIB + 44 * HD * half)
                ),
                cost_estimate=pl.CostEstimate(
                    flops=16 * rows * half * across, bytes_accessed=8 * half * HD, transcendentals=0
                ),
                name="attend",
            )(scalars, queries, *in_far(*keys, *values))
        )
    if len(results) == 1:
        return results[0]
    return [jnp.concatenate(both, axis=1 - i) for i, both in enumerate(zip(*results))]


def attend_back(scalars, queries, grad_context, context, lse, keys, values, span):
    rows, width = queries.shape
    half = keys[0].shape[0]
    kv_local = keys[0].shape[1] // HD
    heads, firsts = head_groups(kv_local, half)
    across = width // kv_local * heads
    stacked = width // kv_local // HD * span
    far = pl.BlockSpec(memory_space=pl.ANY)
    tall = pl.BlockSpec((half, heads * HD), lambda i, sc: (0, 0))
    grads = pltpu.HBM((half, heads * HD), BF16)
    results = []
    for head in firsts:
        at = head // heads
        wide = pl.BlockSpec((rows, across), lambda i, sc, at=at: (0, at))
        results.append(
            pl.pallas_call(
                functools.partial(attend_back_kernel, span, head, heads),
                grid_spec=pltpu.PrefetchScalarGridSpec(
                    num_scalar_prefetch=1,
                    grid=(1,),
                    in_specs=[wide] * 3
                    + [pl.BlockSpec((heads, 2, stacked), lambda i, sc, at=at: (at, 0, 0))]
                    + [far] * 4,
                    out_specs=[pl.BlockSpec((rows, across), lambda i, sc: (0, 0))] + [tall] * 4,
                    scratch_shapes=[pltpu.VMEM((2 * half, heads * HD), BF16)] * 2
                    + [pltpu.VMEM((2 * half, heads * HD), F32)] * 2
                    + [pltpu.VMEM((heads, HD, stacked), F32), pltpu.SemaphoreType.DMA((4,))],
                ),
                out_shape=[pltpu.HBM((rows, across), F32)] + [grads] * 4,
                compiler_params=pltpu.CompilerParams(
                    vmem_limit_bytes=min(60 * MIB, 16 * MIB + 44 * HD * half)
                ),
                cost_estimate=pl.CostEstimate(
                    flops=40 * rows * half * across, bytes_accessed=32 * half * HD, transcendentals=0
                ),
                name="attend_back",
            )(scalars, *in_far(queries, grad_context, context, lse, *keys, *values))
        )
    if len(results) == 1:
        return results[0]
    return [jnp.concatenate(parts, axis=1) for parts in zip(*results)]


def sum_of_parts(part):
    return lax.psum_scatter(part, "fsdp", scatter_dimension=0, tiled=True)


def all_parts(mine):
    return lax.all_gather(mine, "fsdp", axis=0, tiled=True)


def shards(
    tokens,
    span_order,
    input_gain,
    query_weight,
    key_weight,
    value_weight,
    query_gain,
    key_gain,
    output_weight,
    post_gain,
    gate_weight,
    up_weight,
    down_weight,
    cotangent,
):
    n = lax.axis_size("blk")
    me = lax.axis_index("blk")
    bits = high_bits(n)
    flipped = bits[::-1]
    masks = mask_order(n)
    rows, width = tokens.shape
    block = width // n
    split = width // 2
    span = rows // 2
    q_cols = query_weight.shape[1]
    kv_cols = key_weight.shape[1]
    heads = q_cols // HD
    kv_heads = kv_cols // HD
    units = gate_weight.shape[1]
    o_cols = output_weight.shape[0]

    mask_list = jnp.array(masks, jnp.int32)
    order = me ^ mask_list
    pair = [bits, flipped]

    spans = span_order.reshape(n, 2)
    chunk_ids = jnp.sum(
        jnp.where(order[:, None, None] == jnp.arange(n)[None, :, None], spans[None], 0),
        axis=1,
    ).reshape(-1)
    count = 2 * n
    positions = jnp.sum(
        jnp.where(
            chunk_ids[None, :] == jnp.arange(count)[:, None], jnp.arange(count)[None, :], 0
        ),
        axis=1,
    )
    scalars = jnp.concatenate([chunk_ids[:2], positions]).astype(jnp.int32)
    places = (chunk_ids[:2, None] * span + jnp.arange(span)[None, :]).reshape(-1)
    cosine, sine = rope_tables(places, HD)

    parts = lax.axis_size("fsdp")
    quarter = rows // parts
    my_part = lax.axis_index("fsdp") * quarter

    def mine(array):
        return lax.dynamic_slice_in_dim(array, my_part, quarter, 0)

    gains = jnp.concatenate([input_gain, post_gain, query_gain, key_gain]).reshape(1, -1)
    first = [{0: query_weight}, {0: jnp.concatenate([key_weight, value_weight], axis=1)}, {0: gains}]
    triple = [bits, flipped, bits]
    out_t = output_weight.T
    o_half = o_cols // 2
    gather_step(first, triple, 0, beside=(out_t,))
    tokens, cotangent = enter(order, tokens, cotangent)
    my_tokens = mine(tokens)
    my_cotangent = mine(cotangent)
    late = gather_rest(first, triple, 1, beside=(tokens, cotangent, cosine, sine, scalars))
    wq, wkv, gains = gather_end(first)
    gains = jnp.concatenate(gains, axis=0).astype(F32)
    gain_input = gains[:, :block].reshape(1, width)
    gain_post = gains[:, block : 2 * block].reshape(1, width)
    chosen = (me ^ jnp.arange(n))[:, None] == mask_list[None, :]
    head_gains = jnp.sum(jnp.where(chosen[:, :, None], gains[None, :, 2 * block :], 0.0), axis=1)
    part = head_gains.shape[1] // 2
    gain_query = head_gains[:, :part].reshape(1, HD)
    gain_key = head_gains[:, part:].reshape(1, HD)

    normed_low, k_proj, keys, values = project_keys(
        tokens, gain_input, wkv, cosine, sine, gain_key
    )
    outs = [{0: out_t[:, :o_half]}, {0: out_t[:, o_half:]}]
    out_got = gather_step(outs, pair, 0, before=late)
    rows_held = [{0: keys}, {0: values}]
    q_proj, queries = project_queries(after(normed_low, keys), wq, cosine, sine, gain_query)
    gather_step(rows_held, pair, 0, before=out_got, beside=(queries,))
    key_got = gather_rest(rows_held, pair, 1)
    all_keys, all_values = gather_end(rows_held)
    context, lse = attend(scalars, queries, all_keys, all_values, span)
    out_got = gather_rest(outs, pair, 1, before=key_got, beside=(context,))
    wo_a, wo_b = gather_end(outs)
    wide = [{0: gate_weight}, {0: up_weight}]
    down_t = down_weight.T
    middle = units // 2
    downs = [{0: down_t[:, :middle]}, {0: down_t[:, middle:]}]
    gather_step(downs, pair, 0, before=out_got, beside=(context,))
    down_got = gather_rest(downs, pair, 1)

    attn_part = to_width(
        "attention_out",
        (context, 0, wo_a, 0, o_half),
        (context, 1, wo_b, 0, o_half),
        tile=512,
    )
    my_attn = sum_of_parts(attn_part)
    my_post = on_quarter(post_kernel, "post", (my_tokens, my_attn), (gain_post,), (BF16,))[0]
    post_low = all_parts(my_post)
    gather_step(wide, pair, 0, before=down_got)
    side_a, side_b = gather_end(downs)
    grad_act = from_width(
        "grad_act", after(cotangent, my_post), (side_a, 0, middle), (side_b, 0, middle)
    )
    gather_rest(wide, pair, 1, beside=(my_post, grad_act))
    wg, wu = gather_end(wide)
    act, grad_gate, grad_up = hidden_units(post_low, wg, wu, grad_act)
    post_part = to_width("grad_post", (grad_gate, 0, wg, 0, units), (grad_up, 0, wu, 0, units), near=(2, 3, 4, 5))
    my_grad_post = sum_of_parts(post_part)

    starts = bits[0], flipped[0]
    act_now, gate_later, up_later = together((act, grad_gate, grad_up), (post_part,))
    unit_terms = weight_grads(
        "units_grad", n, starts, [post_low], [(0, gate_later, 0, units)], [(0, up_later, 0, units)]
    )
    (gate_sum, up_sum), unit_sends, unit_gots = scatter_sums(unit_terms, pair, beside=((), (post_part,)))
    mlp_part = to_width(
        "units_out",
        (act_now, 0, side_a, 0, middle),
        (act_now, 1, side_b, 0, middle),
        tile=512,
    )
    act_later = after(act, mlp_part, *unit_gots[0])
    down_terms = weight_grads(
        "down_grad", n, starts, [cotangent], [(0, act_later, 0, middle)], [(0, act_later, 1, middle)]
    )
    my_grad_post = after(my_grad_post, *[leave for leave, _ in unit_terms])
    my_grad_hidden, my_hidden_low = on_quarter(
        grad_hidden_kernel,
        "grad_hidden",
        (my_tokens, my_attn, my_cotangent, my_grad_post),
        (gain_post,),
        (F32, BF16),
    )
    hidden_low = all_parts(my_hidden_low)
    mlp_part, hidden_low = together(
        (mlp_part, hidden_low), (*unit_sends[-1], *[leave for leave, _ in down_terms])
    )
    my_mlp = sum_of_parts(mlp_part)

    grad_context = from_width("grad_context", hidden_low, (wo_a, 0, o_half), (wo_b, 0, o_half))
    dq, dk_own, dk_other, dv_own, dv_other = attend_back(
        scalars, queries, grad_context, context, lse, all_keys, all_values, span
    )
    (down_a, down_b), _, down_gots = scatter_sums(down_terms, pair, beside=((dk_own,),))
    down_sum = jnp.concatenate([down_a, down_b], axis=1).T
    dk_other, dv_other = together((dk_other, dv_other), (*unit_gots[-1], *down_gots[0]))
    dk_got, dv_got = together((exchange(dk_other, 1), exchange(dv_other, 1)))
    key_sums = split_sum(dk_own, dk_got, n, bits[0])
    value_sums = split_sum(dv_own, dv_got, n, flipped[0])
    (key_terms, value_terms), sends, _ = scatter_terms([key_sums, value_sums], pair)
    my_layer_out = on_quarter(
        layer_out_kernel, "layer_out_rows", (my_tokens, my_attn, after(my_mlp, *sends[0])), (), (BF16,)
    )[0]
    all_layer_out = all_parts(my_layer_out)
    dq, hidden_later = together((dq, hidden_low), tuple(sends[0]))
    grad_q_low, q_gain_part = heads_back("queries_back", [dq], [], q_proj, cosine, sine, gain_query)
    grad_kv_low, k_gain_part = heads_back(
        "keys_back", key_terms, value_terms, k_proj, cosine, sine, gain_key
    )
    normed_part = to_width(
        "grad_normed", (grad_q_low, 0, wq, 0, q_cols), (grad_kv_low, 0, wkv, 0, 2 * kv_cols), tile=512
    )
    my_grad_normed = sum_of_parts(after(normed_part, all_layer_out))
    query_terms = weight_grads(
        "attention_grad",
        n,
        starts,
        [normed_low, hidden_later],
        [(0, grad_q_low, 0, q_cols), (1, context, 0, o_half)],
        [(0, after(grad_kv_low, normed_part, *down_gots[-1]), 0, 2 * kv_cols), (1, context, 1, o_half)],
    )
    my_grad_normed = after(my_grad_normed, query_terms[0][0], query_terms[1][0])
    my_tokens_grad = on_quarter(
        tokens_grad_kernel,
        "tokens_grad_rows",
        (my_tokens, my_grad_hidden, my_grad_normed),
        (gain_input,),
        (BF16,),
    )[0]

    (qo, kvo), _, _ = scatter_sums(query_terms, pair, beside=((my_tokens_grad,),))
    query_sum = qo[:, :q_cols]
    key_sum = kvo[:, :kv_cols]
    value_sum = kvo[:, kv_cols : 2 * kv_cols]
    out_sum = jnp.concatenate([qo[:, q_cols:], kvo[:, 2 * kv_cols :]], axis=1).T

    heads_sum = jnp.concatenate([jnp.sum(q_gain_part, axis=0), jnp.sum(k_gain_part, axis=0)])[None, :]
    for bit in [1] + bits:
        heads_sum = heads_sum + exchange(heads_sum, bit)
    head = HD // n
    heads_sum = lax.dynamic_slice_in_dim(heads_sum.reshape(2, n, head), me, 1, 1).reshape(-1)

    def along_rows(weight, grad):
        return jnp.sum(weight.astype(F32) * grad, axis=1)

    input_gain_part = (
        along_rows(query_weight, query_sum)
        + along_rows(key_weight, key_sum)
        + along_rows(value_weight, value_sum)
    ) / input_gain.astype(F32)
    post_gain_part = (
        along_rows(gate_weight, gate_sum) + along_rows(up_weight, up_sum)
    ) / post_gain.astype(F32)
    small = jnp.concatenate([input_gain_part, post_gain_part, heads_sum])[None, :]
    step = 1
    while step < parts:
        small = small + lax.ppermute(small, "fsdp", [(i, i ^ step) for i in range(parts)])
        step *= 2
    small = small[0]

    tokens_grad = leave("tokens_grad", order, all_parts(my_tokens_grad), jnp.arange(parts), F32)
    layer_out = leave("layer_out", order, all_layer_out, jnp.arange(parts), BF16)
    return (
        layer_out,
        tokens_grad,
        small[:block],
        query_sum,
        key_sum,
        value_sum,
        small[2 * block : 2 * block + head],
        small[2 * block + head :],
        out_sum,
        small[block : 2 * block],
        gate_sum,
        up_sum,
        down_sum,
    )


def solution(mesh):
    placed = (
        P("blk", None),
        P(),
        P("blk"),
        P("blk", "fsdp"),
        P("blk", "fsdp"),
        P("blk", "fsdp"),
        P("blk"),
        P("blk"),
        P("fsdp", "blk"),
        P("blk"),
        P("blk", "fsdp"),
        P("blk", "fsdp"),
        P("fsdp", "blk"),
        P("blk", None),
    )
    return jax.shard_map(
        shards,
        mesh=mesh,
        in_specs=placed,
        out_specs=(
            P("blk", None),
            P("blk", None),
            P("blk"),
            P("blk", "fsdp"),
            P("blk", "fsdp"),
            P("blk", "fsdp"),
            P("blk"),
            P("blk"),
            P("fsdp", "blk"),
            P("blk"),
            P("blk", "fsdp"),
            P("blk", "fsdp"),
            P("fsdp", "blk"),
        ),
        check_vma=False,
    )
```

```python
import functools
import math

import jax
import jax.numpy as jnp
from jax import lax
from jax.experimental import pallas as pl
from jax.experimental.pallas import tpu as pltpu
from jax.sharding import PartitionSpec as P

HD = 128
EPS = 1e-06
THETA = 1000000.0
LOG2E = math.log2(math.e)
LN2 = math.log(2.0)
MIB = 1024 * 1024

F32 = jnp.float32
BF16 = jnp.bfloat16


def dims(lhs, rhs, left, right):
    return lax.dot_general(lhs, rhs, (((left,), (right,)), ((), ())), preferred_element_type=F32)


def mask_order(n):
    return [2 * i for i in range(n // 2)] + [2 * i + 1 for i in range(n // 2)]


def high_bits(n):
    return [1 << i for i in range(1, n.bit_length() - 1)]


def exchange(block, bit):
    n = lax.axis_size("blk")
    return lax.ppermute(block, "blk", [(i, i ^ bit) for i in range(n)])


def together(values, others=()):
    return lax.optimization_barrier((*values, *others))[: len(values)]


def after(value, *others):
    return lax.optimization_barrier((value,) + others)[0]


def gather_step(held, orders, step, before=(), beside=()):
    sent = []
    for have in held:
        one = [have[m] for m in sorted(have)]
        sent.append(one[0] if len(one) == 1 else jnp.concatenate(one, axis=0))
    sent = together(sent, before)
    raw = [exchange(x, order[step]) for x, order in zip(sent, orders)]
    got = together(raw, beside)
    for have, brought, order in zip(held, got, orders):
        rows = have[0].shape[0]
        for i, m in enumerate(sorted(have)):
            have[m | order[step]] = brought[i * rows : (i + 1) * rows]
    return tuple(raw)


def gather_end(held):
    own = [jnp.concatenate([have[m] for m in sorted(have)], axis=0) for have in held]
    return [(x, exchange(x, 1)) for x in own]


def gather_rest(held, orders, start, before=(), beside=()):
    raw = ()
    for step in range(start, len(orders[0])):
        raw = gather_step(
            held,
            orders,
            step,
            before if step == start else (),
            beside if step == len(orders[0]) - 1 else (),
        )
    return raw


def add_low(a, b):
    return (a.astype(F32) + b.astype(F32)).astype(BF16)


def scatter_terms(parts, orders, beside=()):
    held = []
    sent = [part[0] for part in parts]
    for (leave, stay), order in zip(parts, orders):
        masks = [m for m in range(0, 4 * stay.shape[0], 2) if not m & order[0]][: 2 ** (len(order) - 1)]
        rows = stay.shape[0] // len(masks)
        held.append({m: stay[i * rows : (i + 1) * rows] for i, m in enumerate(masks)})
    sends, gots = [], []
    for step in range(len(orders[0])):
        if step:
            sent = []
            for have, order in zip(held, orders):
                leave = [add_low(*have.pop(m)) for m in sorted(have) if m & order[step]]
                sent.append(leave[0] if len(leave) == 1 else jnp.concatenate(leave, axis=0))
                for m in have:
                    have[m] = add_low(*have[m])
        sent = together(sent)
        sends.append(sent)
        raw = [exchange(x, order[step]) for x, order in zip(sent, orders)]
        gots.append(tuple(raw))
        got = together(raw, beside[step] if step < len(beside) else ())
        for have, back in zip(held, got):
            rows = back.shape[0] // len(have)
            for i, m in enumerate(sorted(have)):
                have[m] = (have[m], back[i * rows : (i + 1) * rows])
    return [have[0] for have in held], sends, gots


def scatter_sums(parts, orders, beside=()):
    terms, sends, gots = scatter_terms(parts, orders, beside)
    return [a.astype(F32) + b.astype(F32) for a, b in terms], sends, gots


def leaving_first(n, bit):
    masks = [2 * i for i in range(n // 2)]
    return [i for i, m in enumerate(masks) if m & bit] + [i for i, m in enumerate(masks) if not m & bit]


def split_sum(own, got, n, bit):
    rows = own.shape[0] // (n // 2)
    at = leaving_first(n, bit)

    def part(array, which):
        return jnp.concatenate([array[i * rows : (i + 1) * rows] for i in which], axis=0)

    half = len(at) // 2
    return tuple(add_low(part(own, w), part(got, w)) for w in (at[:half], at[half:]))


def norm_scale(values):
    return lax.rsqrt(jnp.mean(values * values, axis=-1, keepdims=True) + EPS)


def norm_back(values, scale, weighted):
    inner = jnp.mean(weighted * values, axis=-1, keepdims=True)
    return scale * (weighted - values * scale * scale * inner)


def rope_tables(places, width):
    half = width // 2
    freqs = THETA ** (-jnp.arange(half, dtype=F32) * 2.0 / width)
    angles = places.astype(F32)[:, None] * freqs[None, :]
    sine = jnp.sin(angles)
    cosine = jnp.cos(angles)
    return (jnp.concatenate([cosine, cosine], axis=1), jnp.concatenate([-sine, sine], axis=1))


def turned(values):
    return pltpu.roll(values, HD // 2, 1)


def call(kernel, name, grid, in_specs, out_specs, out_shape, args, flops, scratch=(), scalars=None, near=(), near_out=False):
    if scalars is None:
        spec = {"grid": grid, "in_specs": in_specs, "out_specs": out_specs, "scratch_shapes": scratch}
    else:
        spec = {
            "grid_spec": pltpu.PrefetchScalarGridSpec(
                num_scalar_prefetch=1,
                grid=grid,
                in_specs=in_specs,
                out_specs=out_specs,
                scratch_shapes=scratch,
            )
        }
    args = [a if i in near else in_far(a)[0] for i, a in enumerate(args)]
    if not near_out:
        out_shape = [pltpu.HBM(o.shape, o.dtype) for o in out_shape]
    if scalars is not None:
        args = (scalars, *args)
    return pl.pallas_call(
        kernel,
        out_shape=out_shape,
        compiler_params=pltpu.CompilerParams(vmem_limit_bytes=28 * MIB),
        cost_estimate=pl.CostEstimate(flops=0, bytes_accessed=0, transcendentals=0),
        name=name,
        **spec,
    )(*args)


def in_far(*arrays):
    big = 1 << 17
    return [
        pltpu.with_memory_space_constraint(a, pltpu.HBM) if a.size * a.dtype.itemsize >= big else a
        for a in arrays
    ]


def shape(dims_, dtype):
    return jax.ShapeDtypeStruct(dims_, dtype)


def picked(array, order):
    n = order.shape[0]
    block = array.shape[1] // n
    return jnp.concatenate(
        [lax.dynamic_slice_in_dim(array, order[i] * block, block, 1) for i in range(n)], axis=1
    )


def enter_kernel(sc, a_ref, b_ref, a_out, b_out):
    a_out[...] = a_ref[...]
    b_out[...] = b_ref[...]


def enter(order, first, second):
    rows, width = first.shape
    n = order.shape[0]
    block = width // n
    if block % 128:
        return picked(first, order), picked(second, order)
    source = pl.BlockSpec((rows, block), lambda p, sc: (0, sc[p]))
    target = pl.BlockSpec((rows, block), lambda p, sc: (0, p))
    return call(
        enter_kernel,
        "enter",
        (n,),
        [source, source],
        [target, target],
        [shape(first.shape, first.dtype), shape(second.shape, second.dtype)],
        (first, second),
        0,
        scalars=order,
        near=(0, 1),
        near_out=True,
    )


def leave_blocks(sc, out_ref, result):
    width = result.shape[1]
    n = len(sc)
    block = width // n
    if block % 128:
        out_ref[...] = result.astype(out_ref.dtype)
        return
    for p in range(n):
        at = pl.ds(pl.multiple_of(sc[p] * block, 128), block)
        out_ref[:, at] = result[:, p * block : (p + 1) * block].astype(out_ref.dtype)


def leave_kernel(n, sc, value_ref, out_ref):
    leave_blocks([sc[p] for p in range(n)], out_ref, value_ref[...])


def leave(name, order, value, places, dtype):
    rows, width = value.shape
    n = order.shape[0]
    parts = places.shape[0]
    height = rows // parts
    result = call(
        functools.partial(leave_kernel, n),
        name,
        (parts,),
        [pl.BlockSpec((height, width), lambda i, sc: (sc[n + i], 0))],
        [pl.BlockSpec((height, width), lambda i, sc: (i, 0))],
        [shape((rows, width), dtype)],
        (value,),
        0,
        scalars=jnp.concatenate([order, places.astype(jnp.int32)]),
    )[0]
    if width // n % 128:
        index = jnp.arange(n)
        back = jnp.sum(jnp.where(order[None, :] == index[:, None], index[None, :], 0), axis=1)
        return picked(result, back)
    return result


def post_kernel(tokens_ref, attn_ref, gain_ref, out_ref):
    hidden = tokens_ref[...].astype(F32) + attn_ref[...].astype(F32)
    out_ref[...] = (hidden * norm_scale(hidden) * gain_ref[...]).astype(BF16)


def layer_out_kernel(tokens_ref, attn_ref, mlp_ref, out_ref):
    hidden = tokens_ref[...].astype(F32) + attn_ref[...].astype(F32)
    out_ref[...] = (hidden + mlp_ref[...].astype(F32)).astype(BF16)


def grad_hidden_kernel(tokens_ref, attn_ref, cotangent_ref, grad_ref, gain_ref, out_ref, low_ref):
    hidden = tokens_ref[...].astype(F32) + attn_ref[...].astype(F32)
    weighted = grad_ref[...].astype(F32) * gain_ref[...]
    grad = cotangent_ref[...].astype(F32) + norm_back(hidden, norm_scale(hidden), weighted)
    out_ref[...] = grad
    low_ref[...] = grad.astype(BF16)


def tokens_grad_kernel(tokens_ref, hidden_ref, grad_ref, gain_ref, out_ref):
    inputs = tokens_ref[...].astype(F32)
    weighted = grad_ref[...].astype(F32) * gain_ref[...]
    back = norm_back(inputs, norm_scale(inputs), weighted)
    out_ref[...] = (hidden_ref[...] + back).astype(BF16)


def on_quarter(kernel, name, arrays, gains, dtypes):
    rows, width = arrays[0].shape
    spec = pl.BlockSpec((rows, width), lambda i: (0, 0))
    full = [pl.BlockSpec(g.shape, lambda i: (0, 0)) for g in gains]
    return call(
        kernel,
        name,
        (1,),
        [spec] * len(arrays) + full,
        [spec] * len(dtypes),
        [shape((rows, width), dtype) for dtype in dtypes],
        tuple(arrays) + tuple(gains),
        0,
    )


def head_outputs(product, proj_ref, out_ref, cos_ref, sin_ref, gain_ref, factor):
    proj_ref[...] = product
    for h in range(product.shape[1] // HD):
        one = slice(h * HD, (h + 1) * HD)
        u = product[:, one]
        u = u * norm_scale(u) * gain_ref[...]
        u = u * cos_ref[...] + turned(u) * sin_ref[...]
        out_ref[:, one] = (u * factor if factor else u).astype(BF16)


def halves_product(left_ref, split, w0, w1):
    return dims(left_ref[:, :split], w0[...], 1, 0) + dims(left_ref[:, split:], w1[...], 1, 0)


def keys_kernel(
    split, tokens_ref, gain_ref, w0, w1, cos_ref, sin_ref, head_gain, normed_ref, proj_ref, keys, values
):
    @pl.when(pl.program_id(0) == 0)
    def _():
        inputs = tokens_ref[...].astype(F32)
        normed_ref[...] = (inputs * norm_scale(inputs) * gain_ref[...]).astype(BF16)
        product = halves_product(normed_ref, split, w0, w1)
        head_outputs(product, proj_ref, keys, cos_ref, sin_ref, head_gain, None)

    @pl.when(pl.program_id(0) == 1)
    def _():
        values[...] = halves_product(normed_ref, split, w0, w1).astype(BF16)


def queries_kernel(split, normed_ref, w0, w1, cos_ref, sin_ref, head_gain, proj_ref, queries):
    product = halves_product(normed_ref, split, w0, w1)
    head_outputs(product, proj_ref, queries, cos_ref, sin_ref, head_gain, HD**-0.5 * LOG2E)


def whole_block(array):
    return pl.BlockSpec(array.shape, lambda *i: (0, 0))


def project_keys(tokens, gain, pair, cosine, sine, head_gain):
    rows, width = tokens.shape
    columns = pair[0].shape[1] // 2
    split = width // 2
    side = pl.BlockSpec((split, columns), lambda j: (0, j))
    out = pl.BlockSpec((rows, columns), lambda j: (0, 0))
    small = [cosine, sine, head_gain]
    return call(
        functools.partial(keys_kernel, split),
        "project_keys",
        (2,),
        [whole_block(tokens), whole_block(gain), side, side] + [whole_block(a) for a in small],
        [whole_block(tokens), out, out, out],
        [
            shape((rows, width), BF16),
            shape((rows, columns), F32),
            shape((rows, columns), BF16),
            shape((rows, columns), BF16),
        ],
        (tokens, gain, *pair, *small),
        4 * rows * width * columns,
        near=range(7),
    )


def project_queries(normed, pair, cosine, sine, head_gain, tile=256):
    rows, width = normed.shape
    columns = pair[0].shape[1]
    split = width // 2
    side = pl.BlockSpec((split, tile), lambda j: (0, j))
    out = pl.BlockSpec((rows, tile), lambda j: (0, j))
    small = [cosine, sine, head_gain]
    return call(
        functools.partial(queries_kernel, split),
        "project_queries",
        (columns // tile,),
        [whole_block(normed), side, side] + [whole_block(a) for a in small],
        [out, out],
        [shape((rows, columns), F32), shape((rows, columns), BF16)],
        (normed, *pair, *small),
        2 * rows * width * columns,
    )


def to_width_kernel(count, half, *refs):
    i = pl.program_id(0)
    lefts = refs[:count]
    rights = refs[count : 3 * count]
    out_ref = refs[-1]
    for parity, here in ((0, i < half), (1, i >= half)):

        @pl.when(here)
        def _(parity=parity):
            total = None
            for left, pair in zip(lefts, zip(rights[::2], rights[1::2])):
                term = dims(left[...], pair[parity][...], 1, 1)
                total = term if total is None else total + term
            out_ref[...] = total.astype(out_ref.dtype)


def to_width(name, *terms, tile=256, near=()):
    rows = terms[0][0].shape[0]
    split = terms[0][2][0].shape[0]
    half = split // tile
    in_specs = []
    for left, at, pair, where, columns in terms:
        in_specs.append(pl.BlockSpec((rows, columns), lambda i, at=at: (0, at)))
    args = [t[0] for t in terms]
    flops = 0
    for left, at, pair, where, columns in terms:
        in_specs.append(
            pl.BlockSpec((tile, columns), lambda i, w=where: (jnp.minimum(i, half - 1), w))
        )
        in_specs.append(
            pl.BlockSpec((tile, columns), lambda i, w=where: (jnp.maximum(i - half, 0), w))
        )
        args += list(pair)
        flops += 4 * rows * split * columns
    return call(
        functools.partial(to_width_kernel, len(terms), half),
        name,
        (2 * half,),
        in_specs,
        [pl.BlockSpec((rows, tile), lambda i: (0, i))],
        [shape((rows, 2 * split), BF16)],
        tuple(args),
        flops,
        near=near,
    )[0]


def from_width_kernel(split, bounds, left_ref, *refs):
    out_ref = refs[-1]
    j = pl.program_id(0)
    for k in range(len(bounds) - 1):

        @pl.when((j >= bounds[k]) & (j < bounds[k + 1]))
        def _(w0=refs[2 * k], w1=refs[2 * k + 1]):
            product = dims(left_ref[:, :split], w0[...], 1, 0) + dims(left_ref[:, split:], w1[...], 1, 0)
            out_ref[...] = product.astype(out_ref.dtype)


def from_width(name, left, *sides, tile=256):
    rows, width = left.shape
    split = width // 2
    bounds = [0]
    specs, args = [], [left]
    for pair, start, columns in sides:
        low, high = bounds[-1], bounds[-1] + columns // tile
        bounds.append(high)
        specs += [
            pl.BlockSpec(
                (split, tile),
                lambda j, low=low, high=high, first=start // tile: (0, first + jnp.clip(j, low, high - 1) - low),
            )
        ] * 2
        args += list(pair)
    return call(
        functools.partial(from_width_kernel, split, tuple(bounds)),
        name,
        (bounds[-1],),
        [pl.BlockSpec((rows, width), lambda j: (0, 0))] + specs,
        [pl.BlockSpec((rows, tile), lambda j: (0, j))],
        [shape((rows, bounds[-1] * tile), BF16)],
        tuple(args),
        2 * rows * width * bounds[-1] * tile,
    )[0]


def units_kernel(split, post_ref, wg0, wg1, wu0, wu1, grad_ref, act_ref, gate_out, up_out):
    def product(w0, w1):
        return dims(post_ref[:, :split], w0[...], 1, 0) + dims(post_ref[:, split:], w1[...], 1, 0)

    gate = product(wg0, wg1)
    up = product(wu0, wu1)
    grad_act = grad_ref[...].astype(F32)
    sigma = jax.nn.sigmoid(gate)
    silu = gate * sigma
    act_ref[...] = (silu * up).astype(BF16)
    up_out[...] = (grad_act * silu).astype(BF16)
    gate_out[...] = (grad_act * up * sigma * (1.0 + gate * (1.0 - sigma))).astype(BF16)


def hidden_units(post, wg, wu, grad_act, tile=256):
    rows, width = post.shape
    units = grad_act.shape[1]
    split = width // 2
    side = pl.BlockSpec((split, tile), lambda j: (0, j))
    part = pl.BlockSpec((rows, tile), lambda j: (0, j))
    unit = shape((rows, units), BF16)
    return call(
        functools.partial(units_kernel, split),
        "hidden_units",
        (units // tile,),
        [pl.BlockSpec(post.shape, lambda j: (0, 0)), side, side, side, side, part],
        [part, part, part],
        [unit, unit, unit],
        (post, *wg, *wu, grad_act),
        4 * rows * width * units,
        near=(1, 2, 3, 4),
    )


def side_products(count, sides, refs):
    turned_lefts = [left[...].T for left in refs[:count]]
    at = count
    for side in sides:
        start = 0
        terms = []
        for which in side:
            right = refs[at]
            at += 1
            columns = slice(start, start + right.shape[1])
            terms.append((columns, dims(turned_lefts[which], right[...], 1, 0)))
            start = columns.stop
        yield terms


def away_kernel(count, sides, *refs):
    outs = refs[-len(sides) :]
    for out_ref, terms in zip(outs, side_products(count, sides, refs)):
        for columns, term in terms:
            out_ref[:, columns] = term.astype(BF16)


def home_kernel(count, sides, steps, sc, *refs):
    inputs = count + sum(len(side) for side in sides)
    gots = refs[inputs : inputs + len(sides)]
    outs = refs[inputs + len(sides) :]
    step = pl.program_id(0)
    for i, terms in enumerate(side_products(count, sides, refs)):
        leaves = sc[(5 * i + 1) * steps + step] == 1
        for columns, term in terms:
            total = (term + gots[i][:, columns].astype(F32)).astype(BF16)

            @pl.when(leaves)
            def _(i=i, columns=columns, total=total):
                outs[2 * i][:, columns] = total

            @pl.when(jnp.logical_not(leaves))
            def _(i=i, columns=columns, total=total):
                outs[2 * i + 1][:, columns] = total


def visits(places, wanted):
    held = []
    for step, (place, own) in enumerate(zip(places, wanted)):
        if own:
            held.append(place)
        elif any(wanted[:step]):
            held.append(held[-1])
        else:
            held.append(next(p for p, o in zip(places[step:], wanted[step:]) if o))
    return held


def weight_grads(name, n, bits_of, lefts, *sides, tile=512):
    rows, width = lefts[0].shape
    split = width // 2
    count = len(lefts)
    kinds = [[term[0] for term in side] for side in sides]
    rights = [(term[1], term[2], term[3]) for side in sides for term in side]
    totals = [sum(term[3] for term in side) for side in sides]
    args = (*lefts, *[r[0] for r in rights])

    def products(first):
        tiles = split // tile
        return call(
            functools.partial(away_kernel, count, kinds),
            name + "_away" if first else name,
            (tiles,),
            [pl.BlockSpec((rows, tile), lambda i, f=first: (0, f + i))] * count
            + [pl.BlockSpec((rows, c), lambda i, w=w: (0, w)) for _, w, c in rights],
            [pl.BlockSpec((tile, total), lambda i: (i, 0)) for total in totals],
            [shape((split, total), BF16) for total in totals],
            args,
            0,
        )

    gots = together([exchange(away, 1) for away in products(split // tile)])
    block = width // n
    if block % 128:
        return [split_sum(home, got, n, bit) for home, got, bit in zip(products(0), gots, bits_of)]
    steps = n // 2
    order = leaving_first(n, bits_of[0])
    table = []
    for bit in bits_of:
        masks = [2 * i for i in range(steps)]
        gone = [i for i, m in enumerate(masks) if m & bit]
        kept = [i for i, m in enumerate(masks) if not m & bit]
        leaves = [i in gone for i in order]
        places = [(gone if i in gone else kept).index(i) for i in order]
        table += order + [int(x) for x in leaves]
        table += visits(places, leaves) + visits(places, [not x for x in leaves]) + [0] * steps
    outs = call(
        functools.partial(home_kernel, count, kinds, steps),
        name,
        (steps,),
        [pl.BlockSpec((rows, block), lambda i, sc: (0, sc[i]))] * count
        + [pl.BlockSpec((rows, c), lambda i, sc, w=w: (0, w)) for _, w, c in rights]
        + [pl.BlockSpec((block, total), lambda i, sc: (sc[i], 0)) for total in totals],
        [
            pl.BlockSpec((block, total), lambda i, sc, at=(5 * k + 2 + part) * steps: (sc[at + i], 0))
            for k, total in enumerate(totals)
            for part in range(2)
        ],
        [shape((split // 2, total), BF16) for total in totals for part in range(2)],
        (*args, *gots),
        0,
        scalars=jnp.array(table, jnp.int32),
    )
    return list(zip(outs[::2], outs[1::2]))


def heads_back_kernel(terms, passed, *refs):
    grads, refs = refs[:terms], refs[terms:]
    others, refs = refs[:passed], refs[passed:]
    proj_ref, cos_ref, sin_ref, gain_ref, out_ref, sum_ref = refs
    columns = proj_ref.shape[1]
    total = None
    for h in range(columns // HD):
        one = slice(h * HD, (h + 1) * HD)
        grad = grads[0][:, one].astype(F32)
        for more in grads[1:]:
            grad = grad + more[:, one].astype(F32)
        grad = grad * cos_ref[...] + turned(grad * sin_ref[...])
        u = proj_ref[:, one]
        scale = norm_scale(u)
        term = jnp.sum((grad * u * scale).reshape(-1, 8, HD), axis=0)
        total = term if total is None else total + term
        out_ref[:, one] = norm_back(u, scale, grad * gain_ref[...]).astype(BF16)
    sum_ref[...] = total
    if passed:
        other = others[0][...].astype(F32)
        for more in others[1:]:
            other = other + more[...].astype(F32)
        out_ref[:, columns:] = other.astype(BF16)


def heads_back(name, grads, others, proj, cosine, sine, gain):
    rows, columns = proj.shape
    args = (*grads, *others, proj, cosine, sine, gain)
    total = columns + (others[0].shape[1] if others else 0)
    return call(
        functools.partial(heads_back_kernel, len(grads), len(others)),
        name,
        (1,),
        [pl.BlockSpec(a.shape, lambda i: (0, 0)) for a in args],
        [pl.BlockSpec((rows, total), lambda i: (0, 0)), pl.BlockSpec((8, HD), lambda i: (0, 0))],
        [shape((rows, total), BF16), shape((8, HD), F32)],
        args,
        20 * rows * columns,
    )


def fetch(halves, columns, scratch, sems):
    copies = []
    for i, half in enumerate(halves):
        rows = half.shape[0]
        at = pl.ds((i % 2) * rows, rows)
        copy = pltpu.make_async_copy(half.at[:, columns], scratch[i // 2].at[at], sems.at[i])
        copy.start()
        copies.append(copy)
    return copies


def attend_kernel(
    span, head, heads, sc, q_ref, k0, k1, v0, v1, ctx_ref, lse_ref, k_s, v_s, acc_s, sum_s, sems
):
    columns = slice(head * HD, (head + heads) * HD)
    copies = fetch((k0, k1, v0, v1), columns, (k_s, v_s), sems)
    group = q_ref.shape[1] // HD // heads
    rows = span * group
    for copy in copies:
        copy.wait()
    for s in range(2):
        top = slice(s * span, (s + 1) * span)

        def stacked(h):
            parts = range(h * group, (h + 1) * group)
            return jnp.concatenate([q_ref[top, g * HD : (g + 1) * HD] for g in parts], axis=0)

        qs = [stacked(h) for h in range(heads)]
        acc_s[...] = jnp.zeros_like(acc_s)
        sum_s[...] = jnp.zeros_like(sum_s)

        def step(p, masked):
            at = pl.ds(pl.multiple_of(sc[2 + p] * span, span), span)
            es = [jnp.exp2(dims(qs[h], k_s[at, h * HD : (h + 1) * HD], 1, 1)) for h in range(heads)]
            if masked:
                row = lax.broadcasted_iota(jnp.int32, (rows, span), 0) % span
                col = lax.broadcasted_iota(jnp.int32, (rows, span), 1)
                es = [jnp.where(row >= col, e, 0.0) for e in es]
            for h, e in enumerate(es):
                part = e[:, :HD]
                for c in range(HD, span, HD):
                    part = part + e[:, c : c + HD]
                sum_s[h] += part
                acc_s[h] += dims(e.astype(BF16), v_s[at, h * HD : (h + 1) * HD], 1, 0)

        pl.loop(0, sc[s])(lambda p: step(p, False))
        step(sc[s], True)
        for h in range(heads):
            total = jnp.sum(sum_s[h], axis=1, keepdims=True)
            ctx = (acc_s[h] / total).astype(BF16)
            for g in range(group):
                at = slice((h * group + g) * HD, (h * group + g + 1) * HD)
                ctx_ref[top, at] = ctx[g * span : (g + 1) * span]
            wide = jnp.broadcast_to(jnp.log2(total), (rows, HD))
            lse_ref[h, s : s + 1, :] = wide.T[0:1]


def attend_back_kernel(
    span, head, heads, sc, q_ref, do_ref, ctx_ref, lse_ref, k0, k1, v0, v1,
    dq_ref, dk0, dk1, dv0, dv1, k_s, v_s, dk_s, dv_s, dq_s, sems,
):
    half = k0.shape[0]
    columns = slice(head * HD, (head + heads) * HD)
    copies = fetch((k0, k1, v0, v1), columns, (k_s, v_s), sems)
    group = q_ref.shape[1] // HD // heads
    rows = span * group
    chunks = 2 * half // span
    cols = [slice(h * HD, (h + 1) * HD) for h in range(heads)]
    later = (sc[1] > sc[0]).astype(jnp.int32)

    def clear(p):
        at = pl.ds(pl.multiple_of(sc[2 + p] * span, span), span)
        dk_s[at] = jnp.zeros((span, heads * HD), F32)
        dv_s[at] = jnp.zeros((span, heads * HD), F32)

    pl.loop(jnp.maximum(sc[0], sc[1]) + 1, chunks)(clear)
    for first in (True, False):
        which = later if first else 1 - later
        top = pl.ds(pl.multiple_of(which * span, span), span)

        def stacked(ref, h):
            parts = range(h * group, (h + 1) * group)
            return jnp.concatenate([ref[top, g * HD : (g + 1) * HD] for g in parts], axis=0)

        qs = [stacked(q_ref, h) for h in range(heads)]
        dos = [stacked(do_ref, h) for h in range(heads)]
        q_ts = [q.T for q in qs]
        do_ts = [do.T for do in dos]
        products = [dos[h].astype(F32) * stacked(ctx_ref, h).astype(F32) for h in range(heads)]
        deltas = [jnp.sum(product.T, axis=0, keepdims=True) for product in products]
        lses = [lse_ref[h, pl.ds(which, 1), :] for h in range(heads)]
        dq_s[...] = jnp.zeros_like(dq_s)
        if first:
            for copy in copies:
                copy.wait()

        def step(p, masked):
            at = pl.ds(pl.multiple_of(sc[2 + p] * span, span), span)
            ks = [k_s[at, c] for c in cols]
            scores = [dims(ks[h], q_ts[h], 1, 0) for h in range(heads)]
            grad_probs = [dims(v_s[at, cols[h]], do_ts[h], 1, 0) for h in range(heads)]
            probs = [jnp.exp2(scores[h] - lses[h]) for h in range(heads)]
            if masked:
                key = lax.broadcasted_iota(jnp.int32, (span, rows), 0)
                query = lax.broadcasted_iota(jnp.int32, (span, rows), 1) % span
                probs = [jnp.where(query >= key, p, 0.0) for p in probs]
            grads = [(probs[h] * (grad_probs[h] - deltas[h])).astype(BF16) for h in range(heads)]
            for h in range(heads):
                dv = dims(probs[h].astype(BF16), dos[h], 1, 0)
                dk = dims(grads[h], qs[h], 1, 0)
                if first:
                    dv_s[at, cols[h]] = dv
                    dk_s[at, cols[h]] = dk
                else:
                    dv_s[at, cols[h]] += dv
                    dk_s[at, cols[h]] += dk
                dq_s[h] += dims(ks[h], grads[h], 0, 0)

        pl.loop(0, sc[which])(lambda p: step(p, False))
        step(sc[which], True)
        for h in range(heads):
            dq = dq_s[h].T * (HD**-0.5)
            for g in range(group):
                at = slice((h * group + g) * HD, (h * group + g + 1) * HD)
                dq_ref[top, at] = dq[g * span : (g + 1) * span]
    dk0[...] = (dk_s[:half] * LN2).astype(BF16)
    dk1[...] = (dk_s[half:] * LN2).astype(BF16)
    dv0[...] = dv_s[:half].astype(BF16)
    dv1[...] = dv_s[half:].astype(BF16)


def head_groups(kv_local, half):
    heads = kv_local if half <= 4096 else 1
    return heads, range(0, kv_local, heads)


def attend(scalars, queries, keys, values, span):
    rows, width = queries.shape
    half = keys[0].shape[0]
    kv_local = keys[0].shape[1] // HD
    heads, firsts = head_groups(kv_local, half)
    across = width // kv_local * heads
    stacked = width // kv_local // HD * span
    far = pl.BlockSpec(memory_space=pl.ANY)
    results = []
    for head in firsts:
        results.append(
            pl.pallas_call(
                functools.partial(attend_kernel, span, head, heads),
                grid_spec=pltpu.PrefetchScalarGridSpec(
                    num_scalar_prefetch=1,
                    grid=(1,),
                    in_specs=[pl.BlockSpec((rows, across), lambda i, sc, at=head // heads: (0, at))]
                    + [far] * 4,
                    out_specs=[
                        pl.BlockSpec((rows, across), lambda i, sc: (0, 0)),
                        pl.BlockSpec((heads, 2, stacked), lambda i, sc: (0, 0, 0)),
                    ],
                    scratch_shapes=[pltpu.VMEM((2 * half, heads * HD), BF16)] * 2
                    + [pltpu.VMEM((heads, stacked, HD), F32)] * 2
                    + [pltpu.SemaphoreType.DMA((4,))],
                ),
                out_shape=[shape((rows, across), BF16), shape((heads, 2, stacked), F32)],
                compiler_params=pltpu.CompilerParams(
                    vmem_limit_bytes=min(60 * MIB, 16 * MIB + 44 * HD * half)
                ),
                cost_estimate=pl.CostEstimate(
                    flops=16 * rows * half * across, bytes_accessed=8 * half * HD, transcendentals=0
                ),
                name="attend",
            )(scalars, queries, *in_far(*keys, *values))
        )
    if len(results) == 1:
        return results[0]
    return [jnp.concatenate(both, axis=1 - i) for i, both in enumerate(zip(*results))]


def attend_back(scalars, queries, grad_context, context, lse, keys, values, span):
    rows, width = queries.shape
    half = keys[0].shape[0]
    kv_local = keys[0].shape[1] // HD
    heads, firsts = head_groups(kv_local, half)
    across = width // kv_local * heads
    stacked = width // kv_local // HD * span
    far = pl.BlockSpec(memory_space=pl.ANY)
    tall = pl.BlockSpec((half, heads * HD), lambda i, sc: (0, 0))
    grads = pltpu.HBM((half, heads * HD), BF16)
    results = []
    for head in firsts:
        at = head // heads
        wide = pl.BlockSpec((rows, across), lambda i, sc, at=at: (0, at))
        results.append(
            pl.pallas_call(
                functools.partial(attend_back_kernel, span, head, heads),
                grid_spec=pltpu.PrefetchScalarGridSpec(
                    num_scalar_prefetch=1,
                    grid=(1,),
                    in_specs=[wide] * 3
                    + [pl.BlockSpec((heads, 2, stacked), lambda i, sc, at=at: (at, 0, 0))]
                    + [far] * 4,
                    out_specs=[pl.BlockSpec((rows, across), lambda i, sc: (0, 0))] + [tall] * 4,
                    scratch_shapes=[pltpu.VMEM((2 * half, heads * HD), BF16)] * 2
                    + [pltpu.VMEM((2 * half, heads * HD), F32)] * 2
                    + [pltpu.VMEM((heads, HD, stacked), F32), pltpu.SemaphoreType.DMA((4,))],
                ),
                out_shape=[pltpu.HBM((rows, across), F32)] + [grads] * 4,
                compiler_params=pltpu.CompilerParams(
                    vmem_limit_bytes=min(60 * MIB, 16 * MIB + 44 * HD * half)
                ),
                cost_estimate=pl.CostEstimate(
                    flops=40 * rows * half * across, bytes_accessed=32 * half * HD, transcendentals=0
                ),
                name="attend_back",
            )(scalars, *in_far(queries, grad_context, context, lse, *keys, *values))
        )
    if len(results) == 1:
        return results[0]
    return [jnp.concatenate(parts, axis=1) for parts in zip(*results)]


def sum_of_parts(part):
    return lax.psum_scatter(part, "fsdp", scatter_dimension=0, tiled=True)


def all_parts(mine):
    return lax.all_gather(mine, "fsdp", axis=0, tiled=True)


def shards(
    tokens,
    span_order,
    input_gain,
    query_weight,
    key_weight,
    value_weight,
    query_gain,
    key_gain,
    output_weight,
    post_gain,
    gate_weight,
    up_weight,
    down_weight,
    cotangent,
):
    n = lax.axis_size("blk")
    me = lax.axis_index("blk")
    bits = high_bits(n)
    flipped = bits[::-1]
    masks = mask_order(n)
    rows, width = tokens.shape
    block = width // n
    split = width // 2
    span = rows // 2
    q_cols = query_weight.shape[1]
    kv_cols = key_weight.shape[1]
    heads = q_cols // HD
    kv_heads = kv_cols // HD
    units = gate_weight.shape[1]
    o_cols = output_weight.shape[0]

    mask_list = jnp.array(masks, jnp.int32)
    order = me ^ mask_list
    pair = [bits, flipped]

    spans = span_order.reshape(n, 2)
    chunk_ids = jnp.sum(
        jnp.where(order[:, None, None] == jnp.arange(n)[None, :, None], spans[None], 0),
        axis=1,
    ).reshape(-1)
    count = 2 * n
    positions = jnp.sum(
        jnp.where(
            chunk_ids[None, :] == jnp.arange(count)[:, None], jnp.arange(count)[None, :], 0
        ),
        axis=1,
    )
    scalars = jnp.concatenate([chunk_ids[:2], positions]).astype(jnp.int32)
    places = (chunk_ids[:2, None] * span + jnp.arange(span)[None, :]).reshape(-1)
    cosine, sine = rope_tables(places, HD)

    parts = lax.axis_size("fsdp")
    quarter = rows // parts
    my_part = lax.axis_index("fsdp") * quarter

    def mine(array):
        return lax.dynamic_slice_in_dim(array, my_part, quarter, 0)

    gains = jnp.concatenate([input_gain, post_gain, query_gain, key_gain]).reshape(1, -1)
    first = [{0: query_weight}, {0: jnp.concatenate([key_weight, value_weight], axis=1)}, {0: gains}]
    triple = [bits, flipped, bits]
    out_t = output_weight.T
    o_half = o_cols // 2
    gather_step(first, triple, 0, beside=(out_t,))
    tokens, cotangent = enter(order, tokens, cotangent)
    my_tokens = mine(tokens)
    my_cotangent = mine(cotangent)
    late = gather_rest(first, triple, 1, beside=(tokens, cotangent, cosine, sine, scalars))
    wq, wkv, gains = gather_end(first)
    gains = jnp.concatenate(gains, axis=0).astype(F32)
    gain_input = gains[:, :block].reshape(1, width)
    gain_post = gains[:, block : 2 * block].reshape(1, width)
    chosen = (me ^ jnp.arange(n))[:, None] == mask_list[None, :]
    head_gains = jnp.sum(jnp.where(chosen[:, :, None], gains[None, :, 2 * block :], 0.0), axis=1)
    part = head_gains.shape[1] // 2
    gain_query = head_gains[:, :part].reshape(1, HD)
    gain_key = head_gains[:, part:].reshape(1, HD)

    normed_low, k_proj, keys, values = project_keys(
        tokens, gain_input, wkv, cosine, sine, gain_key
    )
    outs = [{0: out_t[:, :o_half]}, {0: out_t[:, o_half:]}]
    out_got = gather_step(outs, pair, 0, before=late)
    rows_held = [{0: keys}, {0: values}]
    q_proj, queries = project_queries(after(normed_low, keys), wq, cosine, sine, gain_query)
    gather_step(rows_held, pair, 0, before=out_got, beside=(queries,))
    key_got = gather_rest(rows_held, pair, 1)
    all_keys, all_values = gather_end(rows_held)
    context, lse = attend(scalars, queries, all_keys, all_values, span)
    out_got = gather_rest(outs, pair, 1, before=key_got, beside=(context,))
    wo_a, wo_b = gather_end(outs)
    wide = [{0: gate_weight}, {0: up_weight}]
    down_t = down_weight.T
    middle = units // 2
    downs = [{0: down_t[:, :middle]}, {0: down_t[:, middle:]}]
    gather_step(downs, pair, 0, before=out_got, beside=(context,))
    down_got = gather_rest(downs, pair, 1)

    attn_part = to_width(
        "attention_out",
        (context, 0, wo_a, 0, o_half),
        (context, 1, wo_b, 0, o_half),
        tile=512,
    )
    my_attn = sum_of_parts(attn_part)
    my_post = on_quarter(post_kernel, "post", (my_tokens, my_attn), (gain_post,), (BF16,))[0]
    post_low = all_parts(my_post)
    gather_step(wide, pair, 0, before=down_got, beside=(my_tokens,))
    side_a, side_b = gather_end(downs)
    grad_act = from_width(
        "grad_act", after(cotangent, my_post), (side_a, 0, middle), (side_b, 0, middle), tile=middle
    )
    gather_rest(wide, pair, 1, beside=(my_post, grad_act))
    wg, wu = gather_end(wide)
    act, grad_gate, grad_up = hidden_units(post_low, wg, wu, grad_act)
    post_part = to_width("grad_post", (grad_gate, 0, wg, 0, units), (grad_up, 0, wu, 0, units), near=(2, 3, 4, 5))
    my_grad_post = sum_of_parts(post_part)

    starts = bits[0], flipped[0]
    act_now, gate_later, up_later = together((act, grad_gate, grad_up), (post_part,))
    unit_terms = weight_grads(
        "units_grad", n, starts, [post_low], [(0, gate_later, 0, units)], [(0, up_later, 0, units)]
    )
    (gate_sum, up_sum), unit_sends, unit_gots = scatter_sums(unit_terms, pair, beside=((), (post_part,)))
    mlp_part = to_width(
        "units_out",
        (act_now, 0, side_a, 0, middle),
        (act_now, 1, side_b, 0, middle),
        tile=512,
    )
    act_later = after(act, mlp_part, *unit_gots[0])
    down_terms = weight_grads(
        "down_grad", n, starts, [cotangent], [(0, act_later, 0, middle)], [(0, act_later, 1, middle)]
    )
    my_grad_post = after(my_grad_post, *[leave for leave, _ in unit_terms])
    my_grad_hidden, my_hidden_low = on_quarter(
        grad_hidden_kernel,
        "grad_hidden",
        (my_tokens, my_attn, my_cotangent, my_grad_post),
        (gain_post,),
        (F32, BF16),
    )
    hidden_low = all_parts(my_hidden_low)
    mlp_part, hidden_low = together(
        (mlp_part, hidden_low), (*unit_sends[-1], *[leave for leave, _ in down_terms])
    )
    my_mlp = sum_of_parts(mlp_part)

    grad_context = from_width("grad_context", hidden_low, (wo_a, 0, o_half), (wo_b, 0, o_half))
    dq, dk_own, dk_other, dv_own, dv_other = attend_back(
        scalars, queries, grad_context, context, lse, all_keys, all_values, span
    )
    (down_a, down_b), _, down_gots = scatter_sums(down_terms, pair, beside=((dk_own,),))
    down_sum = jnp.concatenate([down_a, down_b], axis=1).T
    dk_other, dv_other = together((dk_other, dv_other), (*unit_gots[-1], *down_gots[0]))
    dk_got, dv_got = together((exchange(dk_other, 1), exchange(dv_other, 1)))
    key_sums = split_sum(dk_own, dk_got, n, bits[0])
    value_sums = split_sum(dv_own, dv_got, n, flipped[0])
    (key_terms, value_terms), sends, _ = scatter_terms([key_sums, value_sums], pair)
    my_layer_out = on_quarter(
        layer_out_kernel, "layer_out_rows", (my_tokens, my_attn, after(my_mlp, *sends[0])), (), (BF16,)
    )[0]
    all_layer_out = all_parts(my_layer_out)
    dq, hidden_later = together((dq, hidden_low), tuple(sends[0]))
    grad_q_low, q_gain_part = heads_back("queries_back", [dq], [], q_proj, cosine, sine, gain_query)
    grad_kv_low, k_gain_part = heads_back(
        "keys_back", key_terms, value_terms, k_proj, cosine, sine, gain_key
    )
    normed_part = to_width(
        "grad_normed", (grad_q_low, 0, wq, 0, q_cols), (grad_kv_low, 0, wkv, 0, 2 * kv_cols), tile=512
    )
    my_grad_normed = sum_of_parts(after(normed_part, all_layer_out))
    query_terms = weight_grads(
        "attention_grad",
        n,
        starts,
        [normed_low, hidden_later],
        [(0, grad_q_low, 0, q_cols), (1, context, 0, o_half)],
        [(0, after(grad_kv_low, normed_part, *down_gots[-1]), 0, 2 * kv_cols), (1, context, 1, o_half)],
    )
    my_grad_normed = after(my_grad_normed, query_terms[0][0], query_terms[1][0])
    my_tokens_grad = on_quarter(
        tokens_grad_kernel,
        "tokens_grad_rows",
        (my_tokens, my_grad_hidden, my_grad_normed),
        (gain_input,),
        (BF16,),
    )[0]

    (qo, kvo), _, _ = scatter_sums(query_terms, pair, beside=((my_tokens_grad,),))
    query_sum = qo[:, :q_cols]
    key_sum = kvo[:, :kv_cols]
    value_sum = kvo[:, kv_cols : 2 * kv_cols]
    out_sum = jnp.concatenate([qo[:, q_cols:], kvo[:, 2 * kv_cols :]], axis=1).T

    heads_sum = jnp.concatenate([jnp.sum(q_gain_part, axis=0), jnp.sum(k_gain_part, axis=0)])[None, :]
    for bit in [1] + bits:
        heads_sum = heads_sum + exchange(heads_sum, bit)
    head = HD // n
    heads_sum = lax.dynamic_slice_in_dim(heads_sum.reshape(2, n, head), me, 1, 1).reshape(-1)

    def along_rows(weight, grad):
        return jnp.sum(weight.astype(F32) * grad, axis=1)

    input_gain_part = (
        along_rows(query_weight, query_sum)
        + along_rows(key_weight, key_sum)
        + along_rows(value_weight, value_sum)
    ) / input_gain.astype(F32)
    post_gain_part = (
        along_rows(gate_weight, gate_sum) + along_rows(up_weight, up_sum)
    ) / post_gain.astype(F32)
    small = jnp.concatenate([input_gain_part, post_gain_part, heads_sum])[None, :]
    step = 1
    while step < parts:
        small = small + lax.ppermute(small, "fsdp", [(i, i ^ step) for i in range(parts)])
        step *= 2
    small = small[0]

    tokens_grad = leave("tokens_grad", order, all_parts(my_tokens_grad), jnp.arange(parts), F32)
    layer_out = leave("layer_out", order, all_layer_out, jnp.arange(parts), BF16)
    return (
        layer_out,
        tokens_grad,
        small[:block],
        query_sum,
        key_sum,
        value_sum,
        small[2 * block : 2 * block + head],
        small[2 * block + head :],
        out_sum,
        small[block : 2 * block],
        gate_sum,
        up_sum,
        down_sum,
    )


def solution(mesh):
    placed = (
        P("blk", None),
        P(),
        P("blk"),
        P("blk", "fsdp"),
        P("blk", "fsdp"),
        P("blk", "fsdp"),
        P("blk"),
        P("blk"),
        P("fsdp", "blk"),
        P("blk"),
        P("blk", "fsdp"),
        P("blk", "fsdp"),
        P("fsdp", "blk"),
        P("blk", None),
    )
    return jax.shard_map(
        shards,
        mesh=mesh,
        in_specs=placed,
        out_specs=(
            P("blk", None),
            P("blk", None),
            P("blk"),
            P("blk", "fsdp"),
            P("blk", "fsdp"),
            P("blk", "fsdp"),
            P("blk"),
            P("blk"),
            P("fsdp", "blk"),
            P("blk"),
            P("blk", "fsdp"),
            P("blk", "fsdp"),
            P("fsdp", "blk"),
        ),
        check_vma=False,
    )
```

```python
import functools
import math

import jax
import jax.numpy as jnp
from jax import lax
from jax.experimental import pallas as pl
from jax.experimental.pallas import tpu as pltpu
from jax.sharding import PartitionSpec as P

HD = 128
EPS = 1e-06
THETA = 1000000.0
LOG2E = math.log2(math.e)
LN2 = math.log(2.0)
MIB = 1024 * 1024

F32 = jnp.float32
BF16 = jnp.bfloat16


def dims(lhs, rhs, left, right):
    return lax.dot_general(lhs, rhs, (((left,), (right,)), ((), ())), preferred_element_type=F32)


def mask_order(n):
    return [2 * i for i in range(n // 2)] + [2 * i + 1 for i in range(n // 2)]


def high_bits(n):
    return [1 << i for i in range(1, n.bit_length() - 1)]


def exchange(block, bit):
    n = lax.axis_size("blk")
    return lax.ppermute(block, "blk", [(i, i ^ bit) for i in range(n)])


def together(values, others=()):
    return lax.optimization_barrier((*values, *others))[: len(values)]


def after(value, *others):
    return lax.optimization_barrier((value,) + others)[0]


def gather_step(held, orders, step, before=(), beside=()):
    sent = []
    for have in held:
        one = [have[m] for m in sorted(have)]
        sent.append(one[0] if len(one) == 1 else jnp.concatenate(one, axis=0))
    sent = together(sent, before)
    raw = [exchange(x, order[step]) for x, order in zip(sent, orders)]
    got = together(raw, beside)
    for have, brought, order in zip(held, got, orders):
        rows = have[0].shape[0]
        for i, m in enumerate(sorted(have)):
            have[m | order[step]] = brought[i * rows : (i + 1) * rows]
    return tuple(raw)


def gather_end(held):
    own = [jnp.concatenate([have[m] for m in sorted(have)], axis=0) for have in held]
    return [(x, exchange(x, 1)) for x in own]


def gather_rest(held, orders, start, before=(), beside=()):
    raw = ()
    for step in range(start, len(orders[0])):
        raw = gather_step(
            held,
            orders,
            step,
            before if step == start else (),
            beside if step == len(orders[0]) - 1 else (),
        )
    return raw


def add_low(a, b):
    return (a.astype(F32) + b.astype(F32)).astype(BF16)


def scatter_terms(parts, orders, beside=()):
    held = []
    sent = [part[0] for part in parts]
    for (leave, stay), order in zip(parts, orders):
        masks = [m for m in range(0, 4 * stay.shape[0], 2) if not m & order[0]][: 2 ** (len(order) - 1)]
        rows = stay.shape[0] // len(masks)
        held.append({m: stay[i * rows : (i + 1) * rows] for i, m in enumerate(masks)})
    sends, gots = [], []
    for step in range(len(orders[0])):
        if step:
            sent = []
            for have, order in zip(held, orders):
                leave = [add_low(*have.pop(m)) for m in sorted(have) if m & order[step]]
                sent.append(leave[0] if len(leave) == 1 else jnp.concatenate(leave, axis=0))
                for m in have:
                    have[m] = add_low(*have[m])
        sent = together(sent)
        sends.append(sent)
        raw = [exchange(x, order[step]) for x, order in zip(sent, orders)]
        gots.append(tuple(raw))
        got = together(raw, beside[step] if step < len(beside) else ())
        for have, back in zip(held, got):
            rows = back.shape[0] // len(have)
            for i, m in enumerate(sorted(have)):
                have[m] = (have[m], back[i * rows : (i + 1) * rows])
    return [have[0] for have in held], sends, gots


def scatter_sums(parts, orders, beside=()):
    terms, sends, gots = scatter_terms(parts, orders, beside)
    return [a.astype(F32) + b.astype(F32) for a, b in terms], sends, gots


def leaving_first(n, bit):
    masks = [2 * i for i in range(n // 2)]
    return [i for i, m in enumerate(masks) if m & bit] + [i for i, m in enumerate(masks) if not m & bit]


def split_sum(own, got, n, bit):
    rows = own.shape[0] // (n // 2)
    at = leaving_first(n, bit)

    def part(array, which):
        return jnp.concatenate([array[i * rows : (i + 1) * rows] for i in which], axis=0)

    half = len(at) // 2
    return tuple(add_low(part(own, w), part(got, w)) for w in (at[:half], at[half:]))


def norm_scale(values):
    return lax.rsqrt(jnp.mean(values * values, axis=-1, keepdims=True) + EPS)


def norm_back(values, scale, weighted):
    inner = jnp.mean(weighted * values, axis=-1, keepdims=True)
    return scale * (weighted - values * scale * scale * inner)


def rope_tables(places, width):
    half = width // 2
    freqs = THETA ** (-jnp.arange(half, dtype=F32) * 2.0 / width)
    angles = places.astype(F32)[:, None] * freqs[None, :]
    sine = jnp.sin(angles)
    cosine = jnp.cos(angles)
    return (jnp.concatenate([cosine, cosine], axis=1), jnp.concatenate([-sine, sine], axis=1))


def turned(values):
    return pltpu.roll(values, HD // 2, 1)


def call(kernel, name, grid, in_specs, out_specs, out_shape, args, flops, scratch=(), scalars=None, near=(), near_out=False):
    if scalars is None:
        spec = {"grid": grid, "in_specs": in_specs, "out_specs": out_specs, "scratch_shapes": scratch}
    else:
        spec = {
            "grid_spec": pltpu.PrefetchScalarGridSpec(
                num_scalar_prefetch=1,
                grid=grid,
                in_specs=in_specs,
                out_specs=out_specs,
                scratch_shapes=scratch,
            )
        }
    args = [a if i in near else in_far(a)[0] for i, a in enumerate(args)]
    if not near_out:
        out_shape = [pltpu.HBM(o.shape, o.dtype) for o in out_shape]
    if scalars is not None:
        args = (scalars, *args)
    return pl.pallas_call(
        kernel,
        out_shape=out_shape,
        compiler_params=pltpu.CompilerParams(vmem_limit_bytes=28 * MIB),
        cost_estimate=pl.CostEstimate(flops=0, bytes_accessed=0, transcendentals=0),
        name=name,
        **spec,
    )(*args)


def in_far(*arrays):
    big = 1 << 17
    return [
        pltpu.with_memory_space_constraint(a, pltpu.HBM) if a.size * a.dtype.itemsize >= big else a
        for a in arrays
    ]


def shape(dims_, dtype):
    return jax.ShapeDtypeStruct(dims_, dtype)


def picked(array, order):
    n = order.shape[0]
    block = array.shape[1] // n
    return jnp.concatenate(
        [lax.dynamic_slice_in_dim(array, order[i] * block, block, 1) for i in range(n)], axis=1
    )


def enter_kernel(sc, a_ref, b_ref, a_out, b_out):
    a_out[...] = a_ref[...]
    b_out[...] = b_ref[...]


def enter(order, first, second):
    rows, width = first.shape
    n = order.shape[0]
    block = width // n
    if block % 128:
        return picked(first, order), picked(second, order)
    source = pl.BlockSpec((rows, block), lambda p, sc: (0, sc[p]))
    target = pl.BlockSpec((rows, block), lambda p, sc: (0, p))
    return call(
        enter_kernel,
        "enter",
        (n,),
        [source, source],
        [target, target],
        [shape(first.shape, first.dtype), shape(second.shape, second.dtype)],
        (first, second),
        0,
        scalars=order,
        near=(0, 1),
        near_out=True,
    )


def leave_blocks(sc, out_ref, result):
    width = result.shape[1]
    n = len(sc)
    block = width // n
    if block % 128:
        out_ref[...] = result.astype(out_ref.dtype)
        return
    for p in range(n):
        at = pl.ds(pl.multiple_of(sc[p] * block, 128), block)
        out_ref[:, at] = result[:, p * block : (p + 1) * block].astype(out_ref.dtype)


def leave_kernel(n, sc, value_ref, out_ref):
    leave_blocks([sc[p] for p in range(n)], out_ref, value_ref[...])


def leave(name, order, value, places, dtype):
    rows, width = value.shape
    n = order.shape[0]
    parts = places.shape[0]
    height = rows // parts
    result = call(
        functools.partial(leave_kernel, n),
        name,
        (parts,),
        [pl.BlockSpec((height, width), lambda i, sc: (sc[n + i], 0))],
        [pl.BlockSpec((height, width), lambda i, sc: (i, 0))],
        [shape((rows, width), dtype)],
        (value,),
        0,
        scalars=jnp.concatenate([order, places.astype(jnp.int32)]),
    )[0]
    if width // n % 128:
        index = jnp.arange(n)
        back = jnp.sum(jnp.where(order[None, :] == index[:, None], index[None, :], 0), axis=1)
        return picked(result, back)
    return result


def post_kernel(tokens_ref, attn_ref, gain_ref, out_ref):
    hidden = tokens_ref[...].astype(F32) + attn_ref[...].astype(F32)
    out_ref[...] = (hidden * norm_scale(hidden) * gain_ref[...]).astype(BF16)


def layer_out_kernel(tokens_ref, attn_ref, mlp_ref, out_ref):
    hidden = tokens_ref[...].astype(F32) + attn_ref[...].astype(F32)
    out_ref[...] = (hidden + mlp_ref[...].astype(F32)).astype(BF16)


def grad_hidden_kernel(tokens_ref, attn_ref, cotangent_ref, grad_ref, gain_ref, out_ref, low_ref):
    hidden = tokens_ref[...].astype(F32) + attn_ref[...].astype(F32)
    weighted = grad_ref[...].astype(F32) * gain_ref[...]
    grad = cotangent_ref[...].astype(F32) + norm_back(hidden, norm_scale(hidden), weighted)
    out_ref[...] = grad
    low_ref[...] = grad.astype(BF16)


def tokens_grad_kernel(tokens_ref, hidden_ref, grad_ref, gain_ref, out_ref):
    inputs = tokens_ref[...].astype(F32)
    weighted = grad_ref[...].astype(F32) * gain_ref[...]
    back = norm_back(inputs, norm_scale(inputs), weighted)
    out_ref[...] = (hidden_ref[...] + back).astype(BF16)


def on_quarter(kernel, name, arrays, gains, dtypes):
    rows, width = arrays[0].shape
    spec = pl.BlockSpec((rows, width), lambda i: (0, 0))
    full = [pl.BlockSpec(g.shape, lambda i: (0, 0)) for g in gains]
    return call(
        kernel,
        name,
        (1,),
        [spec] * len(arrays) + full,
        [spec] * len(dtypes),
        [shape((rows, width), dtype) for dtype in dtypes],
        tuple(arrays) + tuple(gains),
        0,
    )


def head_outputs(product, proj_ref, out_ref, cos_ref, sin_ref, gain_ref, factor):
    proj_ref[...] = product
    for h in range(product.shape[1] // HD):
        one = slice(h * HD, (h + 1) * HD)
        u = product[:, one]
        u = u * norm_scale(u) * gain_ref[...]
        u = u * cos_ref[...] + turned(u) * sin_ref[...]
        out_ref[:, one] = (u * factor if factor else u).astype(BF16)


def halves_product(left_ref, split, w0, w1):
    return dims(left_ref[:, :split], w0[...], 1, 0) + dims(left_ref[:, split:], w1[...], 1, 0)


def keys_kernel(
    split, tokens_ref, gain_ref, w0, w1, cos_ref, sin_ref, head_gain, normed_ref, proj_ref, keys, values
):
    @pl.when(pl.program_id(0) == 0)
    def _():
        inputs = tokens_ref[...].astype(F32)
        normed_ref[...] = (inputs * norm_scale(inputs) * gain_ref[...]).astype(BF16)
        product = halves_product(normed_ref, split, w0, w1)
        head_outputs(product, proj_ref, keys, cos_ref, sin_ref, head_gain, None)

    @pl.when(pl.program_id(0) == 1)
    def _():
        values[...] = halves_product(normed_ref, split, w0, w1).astype(BF16)


def queries_kernel(split, normed_ref, w0, w1, cos_ref, sin_ref, head_gain, proj_ref, queries):
    product = halves_product(normed_ref, split, w0, w1)
    head_outputs(product, proj_ref, queries, cos_ref, sin_ref, head_gain, HD**-0.5 * LOG2E)


def whole_block(array):
    return pl.BlockSpec(array.shape, lambda *i: (0, 0))


def project_keys(tokens, gain, pair, cosine, sine, head_gain):
    rows, width = tokens.shape
    columns = pair[0].shape[1] // 2
    split = width // 2
    side = pl.BlockSpec((split, columns), lambda j: (0, j))
    out = pl.BlockSpec((rows, columns), lambda j: (0, 0))
    small = [cosine, sine, head_gain]
    return call(
        functools.partial(keys_kernel, split),
        "project_keys",
        (2,),
        [whole_block(tokens), whole_block(gain), side, side] + [whole_block(a) for a in small],
        [whole_block(tokens), out, out, out],
        [
            shape((rows, width), BF16),
            shape((rows, columns), F32),
            shape((rows, columns), BF16),
            shape((rows, columns), BF16),
        ],
        (tokens, gain, *pair, *small),
        4 * rows * width * columns,
        near=range(7),
    )


def project_queries(normed, pair, cosine, sine, head_gain, tile=256):
    rows, width = normed.shape
    columns = pair[0].shape[1]
    split = width // 2
    side = pl.BlockSpec((split, tile), lambda j: (0, j))
    out = pl.BlockSpec((rows, tile), lambda j: (0, j))
    small = [cosine, sine, head_gain]
    return call(
        functools.partial(queries_kernel, split),
        "project_queries",
        (columns // tile,),
        [whole_block(normed), side, side] + [whole_block(a) for a in small],
        [out, out],
        [shape((rows, columns), F32), shape((rows, columns), BF16)],
        (normed, *pair, *small),
        2 * rows * width * columns,
    )


def to_width_kernel(count, half, *refs):
    i = pl.program_id(0)
    lefts = refs[:count]
    rights = refs[count : 3 * count]
    out_ref = refs[-1]
    for parity, here in ((0, i < half), (1, i >= half)):

        @pl.when(here)
        def _(parity=parity):
            total = None
            for left, pair in zip(lefts, zip(rights[::2], rights[1::2])):
                term = dims(left[...], pair[parity][...], 1, 1)
                total = term if total is None else total + term
            out_ref[...] = total.astype(out_ref.dtype)


def to_width(name, *terms, tile=256, near=()):
    rows = terms[0][0].shape[0]
    split = terms[0][2][0].shape[0]
    half = split // tile
    in_specs = []
    for left, at, pair, where, columns in terms:
        in_specs.append(pl.BlockSpec((rows, columns), lambda i, at=at: (0, at)))
    args = [t[0] for t in terms]
    flops = 0
    for left, at, pair, where, columns in terms:
        in_specs.append(
            pl.BlockSpec((tile, columns), lambda i, w=where: (jnp.minimum(i, half - 1), w))
        )
        in_specs.append(
            pl.BlockSpec((tile, columns), lambda i, w=where: (jnp.maximum(i - half, 0), w))
        )
        args += list(pair)
        flops += 4 * rows * split * columns
    return call(
        functools.partial(to_width_kernel, len(terms), half),
        name,
        (2 * half,),
        in_specs,
        [pl.BlockSpec((rows, tile), lambda i: (0, i))],
        [shape((rows, 2 * split), BF16)],
        tuple(args),
        flops,
        near=near,
    )[0]


def from_width_kernel(split, bounds, left_ref, *refs):
    out_ref = refs[-1]
    j = pl.program_id(0)
    for k in range(len(bounds) - 1):

        @pl.when((j >= bounds[k]) & (j < bounds[k + 1]))
        def _(w0=refs[2 * k], w1=refs[2 * k + 1]):
            product = dims(left_ref[:, :split], w0[...], 1, 0) + dims(left_ref[:, split:], w1[...], 1, 0)
            out_ref[...] = product.astype(out_ref.dtype)


def from_width(name, left, *sides, tile=256):
    rows, width = left.shape
    split = width // 2
    bounds = [0]
    specs, args = [], [left]
    for pair, start, columns in sides:
        low, high = bounds[-1], bounds[-1] + columns // tile
        bounds.append(high)
        specs += [
            pl.BlockSpec(
                (split, tile),
                lambda j, low=low, high=high, first=start // tile: (0, first + jnp.clip(j, low, high - 1) - low),
            )
        ] * 2
        args += list(pair)
    return call(
        functools.partial(from_width_kernel, split, tuple(bounds)),
        name,
        (bounds[-1],),
        [pl.BlockSpec((rows, width), lambda j: (0, 0))] + specs,
        [pl.BlockSpec((rows, tile), lambda j: (0, j))],
        [shape((rows, bounds[-1] * tile), BF16)],
        tuple(args),
        2 * rows * width * bounds[-1] * tile,
    )[0]


def units_kernel(split, post_ref, wg0, wg1, wu0, wu1, grad_ref, act_ref, gate_out, up_out):
    def product(w0, w1):
        return dims(post_ref[:, :split], w0[...], 1, 0) + dims(post_ref[:, split:], w1[...], 1, 0)

    gate = product(wg0, wg1)
    up = product(wu0, wu1)
    grad_act = grad_ref[...].astype(F32)
    sigma = jax.nn.sigmoid(gate)
    silu = gate * sigma
    act_ref[...] = (silu * up).astype(BF16)
    up_out[...] = (grad_act * silu).astype(BF16)
    gate_out[...] = (grad_act * up * sigma * (1.0 + gate * (1.0 - sigma))).astype(BF16)


def hidden_units(post, wg, wu, grad_act, tile=256):
    rows, width = post.shape
    units = grad_act.shape[1]
    split = width // 2
    side = pl.BlockSpec((split, tile), lambda j: (0, j))
    part = pl.BlockSpec((rows, tile), lambda j: (0, j))
    unit = shape((rows, units), BF16)
    return call(
        functools.partial(units_kernel, split),
        "hidden_units",
        (units // tile,),
        [pl.BlockSpec(post.shape, lambda j: (0, 0)), side, side, side, side, part],
        [part, part, part],
        [unit, unit, unit],
        (post, *wg, *wu, grad_act),
        4 * rows * width * units,
        near=(1, 2, 3, 4),
    )


def side_products(count, sides, refs):
    turned_lefts = [left[...].T for left in refs[:count]]
    at = count
    for side in sides:
        start = 0
        terms = []
        for which in side:
            right = refs[at]
            at += 1
            columns = slice(start, start + right.shape[1])
            terms.append((columns, dims(turned_lefts[which], right[...], 1, 0)))
            start = columns.stop
        yield terms


def away_kernel(count, sides, *refs):
    outs = refs[-len(sides) :]
    for out_ref, terms in zip(outs, side_products(count, sides, refs)):
        for columns, term in terms:
            out_ref[:, columns] = term.astype(BF16)


def home_kernel(count, sides, steps, sc, *refs):
    inputs = count + sum(len(side) for side in sides)
    gots = refs[inputs : inputs + len(sides)]
    outs = refs[inputs + len(sides) :]
    step = pl.program_id(0)
    for i, terms in enumerate(side_products(count, sides, refs)):
        leaves = sc[(5 * i + 1) * steps + step] == 1
        for columns, term in terms:
            total = (term + gots[i][:, columns].astype(F32)).astype(BF16)

            @pl.when(leaves)
            def _(i=i, columns=columns, total=total):
                outs[2 * i][:, columns] = total

            @pl.when(jnp.logical_not(leaves))
            def _(i=i, columns=columns, total=total):
                outs[2 * i + 1][:, columns] = total


def visits(places, wanted):
    held = []
    for step, (place, own) in enumerate(zip(places, wanted)):
        if own:
            held.append(place)
        elif any(wanted[:step]):
            held.append(held[-1])
        else:
            held.append(next(p for p, o in zip(places[step:], wanted[step:]) if o))
    return held


def weight_grads(name, n, bits_of, lefts, *sides, tile=512):
    rows, width = lefts[0].shape
    split = width // 2
    count = len(lefts)
    kinds = [[term[0] for term in side] for side in sides]
    rights = [(term[1], term[2], term[3]) for side in sides for term in side]
    totals = [sum(term[3] for term in side) for side in sides]
    args = (*lefts, *[r[0] for r in rights])

    def products(first):
        tiles = split // tile
        return call(
            functools.partial(away_kernel, count, kinds),
            name + "_away" if first else name,
            (tiles,),
            [pl.BlockSpec((rows, tile), lambda i, f=first: (0, f + i))] * count
            + [pl.BlockSpec((rows, c), lambda i, w=w: (0, w)) for _, w, c in rights],
            [pl.BlockSpec((tile, total), lambda i: (i, 0)) for total in totals],
            [shape((split, total), BF16) for total in totals],
            args,
            0,
        )

    gots = together([exchange(away, 1) for away in products(split // tile)])
    block = width // n
    if block % 128:
        return [split_sum(home, got, n, bit) for home, got, bit in zip(products(0), gots, bits_of)]
    steps = n // 2
    order = leaving_first(n, bits_of[0])
    table = []
    for bit in bits_of:
        masks = [2 * i for i in range(steps)]
        gone = [i for i, m in enumerate(masks) if m & bit]
        kept = [i for i, m in enumerate(masks) if not m & bit]
        leaves = [i in gone for i in order]
        places = [(gone if i in gone else kept).index(i) for i in order]
        table += order + [int(x) for x in leaves]
        table += visits(places, leaves) + visits(places, [not x for x in leaves]) + [0] * steps
    outs = call(
        functools.partial(home_kernel, count, kinds, steps),
        name,
        (steps,),
        [pl.BlockSpec((rows, block), lambda i, sc: (0, sc[i]))] * count
        + [pl.BlockSpec((rows, c), lambda i, sc, w=w: (0, w)) for _, w, c in rights]
        + [pl.BlockSpec((block, total), lambda i, sc: (sc[i], 0)) for total in totals],
        [
            pl.BlockSpec((block, total), lambda i, sc, at=(5 * k + 2 + part) * steps: (sc[at + i], 0))
            for k, total in enumerate(totals)
            for part in range(2)
        ],
        [shape((split // 2, total), BF16) for total in totals for part in range(2)],
        (*args, *gots),
        0,
        scalars=jnp.array(table, jnp.int32),
    )
    return list(zip(outs[::2], outs[1::2]))


def heads_back_kernel(terms, passed, *refs):
    grads, refs = refs[:terms], refs[terms:]
    others, refs = refs[:passed], refs[passed:]
    proj_ref, cos_ref, sin_ref, gain_ref, out_ref, sum_ref = refs
    columns = proj_ref.shape[1]
    total = None
    for h in range(columns // HD):
        one = slice(h * HD, (h + 1) * HD)
        grad = grads[0][:, one].astype(F32)
        for more in grads[1:]:
            grad = grad + more[:, one].astype(F32)
        grad = grad * cos_ref[...] + turned(grad * sin_ref[...])
        u = proj_ref[:, one]
        scale = norm_scale(u)
        term = jnp.sum((grad * u * scale).reshape(-1, 8, HD), axis=0)
        total = term if total is None else total + term
        out_ref[:, one] = norm_back(u, scale, grad * gain_ref[...]).astype(BF16)
    sum_ref[...] = total
    if passed:
        other = others[0][...].astype(F32)
        for more in others[1:]:
            other = other + more[...].astype(F32)
        out_ref[:, columns:] = other.astype(BF16)


def heads_back(name, grads, others, proj, cosine, sine, gain):
    rows, columns = proj.shape
    args = (*grads, *others, proj, cosine, sine, gain)
    total = columns + (others[0].shape[1] if others else 0)
    return call(
        functools.partial(heads_back_kernel, len(grads), len(others)),
        name,
        (1,),
        [pl.BlockSpec(a.shape, lambda i: (0, 0)) for a in args],
        [pl.BlockSpec((rows, total), lambda i: (0, 0)), pl.BlockSpec((8, HD), lambda i: (0, 0))],
        [shape((rows, total), BF16), shape((8, HD), F32)],
        args,
        20 * rows * columns,
    )


def fetch(halves, columns, scratch, sems):
    copies = []
    for i, half in enumerate(halves):
        rows = half.shape[0]
        at = pl.ds((i % 2) * rows, rows)
        copy = pltpu.make_async_copy(half.at[:, columns], scratch[i // 2].at[at], sems.at[i])
        copy.start()
        copies.append(copy)
    return copies


def attend_kernel(
    span, head, heads, sc, q_ref, k0, k1, v0, v1, ctx_ref, lse_ref, k_s, v_s, acc_s, sum_s, sems
):
    columns = slice(head * HD, (head + heads) * HD)
    copies = fetch((k0, k1, v0, v1), columns, (k_s, v_s), sems)
    group = q_ref.shape[1] // HD // heads
    rows = span * group
    for copy in copies:
        copy.wait()
    for s in range(2):
        top = slice(s * span, (s + 1) * span)

        def stacked(h):
            parts = range(h * group, (h + 1) * group)
            return jnp.concatenate([q_ref[top, g * HD : (g + 1) * HD] for g in parts], axis=0)

        qs = [stacked(h) for h in range(heads)]
        acc_s[...] = jnp.zeros_like(acc_s)
        sum_s[...] = jnp.zeros_like(sum_s)

        def step(p, masked):
            at = pl.ds(pl.multiple_of(sc[2 + p] * span, span), span)
            es = [jnp.exp2(dims(qs[h], k_s[at, h * HD : (h + 1) * HD], 1, 1)) for h in range(heads)]
            if masked:
                row = lax.broadcasted_iota(jnp.int32, (rows, span), 0) % span
                col = lax.broadcasted_iota(jnp.int32, (rows, span), 1)
                es = [jnp.where(row >= col, e, 0.0) for e in es]
            for h, e in enumerate(es):
                part = e[:, :HD]
                for c in range(HD, span, HD):
                    part = part + e[:, c : c + HD]
                sum_s[h] += part
                acc_s[h] += dims(e.astype(BF16), v_s[at, h * HD : (h + 1) * HD], 1, 0)

        pl.loop(0, sc[s])(lambda p: step(p, False))
        step(sc[s], True)
        for h in range(heads):
            total = jnp.sum(sum_s[h], axis=1, keepdims=True)
            ctx = (acc_s[h] / total).astype(BF16)
            for g in range(group):
                at = slice((h * group + g) * HD, (h * group + g + 1) * HD)
                ctx_ref[top, at] = ctx[g * span : (g + 1) * span]
            wide = jnp.broadcast_to(jnp.log2(total), (rows, HD))
            lse_ref[h, s : s + 1, :] = wide.T[0:1]


def attend_back_kernel(
    span, head, heads, sc, q_ref, do_ref, ctx_ref, lse_ref, k0, k1, v0, v1,
    dq_ref, dk0, dk1, dv0, dv1, k_s, v_s, dk_s, dv_s, dq_s, sems,
):
    half = k0.shape[0]
    columns = slice(head * HD, (head + heads) * HD)
    copies = fetch((k0, k1, v0, v1), columns, (k_s, v_s), sems)
    group = q_ref.shape[1] // HD // heads
    rows = span * group
    chunks = 2 * half // span
    cols = [slice(h * HD, (h + 1) * HD) for h in range(heads)]
    later = (sc[1] > sc[0]).astype(jnp.int32)

    def clear(p):
        at = pl.ds(pl.multiple_of(sc[2 + p] * span, span), span)
        dk_s[at] = jnp.zeros((span, heads * HD), F32)
        dv_s[at] = jnp.zeros((span, heads * HD), F32)

    pl.loop(jnp.maximum(sc[0], sc[1]) + 1, chunks)(clear)
    for first in (True, False):
        which = later if first else 1 - later
        top = pl.ds(pl.multiple_of(which * span, span), span)

        def stacked(ref, h):
            parts = range(h * group, (h + 1) * group)
            return jnp.concatenate([ref[top, g * HD : (g + 1) * HD] for g in parts], axis=0)

        qs = [stacked(q_ref, h) for h in range(heads)]
        dos = [stacked(do_ref, h) for h in range(heads)]
        q_ts = [q.T for q in qs]
        do_ts = [do.T for do in dos]
        products = [dos[h].astype(F32) * stacked(ctx_ref, h).astype(F32) for h in range(heads)]
        deltas = [jnp.sum(product.T, axis=0, keepdims=True) for product in products]
        lses = [lse_ref[h, pl.ds(which, 1), :] for h in range(heads)]
        dq_s[...] = jnp.zeros_like(dq_s)
        if first:
            for copy in copies:
                copy.wait()

        def step(p, masked):
            at = pl.ds(pl.multiple_of(sc[2 + p] * span, span), span)
            ks = [k_s[at, c] for c in cols]
            scores = [dims(ks[h], q_ts[h], 1, 0) for h in range(heads)]
            grad_probs = [dims(v_s[at, cols[h]], do_ts[h], 1, 0) for h in range(heads)]
            probs = [jnp.exp2(scores[h] - lses[h]) for h in range(heads)]
            if masked:
                key = lax.broadcasted_iota(jnp.int32, (span, rows), 0)
                query = lax.broadcasted_iota(jnp.int32, (span, rows), 1) % span
                probs = [jnp.where(query >= key, p, 0.0) for p in probs]
            grads = [(probs[h] * (grad_probs[h] - deltas[h])).astype(BF16) for h in range(heads)]
            for h in range(heads):
                dv = dims(probs[h].astype(BF16), dos[h], 1, 0)
                dk = dims(grads[h], qs[h], 1, 0)
                if first:
                    dv_s[at, cols[h]] = dv
                    dk_s[at, cols[h]] = dk
                else:
                    dv_s[at, cols[h]] += dv
                    dk_s[at, cols[h]] += dk
                dq_s[h] += dims(ks[h], grads[h], 0, 0)

        pl.loop(0, sc[which])(lambda p: step(p, False))
        step(sc[which], True)
        for h in range(heads):
            dq = dq_s[h].T * (HD**-0.5)
            for g in range(group):
                at = slice((h * group + g) * HD, (h * group + g + 1) * HD)
                dq_ref[top, at] = dq[g * span : (g + 1) * span]
    dk0[...] = (dk_s[:half] * LN2).astype(BF16)
    dk1[...] = (dk_s[half:] * LN2).astype(BF16)
    dv0[...] = dv_s[:half].astype(BF16)
    dv1[...] = dv_s[half:].astype(BF16)


def head_groups(kv_local, half):
    heads = kv_local if half <= 4096 else 1
    return heads, range(0, kv_local, heads)


def attend(scalars, queries, keys, values, span):
    rows, width = queries.shape
    half = keys[0].shape[0]
    kv_local = keys[0].shape[1] // HD
    heads, firsts = head_groups(kv_local, half)
    across = width // kv_local * heads
    stacked = width // kv_local // HD * span
    far = pl.BlockSpec(memory_space=pl.ANY)
    results = []
    for head in firsts:
        results.append(
            pl.pallas_call(
                functools.partial(attend_kernel, span, head, heads),
                grid_spec=pltpu.PrefetchScalarGridSpec(
                    num_scalar_prefetch=1,
                    grid=(1,),
                    in_specs=[pl.BlockSpec((rows, across), lambda i, sc, at=head // heads: (0, at))]
                    + [far] * 4,
                    out_specs=[
                        pl.BlockSpec((rows, across), lambda i, sc: (0, 0)),
                        pl.BlockSpec((heads, 2, stacked), lambda i, sc: (0, 0, 0)),
                    ],
                    scratch_shapes=[pltpu.VMEM((2 * half, heads * HD), BF16)] * 2
                    + [pltpu.VMEM((heads, stacked, HD), F32)] * 2
                    + [pltpu.SemaphoreType.DMA((4,))],
                ),
                out_shape=[shape((rows, across), BF16), shape((heads, 2, stacked), F32)],
                compiler_params=pltpu.CompilerParams(
                    vmem_limit_bytes=min(60 * MIB, 16 * MIB + 44 * HD * half)
                ),
                cost_estimate=pl.CostEstimate(
                    flops=16 * rows * half * across, bytes_accessed=8 * half * HD, transcendentals=0
                ),
                name="attend",
            )(scalars, queries, *in_far(*keys, *values))
        )
    if len(results) == 1:
        return results[0]
    return [jnp.concatenate(both, axis=1 - i) for i, both in enumerate(zip(*results))]


def attend_back(scalars, queries, grad_context, context, lse, keys, values, span):
    rows, width = queries.shape
    half = keys[0].shape[0]
    kv_local = keys[0].shape[1] // HD
    heads, firsts = head_groups(kv_local, half)
    across = width // kv_local * heads
    stacked = width // kv_local // HD * span
    far = pl.BlockSpec(memory_space=pl.ANY)
    tall = pl.BlockSpec((half, heads * HD), lambda i, sc: (0, 0))
    grads = pltpu.HBM((half, heads * HD), BF16)
    results = []
    for head in firsts:
        at = head // heads
        wide = pl.BlockSpec((rows, across), lambda i, sc, at=at: (0, at))
        results.append(
            pl.pallas_call(
                functools.partial(attend_back_kernel, span, head, heads),
                grid_spec=pltpu.PrefetchScalarGridSpec(
                    num_scalar_prefetch=1,
                    grid=(1,),
                    in_specs=[wide] * 3
                    + [pl.BlockSpec((heads, 2, stacked), lambda i, sc, at=at: (at, 0, 0))]
                    + [far] * 4,
                    out_specs=[pl.BlockSpec((rows, across), lambda i, sc: (0, 0))] + [tall] * 4,
                    scratch_shapes=[pltpu.VMEM((2 * half, heads * HD), BF16)] * 2
                    + [pltpu.VMEM((2 * half, heads * HD), F32)] * 2
                    + [pltpu.VMEM((heads, HD, stacked), F32), pltpu.SemaphoreType.DMA((4,))],
                ),
                out_shape=[pltpu.HBM((rows, across), F32)] + [grads] * 4,
                compiler_params=pltpu.CompilerParams(
                    vmem_limit_bytes=min(60 * MIB, 16 * MIB + 44 * HD * half)
                ),
                cost_estimate=pl.CostEstimate(
                    flops=40 * rows * half * across, bytes_accessed=32 * half * HD, transcendentals=0
                ),
                name="attend_back",
            )(scalars, *in_far(queries, grad_context, context, lse, *keys, *values))
        )
    if len(results) == 1:
        return results[0]
    return [jnp.concatenate(parts, axis=1) for parts in zip(*results)]


def sum_of_parts(part):
    return lax.psum_scatter(part, "fsdp", scatter_dimension=0, tiled=True)


def all_parts(mine):
    return lax.all_gather(mine, "fsdp", axis=0, tiled=True)


def shards(
    tokens,
    span_order,
    input_gain,
    query_weight,
    key_weight,
    value_weight,
    query_gain,
    key_gain,
    output_weight,
    post_gain,
    gate_weight,
    up_weight,
    down_weight,
    cotangent,
):
    n = lax.axis_size("blk")
    me = lax.axis_index("blk")
    bits = high_bits(n)
    flipped = bits[::-1]
    masks = mask_order(n)
    rows, width = tokens.shape
    block = width // n
    split = width // 2
    span = rows // 2
    q_cols = query_weight.shape[1]
    kv_cols = key_weight.shape[1]
    heads = q_cols // HD
    kv_heads = kv_cols // HD
    units = gate_weight.shape[1]
    o_cols = output_weight.shape[0]

    mask_list = jnp.array(masks, jnp.int32)
    order = me ^ mask_list
    pair = [bits, flipped]

    spans = span_order.reshape(n, 2)
    chunk_ids = jnp.sum(
        jnp.where(order[:, None, None] == jnp.arange(n)[None, :, None], spans[None], 0),
        axis=1,
    ).reshape(-1)
    count = 2 * n
    positions = jnp.sum(
        jnp.where(
            chunk_ids[None, :] == jnp.arange(count)[:, None], jnp.arange(count)[None, :], 0
        ),
        axis=1,
    )
    scalars = jnp.concatenate([chunk_ids[:2], positions]).astype(jnp.int32)
    places = (chunk_ids[:2, None] * span + jnp.arange(span)[None, :]).reshape(-1)
    cosine, sine = rope_tables(places, HD)

    parts = lax.axis_size("fsdp")
    quarter = rows // parts
    my_part = lax.axis_index("fsdp") * quarter

    def mine(array):
        return lax.dynamic_slice_in_dim(array, my_part, quarter, 0)

    gains = jnp.concatenate([input_gain, post_gain, query_gain, key_gain]).reshape(1, -1)
    first = [{0: query_weight}, {0: jnp.concatenate([key_weight, value_weight], axis=1)}, {0: gains}]
    triple = [bits, flipped, bits]
    out_t = output_weight.T
    o_half = o_cols // 2
    gather_step(first, triple, 0, beside=(out_t,))
    tokens, cotangent = enter(order, tokens, cotangent)
    my_tokens = mine(tokens)
    my_cotangent = mine(cotangent)
    late = gather_rest(first, triple, 1, beside=(tokens, cotangent, cosine, sine, scalars))
    wq, wkv, gains = gather_end(first)
    gains = jnp.concatenate(gains, axis=0).astype(F32)
    gain_input = gains[:, :block].reshape(1, width)
    gain_post = gains[:, block : 2 * block].reshape(1, width)
    chosen = (me ^ jnp.arange(n))[:, None] == mask_list[None, :]
    head_gains = jnp.sum(jnp.where(chosen[:, :, None], gains[None, :, 2 * block :], 0.0), axis=1)
    part = head_gains.shape[1] // 2
    gain_query = head_gains[:, :part].reshape(1, HD)
    gain_key = head_gains[:, part:].reshape(1, HD)

    normed_low, k_proj, keys, values = project_keys(
        tokens, gain_input, wkv, cosine, sine, gain_key
    )
    outs = [{0: out_t[:, :o_half]}, {0: out_t[:, o_half:]}]
    out_got = gather_step(outs, pair, 0, before=late)
    rows_held = [{0: keys}, {0: values}]
    q_proj, queries = project_queries(after(normed_low, keys), wq, cosine, sine, gain_query)
    gather_step(rows_held, pair, 0, before=out_got, beside=(queries,))
    key_got = gather_rest(rows_held, pair, 1)
    all_keys, all_values = gather_end(rows_held)
    context, lse = attend(scalars, queries, all_keys, all_values, span)
    out_got = gather_rest(outs, pair, 1, before=key_got, beside=(context,))
    wo_a, wo_b = gather_end(outs)
    wide = [{0: gate_weight}, {0: up_weight}]
    down_t = down_weight.T
    middle = units // 2
    downs = [{0: down_t[:, :middle]}, {0: down_t[:, middle:]}]
    gather_step(downs, pair, 0, before=out_got, beside=(context,))
    down_got = gather_rest(downs, pair, 1)

    attn_part = to_width(
        "attention_out",
        (context, 0, wo_a, 0, o_half),
        (context, 1, wo_b, 0, o_half),
        tile=512,
    )
    my_attn = sum_of_parts(attn_part)
    my_post = on_quarter(post_kernel, "post", (my_tokens, my_attn), (gain_post,), (BF16,))[0]
    post_low = all_parts(my_post)
    gather_step(wide, pair, 0, before=down_got, beside=(my_tokens,))
    side_a, side_b = gather_end(downs)
    grad_act = from_width(
        "grad_act", after(cotangent, my_post), (side_a, 0, middle), (side_b, 0, middle), tile=middle
    )
    gather_rest(wide, pair, 1, beside=(my_post, grad_act))
    wg, wu = gather_end(wide)
    act, grad_gate, grad_up = hidden_units(post_low, wg, wu, grad_act)
    post_part = to_width("grad_post", (grad_gate, 0, wg, 0, units), (grad_up, 0, wu, 0, units), tile=512, near=(2, 3, 4, 5))
    my_grad_post = sum_of_parts(post_part)

    starts = bits[0], flipped[0]
    act_now, gate_later, up_later = together((act, grad_gate, grad_up), (post_part,))
    unit_terms = weight_grads(
        "units_grad", n, starts, [post_low], [(0, gate_later, 0, units)], [(0, up_later, 0, units)]
    )
    (gate_sum, up_sum), unit_sends, unit_gots = scatter_sums(unit_terms, pair, beside=((), (post_part,)))
    mlp_part = to_width(
        "units_out",
        (act_now, 0, side_a, 0, middle),
        (act_now, 1, side_b, 0, middle),
        tile=512,
    )
    act_later = after(act, mlp_part, *unit_gots[0])
    down_terms = weight_grads(
        "down_grad", n, starts, [cotangent], [(0, act_later, 0, middle)], [(0, act_later, 1, middle)]
    )
    my_grad_post = after(my_grad_post, *[leave for leave, _ in unit_terms])
    my_grad_hidden, my_hidden_low = on_quarter(
        grad_hidden_kernel,
        "grad_hidden",
        (my_tokens, my_attn, my_cotangent, my_grad_post),
        (gain_post,),
        (F32, BF16),
    )
    hidden_low = all_parts(my_hidden_low)
    mlp_part, hidden_low = together(
        (mlp_part, hidden_low), (*unit_sends[-1], *[leave for leave, _ in down_terms])
    )
    my_mlp = sum_of_parts(mlp_part)

    grad_context = from_width("grad_context", hidden_low, (wo_a, 0, o_half), (wo_b, 0, o_half))
    dq, dk_own, dk_other, dv_own, dv_other = attend_back(
        scalars, queries, grad_context, context, lse, all_keys, all_values, span
    )
    (down_a, down_b), _, down_gots = scatter_sums(down_terms, pair, beside=((dk_own,),))
    down_sum = jnp.concatenate([down_a, down_b], axis=1).T
    dk_other, dv_other = together((dk_other, dv_other), (*unit_gots[-1], *down_gots[0]))
    dk_got, dv_got = together((exchange(dk_other, 1), exchange(dv_other, 1)))
    key_sums = split_sum(dk_own, dk_got, n, bits[0])
    value_sums = split_sum(dv_own, dv_got, n, flipped[0])
    (key_terms, value_terms), sends, _ = scatter_terms([key_sums, value_sums], pair)
    my_layer_out = on_quarter(
        layer_out_kernel, "layer_out_rows", (my_tokens, my_attn, after(my_mlp, *sends[0])), (), (BF16,)
    )[0]
    all_layer_out = all_parts(my_layer_out)
    dq, hidden_later = together((dq, hidden_low), tuple(sends[0]))
    grad_q_low, q_gain_part = heads_back("queries_back", [dq], [], q_proj, cosine, sine, gain_query)
    grad_kv_low, k_gain_part = heads_back(
        "keys_back", key_terms, value_terms, k_proj, cosine, sine, gain_key
    )
    normed_part = to_width(
        "grad_normed", (grad_q_low, 0, wq, 0, q_cols), (grad_kv_low, 0, wkv, 0, 2 * kv_cols), tile=512
    )
    my_grad_normed = sum_of_parts(after(normed_part, all_layer_out))
    query_terms = weight_grads(
        "attention_grad",
        n,
        starts,
        [normed_low, hidden_later],
        [(0, grad_q_low, 0, q_cols), (1, context, 0, o_half)],
        [(0, after(grad_kv_low, normed_part, *down_gots[-1]), 0, 2 * kv_cols), (1, context, 1, o_half)],
    )
    my_grad_normed = after(my_grad_normed, query_terms[0][0], query_terms[1][0])
    my_tokens_grad = on_quarter(
        tokens_grad_kernel,
        "tokens_grad_rows",
        (my_tokens, my_grad_hidden, my_grad_normed),
        (gain_input,),
        (BF16,),
    )[0]

    (qo, kvo), _, _ = scatter_sums(query_terms, pair, beside=((my_tokens_grad,),))
    query_sum = qo[:, :q_cols]
    key_sum = kvo[:, :kv_cols]
    value_sum = kvo[:, kv_cols : 2 * kv_cols]
    out_sum = jnp.concatenate([qo[:, q_cols:], kvo[:, 2 * kv_cols :]], axis=1).T

    heads_sum = jnp.concatenate([jnp.sum(q_gain_part, axis=0), jnp.sum(k_gain_part, axis=0)])[None, :]
    for bit in [1] + bits:
        heads_sum = heads_sum + exchange(heads_sum, bit)
    head = HD // n
    heads_sum = lax.dynamic_slice_in_dim(heads_sum.reshape(2, n, head), me, 1, 1).reshape(-1)

    def along_rows(weight, grad):
        return jnp.sum(weight.astype(F32) * grad, axis=1)

    input_gain_part = (
        along_rows(query_weight, query_sum)
        + along_rows(key_weight, key_sum)
        + along_rows(value_weight, value_sum)
    ) / input_gain.astype(F32)
    post_gain_part = (
        along_rows(gate_weight, gate_sum) + along_rows(up_weight, up_sum)
    ) / post_gain.astype(F32)
    small = jnp.concatenate([input_gain_part, post_gain_part, heads_sum])[None, :]
    step = 1
    while step < parts:
        small = small + lax.ppermute(small, "fsdp", [(i, i ^ step) for i in range(parts)])
        step *= 2
    small = small[0]

    tokens_grad = leave("tokens_grad", order, all_parts(my_tokens_grad), jnp.arange(parts), F32)
    layer_out = leave("layer_out", order, all_layer_out, jnp.arange(parts), BF16)
    return (
        layer_out,
        tokens_grad,
        small[:block],
        query_sum,
        key_sum,
        value_sum,
        small[2 * block : 2 * block + head],
        small[2 * block + head :],
        out_sum,
        small[block : 2 * block],
        gate_sum,
        up_sum,
        down_sum,
    )


def solution(mesh):
    placed = (
        P("blk", None),
        P(),
        P("blk"),
        P("blk", "fsdp"),
        P("blk", "fsdp"),
        P("blk", "fsdp"),
        P("blk"),
        P("blk"),
        P("fsdp", "blk"),
        P("blk"),
        P("blk", "fsdp"),
        P("blk", "fsdp"),
        P("fsdp", "blk"),
        P("blk", None),
    )
    return jax.shard_map(
        shards,
        mesh=mesh,
        in_specs=placed,
        out_specs=(
            P("blk", None),
            P("blk", None),
            P("blk"),
            P("blk", "fsdp"),
            P("blk", "fsdp"),
            P("blk", "fsdp"),
            P("blk"),
            P("blk"),
            P("fsdp", "blk"),
            P("blk"),
            P("blk", "fsdp"),
            P("blk", "fsdp"),
            P("fsdp", "blk"),
        ),
        check_vma=False,
    )
```
